32 devices in a mesh: row: 4 (over x, core), col: 8 (over z, y).
Axes of the slice: x: 2, y: 2, z: 4, core: 2. Of those that a mesh axis runs over, the one named last changes fastest.
Arguments:
- block_input: bfloat16 [2, 32, 128, 192], P(None, 'row', 'col'), may hold values from -40 to 40
- cotangent: bfloat16 [2, 32, 128, 192], P(None, 'row', 'col'), may hold values from -6 to 6
- qkv_weight: bfloat16 [2, 192, 576], replicated, may hold values from -0.4375 to 0.4375
- proj_weight: bfloat16 [2, 192, 192], replicated, may hold values from -0.4375 to 0.4375
- expand_weight: bfloat16 [2, 192, 768], replicated, may hold values from -0.4375 to 0.4375
- reduce_weight: bfloat16 [2, 768, 192], replicated, may hold values from -0.21875 to 0.21875
- bias_table: float32 [2, 6, 225], replicated, may hold values from -6 to 320
Outputs:
- input_grad: float32 [2, 32, 128, 192], P(None, 'row', 'col')
- qkv_grad: float32 [2, 192, 576], replicated
- proj_grad: float32 [2, 192, 192], replicated
- expand_grad: float32 [2, 192, 768], replicated
- reduce_grad: float32 [2, 768, 192], replicated
- table_grad: float32 [2, 6, 225], replicated
The draws below stay inside these ranges and needn't reach their ends.
All inputs are finite; a program needn't handle non-finite values.
Results may differ from the reference program's by a relative error of at most 0.02.
Values may be sent and summed in bfloat16 or wider, within the bound.
No kernel may reach another device: no remote copies, remote signals or barrier semaphores. Data moves between devices by JAX's collectives and lax.ppermute only.
A program may use at most 64 MiB of HBM per device.

```python
import jax
import jax.numpy as jnp
from jax import lax

WIDTH = 192
HEADS = 6
INNER = 768
WIN = 8
SHIFT = 4
TABLE = 225
FRAMES = 2
ROWS = 8
COLS = 16
HEIGHT = 32
BREADTH = 128
N_ROW = 4
N_COL = 8


def draw_block_input(key, part):
    key = jax.random.fold_in(key, 3)
    first_key = jax.random.fold_in(key, 0)
    noise = jax.random.normal(first_key, (FRAMES, HEIGHT, BREADTH, WIDTH), jnp.float32)
    return jnp.clip(noise, -6.0, 6.0).astype(jnp.bfloat16)


def draw_bias_table(key, part):
    key = jax.random.fold_in(key, 7)
    base_key = jax.random.fold_in(key, 0)
    base = jnp.clip(jax.random.normal(base_key, (2, HEADS, TABLE), jnp.float32), -6.0, 6.0)
    return base.astype(jnp.float32)


def shard_levels(key, dims, pieces, least, high):
    gain = 1.0
    for position, blocks in pieces:
        steps = jax.random.uniform(jax.random.fold_in(jax.random.fold_in(key, 6), position), (blocks,), jnp.float32, least / len(pieces), high / len(pieces))
        gain = gain * jnp.repeat(jnp.exp(steps), dims[position] // blocks).reshape((-1,) + (1,) * (len(dims) - 1 - position))
    return gain


def bell_draw(rng, shape, scale, most, cuts=(), held_as=jnp.bfloat16):
    values = jax.random.normal(rng, shape, jnp.float32) * scale
    if len(cuts) > 0:
        values = shard_levels(rng, shape, cuts, -0.22, 0.18) * values
    return jnp.clip(values, min=-most, max=most).astype(held_as)


def setup_inputs(seed: int = 0) -> dict:
    key_of = jax.random.split(jax.random.key(seed), 8)
    block_input = draw_block_input(jax.random.fold_in(key_of[7], 71), 0)
    cotangent = bell_draw(key_of[1], (FRAMES, HEIGHT, BREADTH, WIDTH), 1.0, 6.0, ((1, 4), (2, 8)))
    qkv_weight = bell_draw(key_of[2], (2, WIDTH, 3 * WIDTH), WIDTH ** -0.5, 0.4375)
    proj_weight = bell_draw(key_of[3], (2, WIDTH, WIDTH), WIDTH ** -0.5, 0.4375)
    expand_weight = bell_draw(key_of[4], (2, WIDTH, INNER), WIDTH ** -0.5, 0.4375)
    reduce_weight = bell_draw(key_of[5], (2, INNER, WIDTH), INNER ** -0.5, 0.21875)
    bias_table = draw_bias_table(jax.random.fold_in(key_of[7], 71), 0)
    return dict(block_input=block_input, cotangent=cotangent, qkv_weight=qkv_weight, proj_weight=proj_weight, expand_weight=expand_weight, reduce_weight=reduce_weight, bias_table=bias_table)


def layer_norm(field):
    center = field - lax.optimization_barrier(jnp.mean(field, axis=-1, keepdims=True))
    spread = lax.optimization_barrier(jnp.mean(center * center, axis=-1, keepdims=True))
    return center * lax.rsqrt(spread + 1e-05)

def to_windows(field):
    frames, rows, cols, width = field.shape
    shaped = field.reshape(frames, rows // WIN, WIN, cols // WIN, WIN, width)
    return shaped.transpose(0, 1, 3, 2, 4, 5).reshape(-1, WIN * WIN, width)

def from_windows(windows, frames, rows, cols):
    shaped = windows.reshape(frames, rows // WIN, cols // WIN, WIN, WIN, -1)
    return shaped.transpose(0, 1, 3, 2, 4, 5).reshape(frames, rows, cols, -1)

def offset_onehot():
    places = jnp.arange(WIN * WIN, dtype=jnp.int32)
    prow = places // WIN
    pcol = places % WIN
    index = (prow[:, None] - prow[None, :] + WIN - 1) * (2 * WIN - 1) + (pcol[:, None] - pcol[None, :] + WIN - 1)
    entries = jnp.arange((2 * WIN - 1) ** 2, dtype=jnp.int32)
    return (entries[:, None] == index.reshape(-1)[None, :]).astype(jnp.float32)

def window_mask(row_start, col_start, rows, cols, height, breadth):
    row_ids = row_start + jnp.arange(rows, dtype=jnp.int32)
    col_ids = col_start + jnp.arange(cols, dtype=jnp.int32)
    label = (row_ids >= height - WIN // 2).astype(jnp.int32)[:, None] * 2 + (col_ids >= breadth - WIN // 2).astype(jnp.int32)[None, :]
    label = label.reshape(rows // WIN, WIN, cols // WIN, WIN).transpose(0, 2, 1, 3).reshape(-1, WIN * WIN)
    return jnp.where(label[:, :, None] == label[:, None, :], 0.0, -10000.0).astype(jnp.float32)

def block_tile(field, weights, masking):
    frames, rows, cols, width = field.shape
    qkv_w, proj_w, expand_w, reduce_w, table = weights
    heads = table.shape[0]
    head = width // heads
    windows = to_windows(field)
    count = windows.shape[0]
    normed = layer_norm(windows).astype(jnp.bfloat16).reshape(-1, width)
    mixed = jnp.dot(normed, qkv_w, preferred_element_type=jnp.float32).reshape(count, WIN * WIN, 3, heads, head)
    query = (mixed[:, :, 0] * head ** (-0.5)).astype(jnp.bfloat16)
    keys = mixed[:, :, 1].astype(jnp.bfloat16)
    values = mixed[:, :, 2].astype(jnp.bfloat16)
    scores = jnp.einsum('nqhd,nkhd->nhqk', query, keys, preferred_element_type=jnp.float32)
    bias = jnp.dot(table, offset_onehot(), precision=lax.Precision.HIGHEST).reshape(heads, WIN * WIN, WIN * WIN)
    scores = scores + bias[None]
    if masking is not None:
        scores = (scores.reshape(frames, -1, heads, WIN * WIN, WIN * WIN) + masking[None, :, None]).reshape(count, heads, WIN * WIN, WIN * WIN)
    top = lax.stop_gradient(lax.optimization_barrier(jnp.max(scores, axis=-1, keepdims=True)))
    expos = jnp.exp(scores - top)
    probs = (expos / lax.optimization_barrier(jnp.sum(expos, axis=-1, keepdims=True))).astype(jnp.bfloat16)
    attended = jnp.einsum('nhqk,nkhd->nqhd', probs, values, preferred_element_type=jnp.float32)
    attended = attended.reshape(-1, width).astype(jnp.bfloat16)
    resid = windows + jnp.dot(attended, proj_w, preferred_element_type=jnp.float32).reshape(count, WIN * WIN, width)
    normed_two = layer_norm(resid).astype(jnp.bfloat16).reshape(-1, width)
    hidden = jax.nn.gelu(jnp.dot(normed_two, expand_w, preferred_element_type=jnp.float32), approximate=False).astype(jnp.bfloat16)
    result = resid + jnp.dot(hidden, reduce_w, preferred_element_type=jnp.float32).reshape(count, WIN * WIN, width)
    return from_windows(result, frames, rows, cols)

def split_tiles(field):
    shaped = field.reshape(FRAMES, N_ROW, ROWS, N_COL, COLS, WIDTH)
    return shaped.transpose(1, 3, 0, 2, 4, 5).reshape(N_ROW * N_COL, FRAMES, ROWS, COLS, WIDTH)

def join_tiles(tiles):
    shaped = tiles.reshape(N_ROW, N_COL, FRAMES, ROWS, COLS, WIDTH)
    return shaped.transpose(2, 0, 3, 1, 4, 5).reshape(FRAMES, N_ROW * ROWS, N_COL * COLS, WIDTH)

def reference(block_input, cotangent, qkv_weight, proj_weight, expand_weight, reduce_weight, bias_table):
    height = ROWS * N_ROW
    breadth = COLS * N_COL
    plain = (qkv_weight[0], proj_weight[0], expand_weight[0], reduce_weight[0], bias_table[0])
    shifted = (qkv_weight[1], proj_weight[1], expand_weight[1], reduce_weight[1], bias_table[1])
    input_tiles = split_tiles(block_input.astype(jnp.float32))
    first = join_tiles(lax.map(lambda tile: block_tile(tile, plain, None), input_tiles))
    moved = split_tiles(jnp.roll(first, (-SHIFT, -SHIFT), axis=(1, 2)))
    turned = split_tiles(jnp.roll(cotangent, (-SHIFT, -SHIFT), axis=(1, 2)).astype(jnp.float32))
    starts = jnp.arange(N_ROW * N_COL, dtype=jnp.int32)

    def second_step(totals, item):
        tile, cot_tile, number = item
        masking = window_mask(number // N_COL * ROWS, number % N_COL * COLS, ROWS, COLS, height, breadth)
        unused, back = jax.vjp(lambda field, weights: block_tile(field, weights, masking), tile, shifted)
        tile_grad, weight_grads = back(cot_tile)
        return (tuple((total + piece.astype(jnp.float32) for total, piece in zip(totals, weight_grads))), tile_grad)
    zeros_two = tuple((jnp.zeros(piece.shape, jnp.float32) for piece in shifted))
    shift_grads, rolled_grad = lax.scan(second_step, zeros_two, (moved, turned, starts))
    middle = split_tiles(jnp.roll(join_tiles(rolled_grad), (SHIFT, SHIFT), axis=(1, 2)))

    def first_step(totals, item):
        tile, cot_tile = item
        unused, back = jax.vjp(lambda field, weights: block_tile(field, weights, None), tile, plain)
        tile_grad, weight_grads = back(cot_tile)
        return (tuple((total + piece.astype(jnp.float32) for total, piece in zip(totals, weight_grads))), tile_grad)
    zeros_one = tuple((jnp.zeros(piece.shape, jnp.float32) for piece in plain))
    plain_grads, input_tiles_grad = lax.scan(first_step, zeros_one, (input_tiles, middle))
    input_grad = join_tiles(input_tiles_grad)
    factor = 1.0 / jnp.sqrt(jnp.float32(FRAMES * height * breadth))
    stacked = [jnp.stack([plain_grads[member], shift_grads[member]]) * factor for member in range(5)]
    return (input_grad, stacked[0], stacked[1], stacked[2], stacked[3], stacked[4])
```

```python
import functools
import math

import jax
import jax.numpy as jnp
from jax import lax
from jax.experimental import pallas as pl
from jax.experimental.pallas import tpu as pltpu
from jax.sharding import PartitionSpec as P

WIN = 8
SHIFT = 4
BF = jnp.bfloat16
F32 = jnp.float32
LIMIT = 48 * 1024 * 1024
ROOT_HALF = 0.7071067811865476
DENSITY = 0.3989422804014327


def dot(a, b):
    return lax.dot_general(a, b, (((1,), (0,)), ((), ())), preferred_element_type=F32)


def dot_nt(a, b):
    return lax.dot_general(a, b, (((1,), (1,)), ((), ())), preferred_element_type=F32)


def dot_tn(a, b):
    return lax.dot_general(a, b, (((0,), (0,)), ((), ())), preferred_element_type=F32)


def iota(shape, axis):
    return lax.broadcasted_iota(jnp.int32, shape, axis)


def norm(field):
    center = field - jnp.mean(field, axis=0, keepdims=True)
    spread = jnp.mean(center * center, axis=0, keepdims=True)
    scale = lax.rsqrt(spread + 1e-05)
    return center * scale, scale


def norm_back(grad, normed, scale):
    along = jnp.mean(grad * normed, axis=0, keepdims=True)
    return scale * (grad - jnp.mean(grad, axis=0, keepdims=True) - normed * along)


def first_half(shape):
    return iota(shape, 1) < 64


def head_masks(heads, head):
    tall = (heads * 64, heads * head)
    wide = (heads * head, heads * 64)
    over = (iota(tall, 0) // 64 == iota(tall, 1) // head).astype(F32).astype(BF)
    across = (iota(wide, 0) // head == iota(wide, 1) // 64).astype(F32).astype(BF)
    return over, across


def spread_bias(table, heads):
    entries = table.shape[1]
    side = 2 * WIN - 1
    lanes = iota((entries, 256), 1)
    rows = iota((entries, 256), 0)
    place = lanes % 128
    down = place // 8 - 8
    right = place % 8 - jnp.where(lanes >= 128, 8, 0)
    wanted = (down + WIN - 1) * side + right + WIN - 1
    fits = (down >= 1 - WIN) & (right >= 1 - WIN)
    pick = (fits & (wanted == rows)).astype(F32)
    vectors = lax.dot_general(
        table, pick, (((1,), (0,)), ((), ())), precision=lax.Precision.HIGHEST, preferred_element_type=F32
    )
    ahead = jnp.broadcast_to(vectors[:, None, :128], (heads, 8, 128)).reshape(heads * 8, 128)
    behind = jnp.broadcast_to(vectors[:, None, 128:], (heads, 8, 128)).reshape(heads * 8, 128)
    shape = (heads * 8, 128)
    col_j = iota(shape, 0) % 8
    col_i = iota(shape, 1) % 8
    built = jnp.zeros(shape, F32)
    for c in range(8):
        line = jnp.where(col_i >= c, pltpu.roll(ahead, 64 + c, 1), pltpu.roll(behind, 56 + c, 1))
        built = jnp.where(col_j == c, line, built)
    rolled = [built] + [pltpu.roll(built, 8 * r, 1) for r in range(1, 8)]
    rolled = [jnp.where(first_half(shape), one, pltpu.roll(one, 64, 1)) for one in rolled]
    parts = []
    for h in range(heads):
        for r in range(8):
            parts.append(rolled[r][8 * h : 8 * h + 8])
    return jnp.concatenate(parts, axis=0)


def fold_bias(grad, heads):
    folded = jnp.where(first_half(grad.shape), grad + pltpu.roll(grad, 64, 1), 0.0)
    split = folded.reshape(heads, 8, 8, 128)
    total = jnp.zeros((heads * 8, 128), F32)
    for r in range(8):
        piece = split[:, r].reshape(heads * 8, 128)
        total = total + pltpu.roll(piece, 64 - 8 * r, 1)
    shape = (heads * 8, 128)
    col_j = iota(shape, 0) % 8
    col_i = iota(shape, 1) % 8
    ahead = jnp.zeros(shape, F32)
    behind = jnp.zeros(shape, F32)
    for c in range(8):
        mine = jnp.where((col_j == c) & (col_i >= c), total, 0.0)
        ahead = ahead + (pltpu.roll(mine, 128 - c, 1) if c else mine)
        rest = jnp.where((col_j == c) & (col_i < c), total, 0.0)
        behind = behind + pltpu.roll(rest, 8 - c, 1)
    ahead = jnp.sum(ahead.reshape(heads, 8, 128), axis=1)
    behind = jnp.sum(behind.reshape(heads, 8, 128), axis=1)
    return ahead, behind


def shift_mask(shape, last_row, last_col):
    j = iota(shape, 0) % 64
    lane = iota(shape, 1)
    i = lane % 64
    low = (j // 8 >= SHIFT) != (i // 8 >= SHIFT)
    side = (j % 8 >= SHIFT) != (i % 8 >= SHIFT)
    differ = (low & last_row) | (side & (lane >= 64) & last_col)
    return jnp.where(differ, -10000.0, 0.0)


def heads_of(weights, field, bias, heads):
    width, tokens = field.shape
    head = width // heads
    qkv_w, proj_w = weights[0][...], weights[1][...]
    over, across = head_masks(heads, head)
    normed, scale = norm(field)
    normed = normed.astype(BF)
    mixed = dot_tn(qkv_w, normed)
    query = (mixed[:width] * head ** (-0.5)).astype(BF)
    natural = mixed[width:].T.astype(BF)
    parts, probs, attended = [], [], []
    half = first_half((width, 128))
    for p in range(tokens // 128):
        lanes = slice(128 * p, 128 * p + 128)
        keys, values = mixed[width : 2 * width, lanes], mixed[2 * width :, lanes]
        pieces = []
        for field_t in (keys, values):
            swapped = pltpu.roll(field_t, 64, 1)
            pieces.append(
                [
                    jnp.concatenate([one.astype(BF)] * (heads // 2), axis=1) * across
                    for one in (jnp.where(half, field_t, swapped), jnp.where(half, swapped, field_t))
                ]
            )
        talls = []
        for which in range(2):
            talls.append(
                [
                    jnp.concatenate(
                        [natural[128 * p + 64 * w : 128 * p + 64 * w + 64, which * width : which * width + width]]
                        * heads,
                        axis=0,
                    )
                    * over
                    for w in range(2)
                ]
            )
        q = query[:, lanes]
        scores = jnp.where(first_half((heads * 64, 128)), dot(talls[0][0], q), dot(talls[0][1], q)) + bias
        scores = scores.reshape(heads, 64, 128)
        expos = jnp.exp(scores - jnp.max(scores, axis=1, keepdims=True))
        prob = (expos / jnp.sum(expos, axis=1, keepdims=True)).reshape(heads * 64, 128)
        prob_b = prob.astype(BF)
        attended.append(jnp.where(half, dot(pieces[1][0], prob_b), dot(pieces[1][1], prob_b)))
        probs.append(prob)
        parts.append((q, pieces[0], talls[1]))
    attended = jnp.concatenate(attended, axis=1).astype(BF)
    resid = field + dot_tn(proj_w, attended)
    return normed, scale, parts, probs, attended, resid


def forward(weights, field, bias, heads):
    expand_w, reduce_w = weights[2][...], weights[3][...]
    normed, scale, parts, probs, attended, resid = heads_of(weights, field, bias, heads)
    normed_two, scale_two = norm(resid)
    normed_two = normed_two.astype(BF)
    pre = dot_tn(expand_w, normed_two)
    bell = 0.5 * (1.0 + lax.erf(pre * ROOT_HALF))
    hidden = (pre * bell).astype(BF)
    result = resid + dot_tn(reduce_w, hidden)
    saved = (normed, scale, parts, probs, attended, resid, normed_two, scale_two, pre, bell, hidden)
    return result, saved


def backward(weights, field, saved, grad, heads):
    qkv_w, proj_w, expand_w, reduce_w = (w[...] for w in weights)
    normed, scale, parts, probs, attended, resid, normed_two, scale_two, pre, bell, hidden = saved
    width, tokens = field.shape
    head = width // heads
    over, across = head_masks(heads, head)
    grad_b = grad.astype(BF)
    grad_hidden = dot(reduce_w, grad_b).astype(BF).astype(F32)
    slope = bell + pre * (DENSITY * jnp.exp(-0.5 * pre * pre))
    grad_pre = (grad_hidden * slope).astype(BF)
    grad_two = dot(expand_w, grad_pre).astype(BF).astype(F32)
    center_two = resid - jnp.mean(resid, axis=0, keepdims=True)
    grad_resid = grad + norm_back(grad_two, center_two * scale_two, scale_two)
    grad_resid_b = grad_resid.astype(BF)
    grad_att = dot(proj_w, grad_resid_b)
    half = first_half((width, 128))
    tall_half = first_half((heads * 64, 128))
    grad_q, grad_k, grad_v = [], [], []
    grad_bias = jnp.zeros((heads * 64, 128), F32)
    for p in range(tokens // 128):
        query, keys_wide, values_tall = parts[p]
        prob = probs[p]
        prob_b = prob.astype(BF)
        att = grad_att[:, 128 * p : 128 * p + 128]
        att_b = att.astype(BF)
        zero = jnp.zeros_like(att)
        att_w = (jnp.where(half, att, zero).astype(BF), jnp.where(half, zero, att).astype(BF))
        query_f = query.astype(F32)
        query_w = (jnp.where(half, query_f, zero).astype(BF), jnp.where(half, zero, query_f).astype(BF))
        grad_prob = jnp.where(tall_half, dot(values_tall[0], att_b), dot(values_tall[1], att_b))
        grad_prob = grad_prob.astype(BF).astype(F32)
        along = jnp.sum((prob * grad_prob).reshape(heads, 64, 128), axis=1, keepdims=True)
        grad_score = prob * (grad_prob.reshape(heads, 64, 128) - along).reshape(heads * 64, 128)
        grad_bias = grad_bias + grad_score
        score_b = grad_score.astype(BF)
        grad_q.append(jnp.where(half, dot(keys_wide[0], score_b), dot(keys_wide[1], score_b)))
        for store, lhs, rhs in ((grad_k, query_w, score_b), (grad_v, att_w, prob_b)):
            both = []
            for w in range(2):
                full = dot_nt(lhs[w], rhs) * across.astype(F32)
                folded = sum(full[:, 128 * n : 128 * n + 128] for n in range(heads // 2))
                both.append(folded + pltpu.roll(folded, 64, 1))
            store.append(jnp.where(half, both[0], both[1]))
    grad_q = jnp.concatenate(grad_q, axis=1).astype(BF).astype(F32) * head ** (-0.5)
    grad_k = jnp.concatenate(grad_k, axis=1)
    grad_v = jnp.concatenate(grad_v, axis=1)
    grad_mixed = jnp.concatenate([grad_q, grad_k, grad_v], axis=0).astype(BF)
    grad_normed = dot(qkv_w, grad_mixed).astype(BF).astype(F32)
    center = field - jnp.mean(field, axis=0, keepdims=True)
    grad_field = grad_resid + norm_back(grad_normed, center * scale, scale)
    operands = (normed, grad_mixed, attended, grad_resid_b, normed_two, grad_pre, hidden, grad_b)
    return grad_field, operands, grad_bias


def pack_grads(operands, ahead, behind, buffer):
    normed, grad_mixed, attended, grad_resid, normed_two, grad_pre, hidden, grad = operands
    width = normed.shape[0]
    qkv = dot_nt(normed, grad_mixed)
    proj = dot_nt(attended, grad_resid)
    expand = dot_nt(normed_two, grad_pre)
    reduce = dot_nt(hidden, grad)
    inner = hidden.shape[0]
    at = 0

    def put(block):
        nonlocal at
        buffer[at : at + block.shape[0], :] = block.astype(BF)
        at += block.shape[0]

    full = 3 * width // 128
    for n in range(full):
        put(qkv[:, 128 * n : 128 * n + 128])
    put(jnp.concatenate([qkv[:, 128 * full :], proj[:, 128:]], axis=1))
    put(proj[:, :128])
    for n in range(inner // 128):
        put(expand[:, 128 * n : 128 * n + 128])
    put(reduce[:, :128])
    put(jnp.concatenate([reduce[: inner // 2, 128:], reduce[inner // 2 :, 128:]], axis=1))
    heads = ahead.shape[0]
    put(jnp.concatenate([ahead, behind, jnp.zeros((16 - 2 * heads, 128), F32)], axis=0))
    rest = buffer.shape[0] - at
    if rest:
        put(jnp.zeros((rest, 128), F32))


def unpack_grads(buffer, outs, block, factor):
    qkv, proj, expand, reduce, table = outs
    width, inner = qkv.shape[1], expand.shape[2]
    heads, entries = table.shape[1:]
    at = 0

    def take(rows):
        nonlocal at
        piece = buffer[at : at + rows, :].astype(F32) * factor
        at += rows
        return piece

    full = 3 * width // 128
    for n in range(full):
        qkv[block, :, 128 * n : 128 * n + 128] = take(width)
    shared = take(width)
    qkv[block, :, 128 * full :] = shared[:, :64]
    proj[block, :, 128:] = shared[:, 64:]
    proj[block, :, :128] = take(width)
    for n in range(inner // 128):
        expand[block, :, 128 * n : 128 * n + 128] = take(width)
    reduce[block, :, :128] = take(inner)
    shared = take(inner // 2)
    reduce[block, : inner // 2, 128:] = shared[:, :64]
    reduce[block, inner // 2 :, 128:] = shared[:, 64:]
    vectors = buffer[at : at + 16, :]
    side = 2 * WIN - 1
    shape = (128, entries)
    rows, lanes = iota(shape, 0), iota(shape, 1)
    down, right = lanes // side - (WIN - 1), lanes % side - (WIN - 1)
    base = 8 * (down + 8) + right
    ahead = ((right >= 0) & (base == rows)).astype(F32).astype(BF)
    behind = ((right < 0) & (base + 8 == rows)).astype(F32).astype(BF)
    table[block] = (dot(vectors, ahead)[:heads] + dot(vectors, behind)[heads : 2 * heads]) * factor


def tokens_of(read):
    flat = [read(f, c).reshape(64, -1) for f in range(2) for c in range(2)]
    return jnp.concatenate(flat, axis=0).T


def plain_forward(x_ref, qkv, proj, expand, reduce, table, first, top, left, corner, tight):
    heads = table.shape[0]
    field = tokens_of(lambda f, c: x_ref[f, :, 8 * c : 8 * c + 8, :].astype(F32))
    result, _ = forward((qkv, proj, expand, reduce), field, spread_bias(table[...], heads), heads)
    natural = result.T
    for f in range(2):
        for c in range(2):
            n = 64 * (2 * f + c)
            first[f, :, 8 * c : 8 * c + 8, :] = natural[n : n + 64].reshape(8, 8, -1)
    top[...] = first[:, :SHIFT].astype(BF)
    for f in range(2):
        for r in range(4):
            n = 16 * f + 4 * r
            tight[n : n + 4, :] = first[f, r, :4, :]
            tight[32 + n : 36 + n, :] = first[f, 4 + r, :4, :]
    corner[...] = tight[:32].astype(BF)
    left[...] = tight[32:].astype(BF)


def shifted_block(
    n_row, n_col, first, below, beside, across, cot, cot_below, cot_beside, cot_across, qkv, proj, expand, reduce, table,
    own, bottom, right, corner, normed, grad_mixed, attended, grad_resid, normed_two, grad_pre, hidden, grad, lines,
    moved, turned, tight,
):
    heads = table.shape[0]
    moved[:, :4, :16, :] = first[:, 4:, :, :]
    moved[:, 4:, :16, :] = below[...].astype(F32)
    turned[:, :4, :16, :] = cot[:, 4:, :, :].astype(F32)
    turned[:, 4:, :16, :] = cot_below[:, :4, :, :].astype(F32)
    turned[:, :4, 16:, :] = cot_beside[:, 4:, :8, :].astype(F32)
    turned[:, 4:, 16:, :] = cot_across[:, :4, :8, :].astype(F32)
    tight[:32] = across[...].astype(F32)
    tight[32:] = beside[...].astype(F32)
    for f in range(2):
        for r in range(4):
            n = 16 * f + 4 * r
            moved[f, 4 + r, 16:20, :] = tight[n : n + 4, :]
            moved[f, r, 16:20, :] = tight[32 + n : 36 + n, :]
    field = tokens_of(lambda f, c: moved[f, :, 4 + 8 * c : 12 + 8 * c, :])
    cotangent = tokens_of(lambda f, c: turned[f, :, 4 + 8 * c : 12 + 8 * c, :])
    last_row = lax.axis_index("row") == n_row - 1
    last_col = lax.axis_index("col") == n_col - 1
    bias = spread_bias(table[...], heads)
    bias = bias + shift_mask(bias.shape, last_row, last_col)
    weights = (qkv, proj, expand, reduce)
    _, saved = forward(weights, field, bias, heads)
    grad_field, operands, grad_bias = backward(weights, field, saved, cotangent, heads)
    natural = grad_field.T
    for f in range(2):
        for c in range(2):
            n = 64 * (2 * f + c)
            moved[f, :, 4 + 8 * c : 12 + 8 * c, :] = natural[n : n + 64].reshape(8, 8, -1)
    own[...] = moved[:, :4, :16, :]
    bottom[...] = moved[:, 4:, :16, :].astype(BF)
    for f in range(2):
        for r in range(4):
            n = 16 * f + 4 * r
            tight[n : n + 4, :] = moved[f, 4 + r, 16:20, :]
            tight[32 + n : 36 + n, :] = moved[f, r, 16:20, :]
    corner[...] = tight[:32].astype(BF)
    right[...] = tight[32:].astype(BF)
    for ref, value in zip(
        (normed, grad_mixed, attended, grad_resid, normed_two, grad_pre, hidden, grad), operands, strict=True
    ):
        ref[...] = value
    lines[...] = grad_bias


def split_core(buffer, keep, send):
    rows = keep.shape[0]
    core = lax.axis_index("row") % 2
    keep[...] = buffer[pl.ds(pl.multiple_of(core * rows, 16), rows), :]
    send[...] = buffer[pl.ds(pl.multiple_of((1 - core) * rows, 16), rows), :]


def shifted_grads(heads, normed, grad_mixed, attended, grad_resid, normed_two, grad_pre, hidden, grad, lines, keep, send, buffer):
    operands = tuple(
        ref[...] for ref in (normed, grad_mixed, attended, grad_resid, normed_two, grad_pre, hidden, grad)
    )
    ahead, behind = fold_bias(lines[...], heads)
    pack_grads(operands, ahead, behind, buffer)
    split_core(buffer, keep, send)


def plain_backward(
    x_ref, own, above, beside, across, qkv, proj, expand, reduce, table, out, keep, send, middle, tight, buffer
):
    heads = table.shape[0]
    field = tokens_of(lambda f, c: x_ref[f, :, 8 * c : 8 * c + 8, :].astype(F32))
    middle[:, 4:] = own[...]
    middle[:, :4] = above[...].astype(F32)
    tight[:32] = across[...].astype(F32)
    tight[32:] = beside[...].astype(F32)
    for f in range(2):
        for r in range(4):
            n = 16 * f + 4 * r
            middle[f, r, :4, :] = tight[n : n + 4, :]
            middle[f, 4 + r, :4, :] = tight[32 + n : 36 + n, :]
    cotangent = tokens_of(lambda f, c: middle[f, :, 8 * c : 8 * c + 8, :])
    weights = (qkv, proj, expand, reduce)
    _, saved = forward(weights, field, spread_bias(table[...], heads), heads)
    grad_field, operands, grad_bias = backward(weights, field, saved, cotangent, heads)
    natural = grad_field.T
    for f in range(2):
        for c in range(2):
            n = 64 * (2 * f + c)
            out[f, :, 8 * c : 8 * c + 8, :] = natural[n : n + 64].reshape(8, 8, -1)
    ahead, behind = fold_bias(grad_bias, heads)
    pack_grads(operands, ahead, behind, buffer)
    split_core(buffer, keep, send)


def near_place():
    return lax.axis_index("row") // 2 * 2 + lax.axis_index("col") % 2


def add_core(keep, came, own, *rest):
    sends, total = rest[:-1], rest[-1]
    total[...] = keep[...].astype(F32) + came[...].astype(F32)
    rows = own.shape[0]
    me = near_place()
    own[...] = total[pl.ds(pl.multiple_of(me * rows, 16), rows), :]
    for d, send in enumerate(sends):
        send[...] = total[pl.ds(pl.multiple_of((me ^ (d + 1)) * rows, 16), rows), :].astype(BF)


def add_near(count, *refs):
    ins, own, sends, total = refs[:4], refs[4], refs[5 : 4 + count], refs[-1]
    total[...] = ins[0][...] + sum(one[...].astype(F32) for one in ins[1:])
    rows = own.shape[0]
    me = lax.axis_index("col") // 2
    own[...] = total[pl.ds(pl.multiple_of(me * rows, 16), rows), :]
    for d, send in enumerate(sends):
        send[...] = total[pl.ds(pl.multiple_of((me ^ (d + 1)) * rows, 16), rows), :].astype(BF)


def add_far(*refs):
    ins, out = refs[:-1], refs[-1]
    out[...] = (ins[0][...] + sum(one[...].astype(F32) for one in ins[1:])).astype(BF)


def join_far(*refs):
    ins, out = refs[:-1], refs[-1]
    rows = ins[0].shape[0]
    me = lax.axis_index("col") // 2
    for d, piece in enumerate(ins):
        out[pl.ds(pl.multiple_of((me ^ d) * rows, 16), rows), :] = piece[...]


def finish(factor, *refs):
    ins, outs, buffer = refs[:16], refs[16:21], refs[21]
    rows = ins[0].shape[0]
    me = near_place()
    core = lax.axis_index("row") % 2
    for block in range(2):
        for n in range(8):
            where = (core ^ (n // 4)) * 4 + (me ^ (n % 4))
            buffer[pl.ds(pl.multiple_of(where * rows, 16), rows), :] = ins[8 * block + n][...]
        unpack_grads(buffer, outs, block, factor)


def call(kernel, outs, scratch, args, block=None, weights=0):
    specs = []
    for n, arg in enumerate(args):
        if n >= len(args) - weights:
            specs.append(pl.BlockSpec((None,) + arg.shape[1:], lambda _, k=arg.ndim: (block,) + (0,) * (k - 1)))
        else:
            specs.append(pl.BlockSpec(arg.shape, lambda _, k=arg.ndim: (0,) * k))
    return pl.pallas_call(
        kernel,
        grid=(1,),
        in_specs=specs,
        out_specs=[pl.BlockSpec(s, lambda _, k=len(s): (0,) * k) for s, _ in outs],
        out_shape=[jax.ShapeDtypeStruct(s, d) for s, d in outs],
        scratch_shapes=[pltpu.VMEM(s, d) for s, d in scratch],
        compiler_params=pltpu.CompilerParams(vmem_limit_bytes=LIMIT),
    )(*args)


def local(block_input, cotangent, qkv_weight, proj_weight, expand_weight, reduce_weight, bias_table):
    frames, rows, cols, width = block_input.shape
    n_row, n_col = lax.axis_size("row"), lax.axis_size("col")
    inner = expand_weight.shape[2]
    heads = bias_table.shape[1]
    tokens = frames * rows * cols
    weights = (qkv_weight, proj_weight, expand_weight, reduce_weight, bias_table)
    axes = ("row", "col")

    def send(block, down, right):
        route = [
            (r * n_col + c, (r + down) % n_row * n_col + (c + right) % n_col)
            for r in range(n_row)
            for c in range(n_col)
        ]
        return lax.ppermute(block, axes, route)

    def swap(block, row_bits, col_bits):
        route = [
            (r * n_col + c, (r ^ row_bits) * n_col + (c ^ col_bits)) for r in range(n_row) for c in range(n_col)
        ]
        return lax.ppermute(block, axes, route)

    cots = [cotangent, send(cotangent, -1, 0), send(cotangent, 0, -1), send(cotangent, -1, -1)]
    tile = (frames, rows, cols, width)
    strip = (frames, SHIFT, cols, width)
    small = (frames * SHIFT * SHIFT, width)
    tight = ((2 * small[0], width), F32)
    first, top, left, corner = call(
        plain_forward, [(tile, F32), (strip, BF), (small, BF), (small, BF)], [tight], [block_input, *weights], 0, 5
    )
    halo = [first, send(top, -1, 0), send(left, 0, -1), send(corner, -1, -1)]
    kinds = [(n, tokens) for n in (width, 3 * width, width, width, width, inner, inner, width)]
    outs = call(
        functools.partial(shifted_block, n_row, n_col),
        [(strip, F32), (strip, BF), (small, BF), (small, BF)]
        + [(kind, BF) for kind in kinds]
        + [((heads * 64, 128), F32)],
        [((frames, rows, cols + 8, width), F32)] * 2 + [tight],
        [*halo, *cots, *weights],
        1,
        5,
    )
    back = [outs[0], send(outs[1], 1, 0), send(outs[2], 0, 1), send(outs[3], 1, 1)]

    far = n_col // 2
    unit = 8 * far * 16
    used = (3 * width + width + inner) * width // 128 + inner * width // 128 + 16
    size = -(-used // unit) * unit
    chunk = size // (8 * far)
    halves = [((size // 2, 128), BF)] * 2
    buffer = ((size, 128), BF)

    def reduce_all(keep, came_from):
        came = swap(came_from, 1, 0)
        quarter = (size // 8, 128)
        own, *sends = call(add_core, [(quarter, F32)] + [(quarter, BF)] * 3, [((size // 2, 128), F32)], [keep, came])
        near = [own] + [swap(one, (d & 2), d & 1) for d, one in enumerate(sends, 1)]
        own, *sends = call(
            functools.partial(add_near, far),
            [((chunk, 128), F32)] + [((chunk, 128), BF)] * (far - 1),
            [(quarter, F32)],
            near,
        )
        distant = [own] + [swap(one, 0, 2 * d) for d, one in enumerate(sends, 1)]
        (done,) = call(add_far, [((chunk, 128), BF)], [], distant)
        distant = [done] + [swap(done, 0, 2 * d) for d in range(1, far)]
        (joined,) = call(join_far, [(quarter, BF)], [], distant)
        near = [joined] + [swap(joined, (d & 2), d & 1) for d in range(1, 4)]
        return near + [swap(one, 1, 0) for one in near]

    keep, away = call(functools.partial(shifted_grads, heads), halves, [buffer], list(outs[4:]))
    shifted = reduce_all(keep, away)
    input_grad, keep, away = call(
        plain_backward,
        [(tile, F32), *halves],
        [(tile, F32), tight, buffer],
        [block_input, *back, *weights],
        0,
        5,
    )
    plain = reduce_all(keep, away)
    factor = 1.0 / math.sqrt(frames * rows * n_row * cols * n_col)
    grads = call(
        functools.partial(finish, factor), [(w.shape, F32) for w in weights], [buffer], plain + shifted
    )
    return (input_grad, *grads)


def solution(mesh):
    in_specs = (P(None, "row", "col", None), P(None, "row", "col", None), P(), P(), P(), P(), P())
    out_specs = (P(None, "row", "col", None), P(), P(), P(), P(), P())
    return jax.shard_map(local, mesh=mesh, in_specs=in_specs, out_specs=out_specs, check_vma=False)
```

```python
import functools
import math

import jax
import jax.numpy as jnp
from jax import lax
from jax.experimental import pallas as pl
from jax.experimental.pallas import tpu as pltpu
from jax.sharding import PartitionSpec as P

WIN = 8
SHIFT = 4
BF = jnp.bfloat16
F32 = jnp.float32
LIMIT = 48 * 1024 * 1024
FULL = 62 * 1024 * 1024
ROOT_HALF = 0.7071067811865476
DENSITY = 0.3989422804014327


def dot(a, b):
    return lax.dot_general(a, b, (((1,), (0,)), ((), ())), preferred_element_type=F32)


def dot_nt(a, b):
    return lax.dot_general(a, b, (((1,), (1,)), ((), ())), preferred_element_type=F32)


def dot_tn(a, b):
    return lax.dot_general(a, b, (((0,), (0,)), ((), ())), preferred_element_type=F32)


def iota(shape, axis):
    return lax.broadcasted_iota(jnp.int32, shape, axis)


def norm(field):
    center = field - jnp.mean(field, axis=0, keepdims=True)
    spread = jnp.mean(center * center, axis=0, keepdims=True)
    scale = lax.rsqrt(spread + 1e-05)
    return center * scale, scale


def norm_back(grad, normed, scale):
    along = jnp.mean(grad * normed, axis=0, keepdims=True)
    return scale * (grad - jnp.mean(grad, axis=0, keepdims=True) - normed * along)


class Late:
    def __init__(self, copy, here):
        self.copy, self.here = copy, here

    def __getitem__(self, index):
        if self.copy is not None:
            self.copy.wait()
            self.copy = None
        return self.here[index]


def first_half(shape):
    return iota(shape, 1) < 64


def head_masks(heads, head):
    tall = (heads * 64, heads * head)
    wide = (heads * head, heads * 64)
    over = (iota(tall, 0) // 64 == iota(tall, 1) // head).astype(F32).astype(BF)
    across = (iota(wide, 0) // head == iota(wide, 1) // 64).astype(F32).astype(BF)
    return over, across


def spread_bias(table, heads):
    entries = table.shape[1]
    side = 2 * WIN - 1
    lanes = iota((entries, 256), 1)
    rows = iota((entries, 256), 0)
    place = lanes % 128
    down = place // 8 - 8
    right = place % 8 - jnp.where(lanes >= 128, 8, 0)
    wanted = (down + WIN - 1) * side + right + WIN - 1
    fits = (down >= 1 - WIN) & (right >= 1 - WIN)
    pick = (fits & (wanted == rows)).astype(F32)
    vectors = lax.dot_general(
        table, pick, (((1,), (0,)), ((), ())), precision=lax.Precision.HIGHEST, preferred_element_type=F32
    )
    ahead = jnp.broadcast_to(vectors[:, None, :128], (heads, 8, 128)).reshape(heads * 8, 128)
    behind = jnp.broadcast_to(vectors[:, None, 128:], (heads, 8, 128)).reshape(heads * 8, 128)
    shape = (heads * 8, 128)
    col_j = iota(shape, 0) % 8
    col_i = iota(shape, 1) % 8
    built = jnp.zeros(shape, F32)
    for c in range(8):
        line = jnp.where(col_i >= c, pltpu.roll(ahead, 64 + c, 1), pltpu.roll(behind, 56 + c, 1))
        built = jnp.where(col_j == c, line, built)
    rolled = [built] + [pltpu.roll(built, 8 * r, 1) for r in range(1, 8)]
    rolled = [jnp.where(first_half(shape), one, pltpu.roll(one, 64, 1)) for one in rolled]
    parts = []
    for h in range(heads):
        for r in range(8):
            parts.append(rolled[r][8 * h : 8 * h + 8])
    return jnp.concatenate(parts, axis=0)


def fold_bias(grad, heads):
    folded = jnp.where(first_half(grad.shape), grad + pltpu.roll(grad, 64, 1), 0.0)
    split = folded.reshape(heads, 8, 8, 128)
    total = jnp.zeros((heads * 8, 128), F32)
    for r in range(8):
        piece = split[:, r].reshape(heads * 8, 128)
        total = total + pltpu.roll(piece, 64 - 8 * r, 1)
    shape = (heads * 8, 128)
    col_j = iota(shape, 0) % 8
    col_i = iota(shape, 1) % 8
    ahead = jnp.zeros(shape, F32)
    behind = jnp.zeros(shape, F32)
    for c in range(8):
        mine = jnp.where((col_j == c) & (col_i >= c), total, 0.0)
        ahead = ahead + (pltpu.roll(mine, 128 - c, 1) if c else mine)
        rest = jnp.where((col_j == c) & (col_i < c), total, 0.0)
        behind = behind + pltpu.roll(rest, 8 - c, 1)
    ahead = jnp.sum(ahead.reshape(heads, 8, 128), axis=1)
    behind = jnp.sum(behind.reshape(heads, 8, 128), axis=1)
    return ahead, behind


def shift_mask(shape, last_row, last_col):
    j = iota(shape, 0) % 64
    lane = iota(shape, 1)
    i = lane % 64
    low = (j // 8 >= SHIFT) != (i // 8 >= SHIFT)
    side = (j % 8 >= SHIFT) != (i % 8 >= SHIFT)
    differ = (low & last_row) | (side & (lane >= 64) & last_col)
    return jnp.where(differ, -10000.0, 0.0)


def wide_of(field, heads, across):
    field = field.astype(F32)
    half = first_half(field.shape)
    swapped = pltpu.roll(field, 64, 1)
    return [
        jnp.concatenate([one.astype(BF)] * (heads // 2), axis=1) * across
        for one in (jnp.where(half, field, swapped), jnp.where(half, swapped, field))
    ]


def tall_of(natural, heads, over):
    return [jnp.concatenate([natural[64 * w : 64 * w + 64]] * heads, axis=0) * over for w in range(2)]


def forward(weights, field, bias, heads):
    width, tokens = field.shape
    head = width // heads
    over, across = head_masks(heads, head)
    center, scale = norm(field)
    normed = center.astype(BF)
    mixed = dot_tn(weights[0][...], normed)
    query = (mixed[:width] * head ** (-0.5)).astype(BF)
    keys = mixed[width : 2 * width].astype(BF)
    natural = mixed[width:].T.astype(BF)
    values = natural[:, width:]
    probs, attended = [], []
    half = first_half((width, 128))
    tall_half = first_half((heads * 64, 128))
    for p in range(tokens // 128):
        lanes = slice(128 * p, 128 * p + 128)
        wide = wide_of(mixed[2 * width :, lanes], heads, across)
        tall = tall_of(natural[lanes, :width], heads, over)
        q = query[:, lanes]
        scores = jnp.where(tall_half, dot(tall[0], q), dot(tall[1], q)) + bias
        scores = scores.reshape(heads, 64, 128)
        expos = jnp.exp(scores - jnp.max(scores, axis=1, keepdims=True))
        prob = (expos / jnp.sum(expos, axis=1, keepdims=True)).reshape(heads * 64, 128)
        prob_b = prob.astype(BF)
        attended.append(jnp.where(half, dot(wide[0], prob_b), dot(wide[1], prob_b)))
        probs.append(prob)
    attended = jnp.concatenate(attended, axis=1).astype(BF)
    prob = jnp.concatenate(probs, axis=1)
    resid = field + dot_tn(weights[1][...], attended)
    center_two, scale_two = norm(resid)
    normed_two = center_two.astype(BF)
    pre = dot_tn(weights[2][...], normed_two)
    bell = 0.5 * (1.0 + lax.erf(pre * ROOT_HALF))
    hidden = (pre * bell).astype(BF)
    saved = (center, scale, query, keys, values, prob, attended, center_two, scale_two, hidden)
    return resid, hidden, pre, bell, saved


def slope_of(pre, bell):
    return bell + pre * (DENSITY * jnp.exp(-0.5 * pre * pre))


def backward(weights, saved, slope, grad, heads):
    qkv_w, proj_w, expand_w, reduce_w = (w[...] for w in weights)
    center, scale, query, keys, values, prob, attended, center_two, scale_two, hidden = saved
    width, tokens = grad.shape
    head = width // heads
    over, across = head_masks(heads, head)
    grad_b = grad.astype(BF)
    grad_hidden = dot_tn(reduce_w, grad_b).astype(BF).astype(F32)
    grad_pre = (grad_hidden * slope).astype(BF)
    grad_two = dot(expand_w, grad_pre).astype(BF).astype(F32)
    grad_resid = grad + norm_back(grad_two, center_two, scale_two)
    grad_resid_b = grad_resid.astype(BF)
    grad_att = dot(proj_w, grad_resid_b)
    half = first_half((width, 128))
    tall_half = first_half((heads * 64, 128))
    across_f = across.astype(F32)
    grad_q, grad_k, grad_v = [], [], []
    grad_bias = jnp.zeros((heads * 64, 128), F32)
    for p in range(tokens // 128):
        lanes = slice(128 * p, 128 * p + 128)
        tall = tall_of(values[lanes], heads, over)
        wide = wide_of(keys[:, lanes], heads, across)
        p_f = prob[:, lanes]
        p_b = p_f.astype(BF)
        att = grad_att[:, lanes]
        att_b = att.astype(BF)
        zero = jnp.zeros_like(att)
        att_w = (jnp.where(half, att, zero).astype(BF), jnp.where(half, zero, att).astype(BF))
        query_f = query[:, lanes].astype(F32)
        query_w = (jnp.where(half, query_f, zero).astype(BF), jnp.where(half, zero, query_f).astype(BF))
        grad_prob = jnp.where(tall_half, dot(tall[0], att_b), dot(tall[1], att_b))
        grad_prob = grad_prob.astype(BF).astype(F32)
        along = jnp.sum((p_f * grad_prob).reshape(heads, 64, 128), axis=1, keepdims=True)
        grad_score = p_f * (grad_prob.reshape(heads, 64, 128) - along).reshape(heads * 64, 128)
        grad_bias = grad_bias + grad_score
        score_b = grad_score.astype(BF)
        grad_q.append(jnp.where(half, dot(wide[0], score_b), dot(wide[1], score_b)))
        for store, lhs, rhs in ((grad_k, query_w, score_b), (grad_v, att_w, p_b)):
            both = []
            for w in range(2):
                full = dot_nt(lhs[w], rhs) * across_f
                folded = sum(full[:, 128 * n : 128 * n + 128] for n in range(heads // 2))
                both.append(folded + pltpu.roll(folded, 64, 1))
            store.append(jnp.where(half, both[0], both[1]))
    grad_q = jnp.concatenate(grad_q, axis=1).astype(BF).astype(F32) * head ** (-0.5)
    grad_k = jnp.concatenate(grad_k, axis=1)
    grad_v = jnp.concatenate(grad_v, axis=1)
    grad_mixed = jnp.concatenate([grad_q, grad_k, grad_v], axis=0).astype(BF)
    grad_normed = dot(qkv_w, grad_mixed).astype(BF).astype(F32)
    grad_field = grad_resid + norm_back(grad_normed, center, scale)
    operands = (center.astype(BF), grad_mixed, attended, grad_resid_b, center_two.astype(BF), grad_pre, hidden, grad_b)
    return grad_field, operands, grad_bias


def pack_grads(operands, ahead, behind, buffer):
    normed, grad_mixed, attended, grad_resid, normed_two, grad_pre, hidden, grad = operands
    width = normed.shape[0]
    qkv = dot_nt(normed, grad_mixed)
    proj = dot_nt(attended, grad_resid)
    expand = dot_nt(normed_two, grad_pre)
    reduce = dot_nt(grad, hidden)
    inner = hidden.shape[0]
    at = 0

    def put(block):
        nonlocal at
        buffer[at : at + block.shape[0], :] = block.astype(BF)
        at += block.shape[0]

    full = 3 * width // 128
    for n in range(full):
        put(qkv[:, 128 * n : 128 * n + 128])
    put(jnp.concatenate([qkv[:, 128 * full :], proj[:, 128:]], axis=1))
    put(proj[:, :128])
    for one in (expand, reduce):
        for n in range(inner // 128):
            put(one[:, 128 * n : 128 * n + 128])
    heads = ahead.shape[0]
    put(jnp.concatenate([ahead, behind, jnp.zeros((16 - 2 * heads, 128), F32)], axis=0))
    rest = buffer.shape[0] - at
    if rest:
        put(jnp.zeros((rest, 128), F32))


def unpack_grads(buffer, outs, block, factor):
    qkv, proj, expand, reduce, table = outs
    width, inner = expand.shape[1:]
    heads, _, entries = table.shape
    at = 0

    def take(rows):
        nonlocal at
        piece = buffer[at : at + rows, :].astype(F32) * factor
        at += rows
        return piece

    full = 3 * width // 128
    for n in range(full):
        qkv[block, :, 128 * n : 128 * n + 128] = take(width)
    shared = take(width)
    qkv[block, :, 128 * full :] = shared[:, :64]
    proj[block, :, 128:] = shared[:, 64:]
    proj[block, :, :128] = take(width)
    for one in (expand, reduce):
        for n in range(inner // 128):
            one[block, :, 128 * n : 128 * n + 128] = take(width)
    vectors = buffer[at : at + 16, :]
    side = 2 * WIN - 1
    shape = (128, entries)
    rows, lanes = iota(shape, 0), iota(shape, 1)
    down, right = lanes // side - (WIN - 1), lanes % side - (WIN - 1)
    base = 8 * (down + 8) + right
    ahead = ((right >= 0) & (base == rows)).astype(F32).astype(BF)
    behind = ((right < 0) & (base + 8 == rows)).astype(F32).astype(BF)
    table[:, block, :] = (dot(vectors, ahead)[:heads] + dot(vectors, behind)[heads : 2 * heads]) * factor


def tokens_of(read):
    flat = [read(f, c).reshape(64, -1) for f in range(2) for c in range(2)]
    return jnp.concatenate(flat, axis=0).T


def tile_of(field, write):
    natural = field.T
    for f in range(2):
        for c in range(2):
            n = 64 * (2 * f + c)
            write(f, c, natural[n : n + 64].reshape(8, 8, -1))


def corners():
    return [(f, r, 16 * f + 4 * r) for f in range(2) for r in range(4)]


def plain_forward(x_far, cot_far, table_far, *refs):
    far, (first, top, left, corner, tight), near, done = refs[:4], refs[4:9], refs[9:17], refs[17]
    heads = table_far.shape[0]
    qkv_far, *rest = (there.at[0] for there in far)
    pairs = [(x_far, near[0]), (qkv_far, near[1]), *zip(rest, near[2:5], strict=True)]
    pairs[1:1] = [(table_far, near[7])]
    pairs.append((cot_far, near[5]))
    copies = [pltpu.make_async_copy(there, here, done.at[n]) for n, (there, here) in enumerate(pairs)]
    for copy in copies:
        copy.start()
    x_ref, table, qkv, proj, expand, reduce, cot = (
        Late(copy, here) for copy, (_, here) in zip(copies, pairs, strict=True)
    )
    whole = near[6]

    def write(f, c, piece):
        whole[f, :, 8 * c : 8 * c + 8, :] = piece

    bias = spread_bias(table[:, 0, :], heads)
    field = tokens_of(lambda f, c: x_ref[f, :, 8 * c : 8 * c + 8, :].astype(F32))
    resid, hidden, _, _, _ = forward((qkv, proj, expand), field, bias, heads)
    tile_of(resid + dot(reduce[...], hidden), write)
    first[...] = whole[:, SHIFT:]
    top[0] = whole[:, :SHIFT].astype(BF)
    top[1] = cot[:, :SHIFT]
    for f, r, n in corners():
        tight[n : n + 4, :] = whole[f, r, :4, :]
        tight[32 + n : 36 + n, :] = cot[f, r, :8, :].astype(F32)[:4]
        tight[64 + n : 68 + n, :] = whole[f, 4 + r, :4, :]
        tight[96 + n : 100 + n, :] = cot[f, 4 + r, :8, :].astype(F32)[:4]
    corner[...] = tight[:64].astype(BF)
    left[...] = tight[64:].astype(BF)


def keep_plain(n_row, n_col, x_ref, table, qkv, proj, expand, bias_out, slope_out, *outs):
    heads = table.shape[0]
    field = tokens_of(lambda f, c: x_ref[f, :, 8 * c : 8 * c + 8, :].astype(F32))
    _, _, pre, bell, saved = forward((qkv, proj, expand), field, spread_bias(table[:, 0, :], heads), heads)
    slope_out[...] = slope_of(pre, bell)
    for ref, value in zip(outs, saved, strict=True):
        ref[...] = value
    last_row = lax.axis_index("row") == n_row - 1
    last_col = lax.axis_index("col") == n_col - 1
    bias_out[...] = spread_bias(table[:, 1, :], heads) + shift_mask(bias_out.shape, last_row, last_col)


def shifted_block(
    first, cot, below, beside, across, bias, qkv, proj, expand, reduce,
    own, bottom, right, corner, keep, send, moved, turned, tight, buffer,
):
    heads = bias.shape[0] // 64
    moved[:, :4, :16, :] = first[...]
    moved[:, 4:, :16, :] = below[0].astype(F32)
    turned[:, :4, :16, :] = cot[:, 4:, :, :].astype(F32)
    turned[:, 4:, :16, :] = below[1].astype(F32)
    tight[:64] = across[...].astype(F32)
    tight[64:] = beside[...].astype(F32)
    for f, r, n in corners():
        moved[f, 4 + r, 16:20, :] = tight[n : n + 4, :]
        turned[f, 4 + r, 16:20, :] = tight[32 + n : 36 + n, :]
        moved[f, r, 16:20, :] = tight[64 + n : 68 + n, :]
        turned[f, r, 16:20, :] = tight[96 + n : 100 + n, :]
    field = tokens_of(lambda f, c: moved[f, :, 4 + 8 * c : 12 + 8 * c, :])
    cotangent = tokens_of(lambda f, c: turned[f, :, 4 + 8 * c : 12 + 8 * c, :])
    weights = (qkv, proj, expand, reduce)
    _, _, pre, bell, saved = forward(weights, field, bias[...], heads)
    grad_field, operands, grad_bias = backward(weights, saved, slope_of(pre, bell), cotangent, heads)

    def write(f, c, piece):
        moved[f, :, 4 + 8 * c : 12 + 8 * c, :] = piece

    tile_of(grad_field, write)
    own[...] = moved[:, :4, :16, :]
    bottom[...] = moved[:, 4:, :16, :].astype(BF)
    for f, r, n in corners():
        tight[n : n + 4, :] = moved[f, 4 + r, 16:20, :]
        tight[32 + n : 36 + n, :] = moved[f, r, 16:20, :]
    corner[...] = tight[:32].astype(BF)
    right[...] = tight[32:64].astype(BF)
    ahead, behind = fold_bias(grad_bias, heads)
    pack_grads(operands, ahead, behind, buffer)
    split_core(buffer, keep, send)


def split_core(buffer, keep, send):
    rows = keep.shape[0]
    core = lax.axis_index("row") % 2
    keep[...] = buffer[pl.ds(pl.multiple_of(core * rows, 16), rows), :]
    send[...] = buffer[pl.ds(pl.multiple_of((1 - core) * rows, 16), rows), :]


def plain_backward(own, above, beside, across, slope, *refs):
    saved, weights = refs[:10], refs[10:14]
    out, lines, outs, middle, tight = refs[14], refs[15], refs[16:21], refs[21], refs[22]
    heads = saved[5].shape[0] // 64
    middle[:, 4:] = own[...]
    middle[:, :4] = above[...].astype(F32)
    tight[:32] = across[...].astype(F32)
    tight[32:64] = beside[...].astype(F32)
    for f, r, n in corners():
        middle[f, r, :4, :] = tight[n : n + 4, :]
        middle[f, 4 + r, :4, :] = tight[32 + n : 36 + n, :]
    cotangent = tokens_of(lambda f, c: middle[f, :, 8 * c : 8 * c + 8, :])
    saved = tuple(ref[...] for ref in saved)
    grad_field, operands, grad_bias = backward(weights, saved, slope[...], cotangent, heads)

    def write(f, c, piece):
        out[f, :, 8 * c : 8 * c + 8, :] = piece

    tile_of(grad_field, write)
    lines[...] = grad_bias
    for ref, n in zip(outs, (0, 1, 3, 5, 7), strict=True):
        ref[...] = operands[n]


def plain_grads(normed, mixed, attended, resid, two, pre, hidden, grad, lines, mine, one, *refs):
    two_came, three_came, keep, send, done, buffer = refs
    kept = (normed, mixed, attended, resid, two, pre, hidden, grad)
    ahead, behind = fold_bias(lines[...], lines.shape[0] // 64)
    pack_grads(tuple(ref[...].astype(BF) for ref in kept), ahead, behind, buffer)
    split_core(buffer, keep, send)
    done[...] = mine[...] + one[...].astype(F32) + two_came[...].astype(F32) + three_came[...].astype(F32)


def near_place():
    return lax.axis_index("row") // 2 * 2 + lax.axis_index("col") % 2


def cut(total, me, own, sends, here=slice(None)):
    rows = total.shape[0] // (len(sends) + 1)
    own[here, :] = total[pl.ds(pl.multiple_of(me * rows, 16), rows), :]
    for d, send in enumerate(sends, 1):
        send[here, :] = total[pl.ds(pl.multiple_of((me ^ d) * rows, 16), rows), :].astype(BF)


def add_core(keep, came, own, *rest):
    sends, total = rest[:-1], rest[-1]
    total[...] = keep[...].astype(F32) + came[...].astype(F32)
    cut(total, near_place(), own, sends)


def add_near(count, mine, one, two, three, other, own, *rest):
    sends, total = rest[: count - 1], rest[-1]
    rows = own.shape[0] // 2
    place = lax.axis_index("col") // 2
    total[...] = mine[...] + one[...].astype(F32) + two[...].astype(F32) + three[...].astype(F32)
    cut(total, place, own, sends, slice(0, rows))
    cut(other, place, own, sends, slice(rows, 2 * rows))


def add_far(*refs):
    ins, out = refs[:-1], refs[-1]
    out[...] = (ins[0][...] + sum(one[...].astype(F32) for one in ins[1:])).astype(BF)


def join_far(*refs):
    ins, out = refs[:-1], refs[-1]
    rows, length = ins[0].shape[0] // 2, out.shape[0] // 2
    me = lax.axis_index("col") // 2
    for d, piece in enumerate(ins):
        for block in range(2):
            there = pl.multiple_of(block * length + (me ^ d) * rows, 16)
            out[pl.ds(there, rows), :] = piece[block * rows : block * rows + rows, :]


def finish(factor, *refs):
    ins, outs, buffer, done, stage = refs[:8], refs[8:13], refs[13], refs[14], refs[15:20]
    rows = ins[0].shape[0] // 2
    me = near_place()
    core = lax.axis_index("row") % 2
    copies = []
    for block in range(2):
        for n in range(8):
            where = (core ^ (n // 4)) * 4 + (me ^ (n % 4))
            piece = ins[n][block * rows : block * rows + rows, :]
            buffer[pl.ds(pl.multiple_of(where * rows, 16), rows), :] = piece
        unpack_grads(buffer, stage, block, factor)
        for n in range(4):
            copies.append(pltpu.make_async_copy(stage[n].at[block], outs[n].at[block], done.at[4 * block + n]))
            copies[-1].start()
    copies.append(pltpu.make_async_copy(stage[4], outs[4], done.at[8]))
    copies[-1].start()
    for copy in copies:
        copy.wait()


class Whole:
    def __init__(self, ref, block):
        self.ref, self.block = ref, block

    def __getitem__(self, index):
        return self.ref[self.block]


def call(kernel, outs, scratch, args, stacked=(), distant=(), micros=0.5, limit=LIMIT, far_outs=False):
    here, there = pl.BlockSpec(memory_space=pltpu.VMEM), pl.BlockSpec(memory_space=pltpu.HBM)
    count = len(args)

    def body(*refs):
        weights = [Whole(ref, block) for ref, (_, block) in zip(refs[count:], stacked)]
        kernel(*refs[:count], *weights, *refs[count + len(stacked) :])

    return pl.pallas_call(
        body,
        in_specs=[here] * (count + len(stacked)) + [there] * len(distant),
        out_specs=[there if far_outs else here] * len(outs),
        out_shape=[jax.ShapeDtypeStruct(s, d) for s, d in outs],
        scratch_shapes=[pltpu.VMEM(*one) if isinstance(one, tuple) else one for one in scratch],
        compiler_params=pltpu.CompilerParams(vmem_limit_bytes=limit),
        cost_estimate=pl.CostEstimate(flops=int(micros * 1.1e9), bytes_accessed=0, transcendentals=0),
    )(*args, *(arg for arg, _ in stacked), *distant)


def local(block_input, cotangent, qkv_weight, proj_weight, expand_weight, reduce_weight, bias_table):
    frames, rows, cols, width = block_input.shape
    n_row, n_col = lax.axis_size("row"), lax.axis_size("col")
    inner = expand_weight.shape[2]
    heads = bias_table.shape[1]
    tokens = frames * rows * cols
    wide = jnp.swapaxes(reduce_weight, 1, 2)
    weights = (qkv_weight, proj_weight, expand_weight, wide)
    table = jnp.swapaxes(bias_table, 0, 1)
    axes = ("row", "col")

    def send(block, down, right):
        route = [
            (r * n_col + c, (r + down) % n_row * n_col + (c + right) % n_col)
            for r in range(n_row)
            for c in range(n_col)
        ]
        return lax.ppermute(block, axes, route)

    def swap(block, row_bits, col_bits):
        route = [
            (r * n_col + c, (r ^ row_bits) * n_col + (c ^ col_bits)) for r in range(n_row) for c in range(n_col)
        ]
        return lax.ppermute(block, axes, route)

    far = n_col // 2
    unit = 8 * far * 16
    used = (4 * width + 2 * inner) * width // 128 + 16
    size = -(-used // unit) * unit
    chunk = size // (8 * far)
    halves = [((size // 2, 128), BF)] * 2
    buffer = ((size, 128), BF)
    tile = (frames, rows, cols, width)
    strip = (frames, SHIFT, cols, width)
    patches = frames * SHIFT * SHIFT
    tight = ((4 * patches, width), F32)
    lines = ((heads * 64, 128), F32)
    first, top, left, corner = call(
        plain_forward,
        [(strip, F32), ((2, *strip), BF), ((2 * patches, width), BF), ((2 * patches, width), BF)],
        [tight, (tile, BF), *((w.shape[1:], BF) for w in weights), (tile, BF), (tile, F32), (table.shape, F32), pltpu.SemaphoreType.DMA((7,))],
        [],
        distant=(block_input, cotangent, table, *weights),
        micros=2.3,
        limit=FULL,
    )
    halo = [send(top, -1, 0), send(left, 0, -1), send(corner, -1, -1)]
    bias, *kept = call(
        functools.partial(keep_plain, n_row, n_col),
        [
            lines,
            ((inner, tokens), F32),
            ((width, tokens), F32),
            ((1, tokens), F32),
            ((width, tokens), BF),
            ((width, tokens), BF),
            ((tokens, width), BF),
            ((heads * 64, tokens), F32),
            ((width, tokens), BF),
            ((width, tokens), F32),
            ((1, tokens), F32),
            ((inner, tokens), BF),
        ],
        [],
        [block_input, table],
        [(w, 0) for w in weights[:3]],
        micros=2.3,
    )
    own, bottom, right, corner, keep, away = call(
        shifted_block,
        [(strip, F32), (strip, BF), ((patches, width), BF), ((patches, width), BF), *halves],
        [((frames, rows, cols + 8, width), F32)] * 2 + [tight, buffer],
        [first, cotangent, *halo, bias],
        [(w, 1) for w in weights],
        micros=4.8,
    )
    back = [own, send(bottom, 1, 0), send(right, 0, 1), send(corner, 1, 1)]

    eighth, quarter, piece = (size // 8, 128), (size // 4, 128), (2 * chunk, 128)

    def near(own, *sends):
        return [own] + [swap(one, d & 2, d & 1) for d, one in enumerate(sends, 1)]

    quarters = [(eighth, F32)] + [(eighth, BF)] * 3
    summed = [((size // 2, 128), F32)]
    shifted = call(add_core, quarters, summed, [keep, swap(away, 1, 0)])
    kept[0], *shifted = lax.optimization_barrier((kept[0], *shifted))
    shifted = near(*shifted)
    operands = [((n, tokens), BF) for n in (width, 3 * width, width, inner, width)]
    input_grad, *given = call(
        plain_backward,
        [(tile, F32), lines, *operands],
        [(tile, F32), tight],
        [*back, *kept],
        [(w, 0) for w in weights],
        micros=3.2,
    )
    given = [given[1], given[2], kept[7], given[3], kept[8], given[4], kept[10], given[5], given[0]]
    keep, away, other = call(plain_grads, [*halves, (eighth, F32)], [buffer], [*given, *shifted])
    plain = call(add_core, quarters, summed, [keep, swap(away, 1, 0)])
    own, *sends = call(
        functools.partial(add_near, far),
        [(piece, F32)] + [(piece, BF)] * (far - 1),
        [(eighth, F32)],
        [*near(*plain), other],
    )
    distant = [own] + [swap(one, 0, 2 * d) for d, one in enumerate(sends, 1)]
    (done,) = call(add_far, [(piece, BF)], [], distant)
    distant = [done] + [swap(done, 0, 2 * d) for d in range(1, far)]
    (joined,) = call(join_far, [(quarter, BF)], [], distant)
    near = [joined] + [swap(joined, d & 2, d & 1) for d in range(1, 4)]
    near = near + [swap(one, 1, 0) for one in near]
    factor = 1.0 / math.sqrt(frames * rows * n_row * cols * n_col)
    shapes = [(w.shape, F32) for w in (*weights, table)]
    qkv, proj, expand, reduce, table = call(
        functools.partial(finish, factor), shapes, [buffer, pltpu.SemaphoreType.DMA((9,)), *shapes], near, far_outs=True
    )
    return input_grad, qkv, proj, expand, jnp.swapaxes(reduce, 1, 2), jnp.swapaxes(table, 0, 1)


def solution(mesh):
    in_specs = (P(None, "row", "col", None), P(None, "row", "col", None), P(), P(), P(), P(), P())
    out_specs = (P(None, "row", "col", None), P(), P(), P(), P(), P())
    return jax.shard_map(local, mesh=mesh, in_specs=in_specs, out_specs=out_specs, check_vma=False)
```

```python
import functools
import math

import jax
import jax.numpy as jnp
from jax import lax
from jax.experimental import pallas as pl
from jax.experimental.pallas import tpu as pltpu
from jax.sharding import PartitionSpec as P

WIN = 8
SHIFT = 4
BF = jnp.bfloat16
F32 = jnp.float32
LIMIT = 48 * 1024 * 1024
FULL = 62 * 1024 * 1024
ROOT_HALF = 0.7071067811865476
DENSITY = 0.3989422804014327


def dot(a, b):
    return lax.dot_general(a, b, (((1,), (0,)), ((), ())), preferred_element_type=F32)


def dot_nt(a, b):
    return lax.dot_general(a, b, (((1,), (1,)), ((), ())), preferred_element_type=F32)


def dot_tn(a, b):
    return lax.dot_general(a, b, (((0,), (0,)), ((), ())), preferred_element_type=F32)


def iota(shape, axis):
    return lax.broadcasted_iota(jnp.int32, shape, axis)


def norm(field):
    center = field - jnp.mean(field, axis=0, keepdims=True)
    spread = jnp.mean(center * center, axis=0, keepdims=True)
    scale = lax.rsqrt(spread + 1e-05)
    return center * scale, scale


def norm_back(grad, normed, scale):
    along = jnp.mean(grad * normed, axis=0, keepdims=True)
    return scale * (grad - jnp.mean(grad, axis=0, keepdims=True) - normed * along)


class Late:
    def __init__(self, copy, here):
        self.copy, self.here = copy, here

    def __getitem__(self, index):
        if self.copy is not None:
            self.copy.wait()
            self.copy = None
        return self.here[index]


def first_half(shape):
    return iota(shape, 1) < 64


def pair_mask(rows, head):
    return (iota((rows, 128), 0) // head) % 2 == iota((rows, 128), 1) // 64


def spread_bias(read, entries, heads):
    side = 2 * WIN - 1
    lanes = iota((entries, 256), 1)
    rows = iota((entries, 256), 0)
    place = lanes % 128
    down = place // 8 - 8
    right = place % 8 - jnp.where(lanes >= 128, 8, 0)
    wanted = (down + WIN - 1) * side + right + WIN - 1
    fits = (down >= 1 - WIN) & (right >= 1 - WIN)
    pick = (fits & (wanted == rows)).astype(F32)
    vectors = lax.dot_general(
        read(), pick, (((1,), (0,)), ((), ())), precision=lax.Precision.HIGHEST, preferred_element_type=F32
    )
    ahead = jnp.broadcast_to(vectors[:, None, :128], (heads, 8, 128)).reshape(heads * 8, 128)
    behind = jnp.broadcast_to(vectors[:, None, 128:], (heads, 8, 128)).reshape(heads * 8, 128)
    shape = (heads * 8, 128)
    col_j = iota(shape, 0) % 8
    col_i = iota(shape, 1) % 8
    built = jnp.zeros(shape, F32)
    for c in range(8):
        line = jnp.where(col_i >= c, pltpu.roll(ahead, 64 + c, 1), pltpu.roll(behind, 56 + c, 1))
        built = jnp.where(col_j == c, line, built)
    rolled = [built] + [pltpu.roll(built, 8 * r, 1) for r in range(1, 8)]
    rolled = [jnp.where(first_half(shape), one, pltpu.roll(one, 64, 1)) for one in rolled]
    parts = []
    for h in range(heads):
        for r in range(8):
            parts.append(rolled[r][8 * h : 8 * h + 8])
    return jnp.concatenate(parts, axis=0)


def fold_bias(grad, heads):
    folded = jnp.where(first_half(grad.shape), grad + pltpu.roll(grad, 64, 1), 0.0)
    split = folded.reshape(heads, 8, 8, 128)
    total = jnp.zeros((heads * 8, 128), F32)
    for r in range(8):
        piece = split[:, r].reshape(heads * 8, 128)
        total = total + pltpu.roll(piece, 64 - 8 * r, 1)
    shape = (heads * 8, 128)
    col_j = iota(shape, 0) % 8
    col_i = iota(shape, 1) % 8
    ahead = jnp.zeros(shape, F32)
    behind = jnp.zeros(shape, F32)
    for c in range(8):
        mine = jnp.where((col_j == c) & (col_i >= c), total, 0.0)
        ahead = ahead + (pltpu.roll(mine, 128 - c, 1) if c else mine)
        rest = jnp.where((col_j == c) & (col_i < c), total, 0.0)
        behind = behind + pltpu.roll(rest, 8 - c, 1)
    ahead = jnp.sum(ahead.reshape(heads, 8, 128), axis=1)
    behind = jnp.sum(behind.reshape(heads, 8, 128), axis=1)
    return ahead, behind


def shift_mask(shape, last_row, last_col):
    j = iota(shape, 0) % 64
    lane = iota(shape, 1)
    i = lane % 64
    low = (j // 8 >= SHIFT) != (i // 8 >= SHIFT)
    side = (j % 8 >= SHIFT) != (i % 8 >= SHIFT)
    differ = (low & last_row) | (side & (lane >= 64) & last_col)
    return jnp.where(differ, -10000.0, 0.0)


def wide_of(field, mask):
    field = field.astype(F32)
    half = first_half(field.shape)
    swapped = pltpu.roll(field, 64, 1)
    return [
        jnp.where(mask, one, 0.0).astype(BF) for one in (jnp.where(half, field, swapped), jnp.where(half, swapped, field))
    ]


def by_pairs(product, lhs, rhs, heads, left, right):
    return jnp.concatenate(
        [
            product(lhs[left * n : left * n + left], rhs[right * n : right * n + right])
            for n in range(heads // 2)
        ],
        axis=0,
    )


def forward(weights, field, bias, heads):
    width, tokens = field.shape
    head = width // heads
    two = 2 * head
    mask = pair_mask(width, head)
    center, scale = norm(field)
    normed = center.astype(BF)
    mixed = dot_tn(weights[0][...], normed)
    query = (mixed[:width] * head ** (-0.5)).astype(BF)
    keys = mixed[width : 2 * width].astype(BF)
    values = mixed[2 * width :].astype(BF)
    probs, attended = [], []
    half = first_half((width, 128))
    tall_half = first_half((heads * 64, 128))
    for p in range(tokens // 128):
        lanes = slice(128 * p, 128 * p + 128)
        k = wide_of(mixed[width : 2 * width, lanes], mask)
        v = wide_of(mixed[2 * width :, lanes], mask)
        q = query[:, lanes]
        first, second = (by_pairs(dot_tn, one, q, heads, two, two) for one in k)
        scores = jnp.where(tall_half, first, second) + bias
        scores = scores.reshape(heads, 64, 128)
        expos = jnp.exp(scores - jnp.max(scores, axis=1, keepdims=True))
        prob = (expos / jnp.sum(expos, axis=1, keepdims=True)).reshape(heads * 64, 128)
        prob_b = prob.astype(BF)
        first, second = (by_pairs(dot, one, prob_b, heads, two, 128) for one in v)
        attended.append(jnp.where(half, first, second))
        probs.append(prob)
    attended = jnp.concatenate(attended, axis=1).astype(BF)
    prob = jnp.concatenate(probs, axis=1)
    resid = field + dot_tn(weights[1][...], attended)
    center_two, scale_two = norm(resid)
    normed_two = center_two.astype(BF)
    pre = dot_tn(weights[2][...], normed_two)
    bell = 0.5 * (1.0 + lax.erf(pre * ROOT_HALF))
    hidden = (pre * bell).astype(BF)
    saved = (center, scale, query, keys, values, prob, attended, center_two, scale_two, hidden)
    return resid, hidden, pre, bell, saved


def slope_of(pre, bell):
    return bell + pre * (DENSITY * jnp.exp(-0.5 * pre * pre))


def backward(weights, saved, slope, grad, heads):
    qkv_w, proj_w, expand_w, reduce_w = (w[...] for w in weights)
    center, scale, query, keys, values, prob, attended, center_two, scale_two, hidden = saved
    width, tokens = grad.shape
    head = width // heads
    two = 2 * head
    mask = pair_mask(width, head)
    grad_b = grad.astype(BF)
    grad_hidden = dot_tn(reduce_w, grad_b).astype(BF).astype(F32)
    grad_pre = (grad_hidden * slope).astype(BF)
    grad_two = dot(expand_w, grad_pre).astype(BF).astype(F32)
    grad_resid = grad + norm_back(grad_two, center_two, scale_two)
    grad_resid_b = grad_resid.astype(BF)
    grad_att = dot(proj_w, grad_resid_b)
    half = first_half((width, 128))
    tall_half = first_half((heads * 64, 128))
    grad_q, grad_k, grad_v = [], [], []
    grad_bias = jnp.zeros((heads * 64, 128), F32)
    for p in range(tokens // 128):
        lanes = slice(128 * p, 128 * p + 128)
        k = wide_of(keys[:, lanes], mask)
        v = wide_of(values[:, lanes], mask)
        p_f = prob[:, lanes]
        p_b = p_f.astype(BF)
        att = grad_att[:, lanes]
        att_b = att.astype(BF)
        zero = jnp.zeros_like(att)
        att_w = (jnp.where(half, att, zero).astype(BF), jnp.where(half, zero, att).astype(BF))
        query_f = query[:, lanes].astype(F32)
        query_w = (jnp.where(half, query_f, zero).astype(BF), jnp.where(half, zero, query_f).astype(BF))
        first, second = (by_pairs(dot_tn, one, att_b, heads, two, two) for one in v)
        grad_prob = jnp.where(tall_half, first, second)
        grad_prob = grad_prob.astype(BF).astype(F32)
        along = jnp.sum((p_f * grad_prob).reshape(heads, 64, 128), axis=1, keepdims=True)
        grad_score = p_f * (grad_prob.reshape(heads, 64, 128) - along).reshape(heads * 64, 128)
        grad_bias = grad_bias + grad_score
        score_b = grad_score.astype(BF)
        first, second = (by_pairs(dot, one, score_b, heads, two, 128) for one in k)
        grad_q.append(jnp.where(half, first, second))
        for store, lhs, rhs in ((grad_k, query_w, score_b), (grad_v, att_w, p_b)):
            both = []
            for w in range(2):
                folded = jnp.where(mask, by_pairs(dot_nt, lhs[w], rhs, heads, two, 128), 0.0)
                both.append(folded + pltpu.roll(folded, 64, 1))
            store.append(jnp.where(half, both[0], both[1]))
    grad_q = jnp.concatenate(grad_q, axis=1).astype(BF).astype(F32) * head ** (-0.5)
    grad_k = jnp.concatenate(grad_k, axis=1)
    grad_v = jnp.concatenate(grad_v, axis=1)
    grad_mixed = jnp.concatenate([grad_q, grad_k, grad_v], axis=0).astype(BF)
    grad_normed = dot(qkv_w, grad_mixed).astype(BF).astype(F32)
    grad_field = grad_resid + norm_back(grad_normed, center, scale)
    operands = (center.astype(BF), grad_mixed, attended, grad_resid_b, center_two.astype(BF), grad_pre, hidden, grad_b)
    return grad_field, operands, grad_bias


def pack_grads(operands, ahead, behind, buffer):
    normed, grad_mixed, attended, grad_resid, normed_two, grad_pre, hidden, grad = operands
    width = normed.shape[0]
    qkv = dot_nt(normed, grad_mixed)
    proj = dot_nt(attended, grad_resid)
    expand = dot_nt(normed_two, grad_pre)
    reduce = dot_nt(grad, hidden)
    inner = hidden.shape[0]
    at = 0

    def put(block):
        nonlocal at
        buffer[at : at + block.shape[0], :] = block.astype(BF)
        at += block.shape[0]

    full = 3 * width // 128
    for n in range(full):
        put(qkv[:, 128 * n : 128 * n + 128])
    put(jnp.concatenate([qkv[:, 128 * full :], proj[:, 128:]], axis=1))
    put(proj[:, :128])
    columns = inner // 128
    for n in range(columns // 2):
        put(expand[:, 128 * n : 128 * n + 128])
    half = buffer.shape[0] // 2
    if half > at:
        put(jnp.zeros((half - at, 128), F32))
    for n in range(columns // 2, columns):
        put(expand[:, 128 * n : 128 * n + 128])
    for n in range(columns):
        put(reduce[:, 128 * n : 128 * n + 128])
    heads = ahead.shape[0]
    put(jnp.concatenate([ahead, behind, jnp.zeros((16 - 2 * heads, 128), F32)], axis=0))
    if buffer.shape[0] > at:
        put(jnp.zeros((buffer.shape[0] - at, 128), F32))


class Taker:
    def __init__(self, buffer, factor):
        self.buffer, self.factor, self.at = buffer, factor, 0

    def __call__(self, rows):
        piece = self.buffer[self.at : self.at + rows, :]
        self.at += rows
        return piece.astype(F32) * self.factor


def unpack_first(buffer, qkv, proj, expand, sent, factor):
    take = Taker(buffer, factor)
    width = proj.shape[0]
    full = 3 * width // 128
    for n in range(full):
        qkv[:, 128 * n : 128 * n + 128] = take(width)
    shared = take(width)
    qkv[:, 128 * full :] = shared[:, :64]
    sent(0)
    proj[:, 128:] = shared[:, 64:]
    proj[:, :128] = take(width)
    sent(1)
    for n in range(expand.shape[1] // 128):
        expand[:, 128 * n : 128 * n + 128] = take(width)
    sent(2)


def unpack_second(buffer, expand, reduce, sent, table, block, factor):
    take = Taker(buffer, factor)
    width = reduce.shape[0]
    for which, one in enumerate((expand, reduce)):
        for n in range(one.shape[1] // 128):
            one[:, 128 * n : 128 * n + 128] = take(width)
        sent(which)
    vectors = buffer[take.at : take.at + 16, :]
    heads, _, entries = table.shape
    side = 2 * WIN - 1
    shape = (128, entries)
    rows, lanes = iota(shape, 0), iota(shape, 1)
    down, right = lanes // side - (WIN - 1), lanes % side - (WIN - 1)
    base = 8 * (down + 8) + right
    ahead = ((right >= 0) & (base == rows)).astype(F32).astype(BF)
    behind = ((right < 0) & (base + 8 == rows)).astype(F32).astype(BF)
    table[:, block, :] = (dot(vectors, ahead)[:heads] + dot(vectors, behind)[heads : 2 * heads]) * factor


def tokens_of(read):
    flat = [read(f, c).reshape(64, -1) for f in range(2) for c in range(2)]
    return jnp.concatenate(flat, axis=0).T


def tile_of(field, write):
    natural = field.T
    for f in range(2):
        for c in range(2):
            n = 64 * (2 * f + c)
            write(f, c, natural[n : n + 64].reshape(8, 8, -1))


def corners():
    return [(f, r, 16 * f + 4 * r) for f in range(2) for r in range(4)]


def plain_forward(x_far, cot_far, table_far, *refs):
    far, outs, (first, top, left, corner), (tight, *near), done = refs[:4], refs[4:8], refs[8:12], refs[12:21], refs[21]
    heads = table_far.shape[0]
    qkv_far, *rest = (there.at[0] for there in far)
    pairs = [(x_far, near[0]), (qkv_far, near[1]), *zip(rest, near[2:5], strict=True)]
    pairs[1:1] = [(table_far, near[7])]
    pairs.append((cot_far, near[5]))
    copies = [pltpu.make_async_copy(there, here, done.at[n]) for n, (there, here) in enumerate(pairs)]
    for copy in copies:
        copy.start()
    x_ref, table, qkv, proj, expand, reduce, cot = (
        Late(copy, here) for copy, (_, here) in zip(copies, pairs, strict=True)
    )
    whole = near[6]

    def write(f, c, piece):
        whole[f, :, 8 * c : 8 * c + 8, :] = piece

    bias = spread_bias(lambda: table[:, 0, :], table_far.shape[2], heads)
    field = tokens_of(lambda f, c: x_ref[f, :, 8 * c : 8 * c + 8, :].astype(F32))
    resid, hidden, _, _, _ = forward((qkv, proj, expand), field, bias, heads)
    tile_of(resid + dot(reduce[...], hidden), write)
    first[...] = whole[:, SHIFT:]
    top[0] = whole[:, :SHIFT].astype(BF)
    top[1] = cot[:, :SHIFT]
    for f, r, n in corners():
        tight[n : n + 4, :] = whole[f, r, :4, :]
        tight[32 + n : 36 + n, :] = cot[f, r, :8, :].astype(F32)[:4]
        tight[64 + n : 68 + n, :] = whole[f, 4 + r, :4, :]
        tight[96 + n : 100 + n, :] = cot[f, 4 + r, :8, :].astype(F32)[:4]
    corner[...] = tight[:64].astype(BF)
    left[...] = tight[64:].astype(BF)
    copies = [pltpu.make_async_copy(here, there, done.at[n]) for n, (here, there) in enumerate(zip((first, top, left, corner), outs, strict=True))]
    for copy in copies:
        copy.start()
    for copy in copies:
        copy.wait()


def keep_plain(n_row, n_col, x_ref, table, qkv, proj, expand, bias_out, slope_out, *outs):
    heads = table.shape[0]
    field = tokens_of(lambda f, c: x_ref[f, :, 8 * c : 8 * c + 8, :].astype(F32))
    _, _, pre, bell, saved = forward((qkv, proj, expand), field, spread_bias(lambda: table[:, 0, :], table.shape[2], heads), heads)
    slope_out[...] = slope_of(pre, bell)
    for ref, value in zip(outs, saved, strict=True):
        ref[...] = value
    last_row = lax.axis_index("row") == n_row - 1
    last_col = lax.axis_index("col") == n_col - 1
    bias_out[...] = spread_bias(lambda: table[:, 1, :], table.shape[2], heads) + shift_mask(bias_out.shape, last_row, last_col)


def shifted_block(
    first, cot, below, beside, across, bias, qkv, proj, expand, reduce,
    own, bottom, right, corner, keep, send, moved, turned, tight, buffer,
):
    heads = bias.shape[0] // 64
    moved[:, :4, :16, :] = first[...]
    moved[:, 4:, :16, :] = below[0].astype(F32)
    turned[:, :4, :16, :] = cot[:, 4:, :, :].astype(F32)
    turned[:, 4:, :16, :] = below[1].astype(F32)
    tight[:64] = across[...].astype(F32)
    tight[64:] = beside[...].astype(F32)
    for f, r, n in corners():
        moved[f, 4 + r, 16:20, :] = tight[n : n + 4, :]
        turned[f, 4 + r, 16:20, :] = tight[32 + n : 36 + n, :]
        moved[f, r, 16:20, :] = tight[64 + n : 68 + n, :]
        turned[f, r, 16:20, :] = tight[96 + n : 100 + n, :]
    field = tokens_of(lambda f, c: moved[f, :, 4 + 8 * c : 12 + 8 * c, :])
    cotangent = tokens_of(lambda f, c: turned[f, :, 4 + 8 * c : 12 + 8 * c, :])
    weights = (qkv, proj, expand, reduce)
    _, _, pre, bell, saved = forward(weights, field, bias[...], heads)
    grad_field, operands, grad_bias = backward(weights, saved, slope_of(pre, bell), cotangent, heads)

    def write(f, c, piece):
        moved[f, :, 4 + 8 * c : 12 + 8 * c, :] = piece

    tile_of(grad_field, write)
    own[...] = moved[:, :4, :16, :]
    bottom[...] = moved[:, 4:, :16, :].astype(BF)
    for f, r, n in corners():
        tight[n : n + 4, :] = moved[f, 4 + r, 16:20, :]
        tight[32 + n : 36 + n, :] = moved[f, r, 16:20, :]
    corner[...] = tight[:32].astype(BF)
    right[...] = tight[32:64].astype(BF)
    ahead, behind = fold_bias(grad_bias, heads)
    pack_grads(operands, ahead, behind, buffer)
    split_core(buffer, keep, send)


def split_core(buffer, keep, send):
    rows = keep.shape[0]
    core = lax.axis_index("row") % 2
    keep[...] = buffer[pl.ds(pl.multiple_of(core * rows, 16), rows), :]
    send[...] = buffer[pl.ds(pl.multiple_of((1 - core) * rows, 16), rows), :]


def plain_backward(own, above, beside, across, slope, *refs):
    saved, weights = refs[:10], refs[10:14]
    out, lines, outs, middle, tight = refs[14], refs[15], refs[16:21], refs[21], refs[22]
    heads = saved[5].shape[0] // 64
    middle[:, 4:] = own[...]
    middle[:, :4] = above[...].astype(F32)
    tight[:32] = across[...].astype(F32)
    tight[32:64] = beside[...].astype(F32)
    for f, r, n in corners():
        middle[f, r, :4, :] = tight[n : n + 4, :]
        middle[f, 4 + r, :4, :] = tight[32 + n : 36 + n, :]
    cotangent = tokens_of(lambda f, c: middle[f, :, 8 * c : 8 * c + 8, :])
    saved = tuple(ref[...] for ref in saved)
    grad_field, operands, grad_bias = backward(weights, saved, slope[...], cotangent, heads)

    def write(f, c, piece):
        out[f, :, 8 * c : 8 * c + 8, :] = piece

    tile_of(grad_field, write)
    lines[...] = grad_bias
    for ref, n in zip(outs, (0, 1, 3, 5, 7), strict=True):
        ref[...] = operands[n]


def plain_grads(normed, mixed, attended, resid, two, pre, hidden, grad, lines, mine, one, *refs):
    two_came, three_came, keep, send, done, buffer = refs
    kept = (normed, mixed, attended, resid, two, pre, hidden, grad)
    ahead, behind = fold_bias(lines[...], lines.shape[0] // 64)
    pack_grads(tuple(ref[...].astype(BF) for ref in kept), ahead, behind, buffer)
    split_core(buffer, keep, send)
    done[...] = mine[...] + one[...].astype(F32) + two_came[...].astype(F32) + three_came[...].astype(F32)


def near_place():
    return lax.axis_index("row") // 2 * 2 + lax.axis_index("col") % 2


def cut(total, me, own, sends, partners, here=slice(None)):
    rows = total.shape[0] // (len(sends) + 1)
    own[here, :] = total[pl.ds(pl.multiple_of(me * rows, 16), rows), :]
    for d, send in zip(partners, sends, strict=True):
        send[here, :] = total[pl.ds(pl.multiple_of((me ^ d) * rows, 16), rows), :].astype(BF)


def add_core(keep, came, own, *rest):
    sends, total = rest[:-1], rest[-1]
    total[...] = keep[...].astype(F32) + came[...].astype(F32)
    cut(total, near_place(), own, sends, (1, 2, 3))


def add_near(count, mine, one, two, three, other, own, *rest):
    sends, total = rest[: count - 1], rest[-1]
    rows = own.shape[0] // 2
    place = lax.axis_index("col") // 2
    total[...] = mine[...] + one[...].astype(F32) + two[...].astype(F32) + three[...].astype(F32)
    partners = range(count - 1, 0, -1)
    cut(total, place, own, sends, partners, slice(0, rows))
    cut(other, place, own, sends, partners, slice(rows, 2 * rows))


def add_far(*refs):
    ins, out = refs[:-1], refs[-1]
    out[...] = (ins[0][...] + sum(one[...].astype(F32) for one in ins[1:])).astype(BF)


def join_far(*refs):
    ins, out = refs[:-1], refs[-1]
    rows, length = ins[0].shape[0] // 2, out.shape[0] // 2
    me = lax.axis_index("col") // 2
    for d, piece in enumerate(ins):
        for block in range(2):
            there = pl.multiple_of(block * length + (me ^ d) * rows, 16)
            out[pl.ds(there, rows), :] = piece[block * rows : block * rows + rows, :]


def finish(other, factor, *refs):
    ins, refs = refs[:4], refs[4 + 5 * other :]
    outs, buffer, done, (qkv, proj, expand, reduce, table) = refs[:5], refs[5], refs[6], refs[7:12]
    rows = ins[0].shape[0] // 2
    me = near_place()
    for block in range(2):
        for d, piece in enumerate(ins):
            there = pl.multiple_of((me ^ d) * rows, 16)
            buffer[block, pl.ds(there, rows), :] = piece[block * rows : block * rows + rows, :]
    half = (lax.axis_index("row") + other) % 2
    columns = expand.shape[2]
    copies = []

    def copy(here, there):
        copies.append(pltpu.make_async_copy(here, there, done.at[len(copies)]))
        copies[-1].start()

    @pl.when(half == 0)
    def _():
        copies.clear()
        for block in range(2):
            pairs = [
                (qkv.at[block], outs[0].at[block]),
                (proj.at[block], outs[1].at[block]),
                (expand.at[block], outs[2].at[block, :, pl.ds(0, columns)]),
            ]
            sent = lambda n, pairs=pairs: copy(*pairs[n])
            unpack_first(buffer.at[block], qkv.at[block], proj.at[block], expand.at[block], sent, factor)
        for one in copies:
            one.wait()

    @pl.when(half == 1)
    def _():
        copies.clear()
        for block in range(2):
            pairs = [
                (expand.at[block], outs[2].at[block, :, pl.ds(columns, columns)]),
                (reduce.at[block], outs[3].at[block]),
            ]
            sent = lambda n, pairs=pairs: copy(*pairs[n])
            unpack_second(buffer.at[block], expand.at[block], reduce.at[block], sent, table, block, factor)
        copy(table, outs[4])
        for one in copies:
            one.wait()


class Whole:
    def __init__(self, ref, block):
        self.ref, self.block = ref, block

    def __getitem__(self, index):
        return self.ref[self.block]


def call(kernel, outs, scratch, args, stacked=(), distant=(), micros=0.5, limit=LIMIT, far_outs=0, aliases=None):
    here, there = pl.BlockSpec(memory_space=pltpu.VMEM), pl.BlockSpec(memory_space=pltpu.HBM)
    count = len(args)

    def body(*refs):
        weights = [Whole(ref, block) for ref, (_, block) in zip(refs[count:], stacked)]
        kernel(*refs[:count], *weights, *refs[count + len(stacked) :])

    return pl.pallas_call(
        body,
        in_specs=[here] * (count + len(stacked)) + [there] * len(distant),
        out_specs=[there] * far_outs + [here] * (len(outs) - far_outs),
        out_shape=[jax.ShapeDtypeStruct(s, d) for s, d in outs],
        scratch_shapes=[pltpu.VMEM(*one) if isinstance(one, tuple) else one for one in scratch],
        input_output_aliases=aliases or {},
        compiler_params=pltpu.CompilerParams(vmem_limit_bytes=limit),
        cost_estimate=pl.CostEstimate(flops=int(micros * 1.1e9), bytes_accessed=0, transcendentals=0),
    )(*args, *(arg for arg, _ in stacked), *distant)


def local(block_input, cotangent, qkv_weight, proj_weight, expand_weight, reduce_weight, bias_table):
    frames, rows, cols, width = block_input.shape
    n_row, n_col = lax.axis_size("row"), lax.axis_size("col")
    inner = expand_weight.shape[2]
    heads = bias_table.shape[1]
    tokens = frames * rows * cols
    wide = jnp.swapaxes(reduce_weight, 1, 2)
    weights = (qkv_weight, proj_weight, expand_weight, wide)
    table = jnp.swapaxes(bias_table, 0, 1)
    axes = ("row", "col")

    def send(block, down, right):
        route = [
            (r * n_col + c, (r + down) % n_row * n_col + (c + right) % n_col)
            for r in range(n_row)
            for c in range(n_col)
        ]
        return lax.ppermute(block, axes, route)

    def swap(block, row_bits, col_bits):
        route = [
            (r * n_col + c, (r ^ row_bits) * n_col + (c ^ col_bits)) for r in range(n_row) for c in range(n_col)
        ]
        return lax.ppermute(block, axes, route)

    far = n_col // 2
    unit = 8 * far * 16
    used = (4 * width + 2 * inner) * width // 128 + 2 * 16
    size = -(-used // unit) * unit
    chunk = size // (8 * far)
    halves = [((size // 2, 128), BF)] * 2
    buffer = ((size, 128), BF)
    tile = (frames, rows, cols, width)
    strip = (frames, SHIFT, cols, width)
    patches = frames * SHIFT * SHIFT
    tight = ((4 * patches, width), F32)
    lines = ((heads * 64, 128), F32)
    sent = [(strip, F32), ((2, *strip), BF), ((2 * patches, width), BF), ((2 * patches, width), BF)]
    first, top, left, corner = call(
        plain_forward,
        sent,
        [*sent, tight, (tile, BF), *((w.shape[1:], BF) for w in weights), (tile, BF), (tile, F32), (table.shape, F32), pltpu.SemaphoreType.DMA((7,))],
        [],
        distant=(block_input, cotangent, table, *weights),
        micros=2.3,
        limit=FULL,
        far_outs=4,
    )
    halo = [send(top, -1, 0), send(left, 0, -1), send(corner, -1, -1)]
    bias, *kept = call(
        functools.partial(keep_plain, n_row, n_col),
        [
            lines,
            ((inner, tokens), F32),
            ((width, tokens), F32),
            ((1, tokens), F32),
            ((width, tokens), BF),
            ((width, tokens), BF),
            ((width, tokens), BF),
            ((heads * 64, tokens), F32),
            ((width, tokens), BF),
            ((width, tokens), F32),
            ((1, tokens), F32),
            ((inner, tokens), BF),
        ],
        [],
        [block_input, table],
        [(w, 0) for w in weights[:3]],
        micros=2.3,
    )
    own, bottom, right, corner, keep, away = call(
        shifted_block,
        [(strip, F32), (strip, BF), ((patches, width), BF), ((patches, width), BF), *halves],
        [((frames, rows, cols + 8, width), F32)] * 2 + [tight, buffer],
        [first, cotangent, *halo, bias],
        [(w, 1) for w in weights],
        micros=4.8,
    )
    back = [own, send(bottom, 1, 0), send(right, 0, 1), send(corner, 1, 1)]

    eighth, quarter, piece = (size // 8, 128), (size // 4, 128), (2 * chunk, 128)

    def near(own, *sends):
        came = [swap(one, d & 2, d & 1) for d, one in reversed(list(enumerate(sends, 1)))]
        return [own] + came[::-1]

    quarters = [(eighth, F32)] + [(eighth, BF)] * 3
    summed = [((size // 2, 128), F32)]
    shifted = call(add_core, quarters, summed, [keep, swap(away, 1, 0)])
    kept[0], *shifted = lax.optimization_barrier((kept[0], *shifted))
    shifted = near(*shifted)
    operands = [((n, tokens), BF) for n in (width, 3 * width, width, inner, width)]
    input_grad, *given = call(
        plain_backward,
        [(tile, F32), lines, *operands],
        [(tile, F32), tight],
        [*back, *kept],
        [(w, 0) for w in weights],
        micros=3.2,
    )
    given = [given[1], given[2], kept[7], given[3], kept[8], given[4], kept[10], given[5], given[0]]
    keep, away, other = call(plain_grads, [*halves, (eighth, F32)], [buffer], [*given, *shifted])
    plain = call(add_core, quarters, summed, [keep, swap(away, 1, 0)])
    own, *sends = call(
        functools.partial(add_near, far),
        [(piece, F32)] + [(piece, BF)] * (far - 1),
        [(eighth, F32)],
        [*near(*plain), other],
    )
    distant = [own] + [swap(one, 0, 2 * d) for d, one in zip(range(far - 1, 0, -1), sends, strict=True)]
    (done,) = call(add_far, [(piece, BF)], [], distant)
    distant = [done] + [swap(done, 0, 2 * d) for d in range(1, far)]
    (joined,) = call(join_far, [(quarter, BF)], [], distant)
    near = [joined] + [swap(joined, d & 2, d & 1) for d in range(1, 4)]
    factor = 1.0 / math.sqrt(frames * rows * n_row * cols * n_col)
    shapes = [(w.shape, F32) for w in (*weights, table)]
    stage = [((2, size // 2, 128), BF), pltpu.SemaphoreType.DMA((6,)), *shapes]
    stage[4] = ((2, width, inner // 2), F32)
    grads = call(functools.partial(finish, 0, factor), shapes, stage, near, far_outs=5, micros=1.2)
    qkv, proj, expand, reduce, table = call(
        functools.partial(finish, 1, factor),
        shapes,
        stage,
        [swap(one, 1, 0) for one in near],
        distant=grads,
        far_outs=5,
        aliases={4 + n: n for n in range(5)},
        micros=1.2,
    )
    return input_grad, qkv, proj, expand, jnp.swapaxes(reduce, 1, 2), jnp.swapaxes(table, 0, 1)


def solution(mesh):
    in_specs = (P(None, "row", "col", None), P(None, "row", "col", None), P(), P(), P(), P(), P())
    out_specs = (P(None, "row", "col", None), P(), P(), P(), P(), P())
    return jax.shard_map(local, mesh=mesh, in_specs=in_specs, out_specs=out_specs, check_vma=False)
```

```python
import functools
import math

import jax
import jax.numpy as jnp
from jax import lax
from jax.experimental import pallas as pl
from jax.experimental.pallas import tpu as pltpu
from jax.sharding import PartitionSpec as P

WIN = 8
SHIFT = 4
BF = jnp.bfloat16
F32 = jnp.float32
LIMIT = 48 * 1024 * 1024
FULL = 62 * 1024 * 1024
ROOT_HALF = 0.7071067811865476
DENSITY = 0.3989422804014327


def dot(a, b):
    return lax.dot_general(a, b, (((1,), (0,)), ((), ())), preferred_element_type=F32)


def dot_nt(a, b):
    return lax.dot_general(a, b, (((1,), (1,)), ((), ())), preferred_element_type=F32)


def dot_tn(a, b):
    return lax.dot_general(a, b, (((0,), (0,)), ((), ())), preferred_element_type=F32)


def iota(shape, axis):
    return lax.broadcasted_iota(jnp.int32, shape, axis)


def norm(field):
    center = field - jnp.mean(field, axis=0, keepdims=True)
    spread = jnp.mean(center * center, axis=0, keepdims=True)
    scale = lax.rsqrt(spread + 1e-05)
    return center * scale, scale


def norm_back(grad, normed, scale):
    along = jnp.mean(grad * normed, axis=0, keepdims=True)
    return scale * (grad - jnp.mean(grad, axis=0, keepdims=True) - normed * along)


class Late:
    def __init__(self, copy, here):
        self.copy, self.here = copy, here

    def __getitem__(self, index):
        if self.copy is not None:
            self.copy.wait()
            self.copy = None
        return self.here[index]


def first_half(shape):
    return iota(shape, 1) < 64


def pair_mask(rows, head):
    return (iota((rows, 128), 0) // head) % 2 == iota((rows, 128), 1) // 64


def spread_bias(read, entries, heads):
    side = 2 * WIN - 1
    lanes = iota((entries, 256), 1)
    rows = iota((entries, 256), 0)
    place = lanes % 128
    down = place // 8 - 8
    right = place % 8 - jnp.where(lanes >= 128, 8, 0)
    wanted = (down + WIN - 1) * side + right + WIN - 1
    fits = (down >= 1 - WIN) & (right >= 1 - WIN)
    pick = (fits & (wanted == rows)).astype(F32)
    vectors = lax.dot_general(
        read(), pick, (((1,), (0,)), ((), ())), precision=lax.Precision.HIGHEST, preferred_element_type=F32
    )
    ahead = jnp.broadcast_to(vectors[:, None, :128], (heads, 8, 128)).reshape(heads * 8, 128)
    behind = jnp.broadcast_to(vectors[:, None, 128:], (heads, 8, 128)).reshape(heads * 8, 128)
    shape = (heads * 8, 128)
    col_j = iota(shape, 0) % 8
    col_i = iota(shape, 1) % 8
    built = jnp.zeros(shape, F32)
    for c in range(8):
        line = jnp.where(col_i >= c, pltpu.roll(ahead, 64 + c, 1), pltpu.roll(behind, 56 + c, 1))
        built = jnp.where(col_j == c, line, built)
    rolled = [built] + [pltpu.roll(built, 8 * r, 1) for r in range(1, 8)]
    rolled = [jnp.where(first_half(shape), one, pltpu.roll(one, 64, 1)) for one in rolled]
    parts = []
    for h in range(heads):
        for r in range(8):
            parts.append(rolled[r][8 * h : 8 * h + 8])
    return jnp.concatenate(parts, axis=0)


def fold_bias(grad, heads):
    folded = jnp.where(first_half(grad.shape), grad + pltpu.roll(grad, 64, 1), 0.0)
    split = folded.reshape(heads, 8, 8, 128)
    total = jnp.zeros((heads * 8, 128), F32)
    for r in range(8):
        piece = split[:, r].reshape(heads * 8, 128)
        total = total + pltpu.roll(piece, 64 - 8 * r, 1)
    shape = (heads * 8, 128)
    col_j = iota(shape, 0) % 8
    col_i = iota(shape, 1) % 8
    ahead = jnp.zeros(shape, F32)
    behind = jnp.zeros(shape, F32)
    for c in range(8):
        mine = jnp.where((col_j == c) & (col_i >= c), total, 0.0)
        ahead = ahead + (pltpu.roll(mine, 128 - c, 1) if c else mine)
        rest = jnp.where((col_j == c) & (col_i < c), total, 0.0)
        behind = behind + pltpu.roll(rest, 8 - c, 1)
    ahead = jnp.sum(ahead.reshape(heads, 8, 128), axis=1)
    behind = jnp.sum(behind.reshape(heads, 8, 128), axis=1)
    return ahead, behind


def shift_mask(shape, last_row, last_col):
    j = iota(shape, 0) % 64
    lane = iota(shape, 1)
    i = lane % 64
    low = (j // 8 >= SHIFT) != (i // 8 >= SHIFT)
    side = (j % 8 >= SHIFT) != (i % 8 >= SHIFT)
    differ = (low & last_row) | (side & (lane >= 64) & last_col)
    return jnp.where(differ, -10000.0, 0.0)


def wide_of(field, mask):
    field = field.astype(F32)
    half = first_half(field.shape)
    swapped = pltpu.roll(field, 64, 1)
    return [
        jnp.where(mask, one, 0.0).astype(BF) for one in (jnp.where(half, field, swapped), jnp.where(half, swapped, field))
    ]


def by_pairs(product, lhs, rhs, heads, left, right):
    return jnp.concatenate(
        [
            product(lhs[left * n : left * n + left], rhs[right * n : right * n + right])
            for n in range(heads // 2)
        ],
        axis=0,
    )


def forward(weights, field, bias, heads):
    width, tokens = field.shape
    head = width // heads
    two = 2 * head
    mask = pair_mask(width, head)
    center, scale = norm(field)
    normed = center.astype(BF)
    mixed = dot_tn(weights[0][...], normed)
    query = (mixed[:width] * head ** (-0.5)).astype(BF)
    keys = mixed[width : 2 * width].astype(BF)
    values = mixed[2 * width :].astype(BF)
    probs, attended = [], []
    half = first_half((width, 128))
    tall_half = first_half((heads * 64, 128))
    for p in range(tokens // 128):
        lanes = slice(128 * p, 128 * p + 128)
        k = wide_of(mixed[width : 2 * width, lanes], mask)
        v = wide_of(mixed[2 * width :, lanes], mask)
        q = query[:, lanes]
        first, second = (by_pairs(dot_tn, one, q, heads, two, two) for one in k)
        scores = jnp.where(tall_half, first, second) + bias
        scores = scores.reshape(heads, 64, 128)
        expos = jnp.exp(scores - jnp.max(scores, axis=1, keepdims=True))
        prob = (expos / jnp.sum(expos, axis=1, keepdims=True)).reshape(heads * 64, 128)
        prob_b = prob.astype(BF)
        first, second = (by_pairs(dot, one, prob_b, heads, two, 128) for one in v)
        attended.append(jnp.where(half, first, second))
        probs.append(prob)
    attended = jnp.concatenate(attended, axis=1).astype(BF)
    prob = jnp.concatenate(probs, axis=1)
    resid = field + dot_tn(weights[1][...], attended)
    center_two, scale_two = norm(resid)
    normed_two = center_two.astype(BF)
    pre = dot_tn(weights[2][...], normed_two)
    bell = 0.5 * (1.0 + lax.erf(pre * ROOT_HALF))
    hidden = (pre * bell).astype(BF)
    saved = (center, scale, query, keys, values, prob, attended, center_two, scale_two, hidden)
    return resid, hidden, pre, bell, saved


def slope_of(pre, bell):
    return bell + pre * (DENSITY * jnp.exp(-0.5 * pre * pre))


def backward(weights, saved, slope, grad, heads):
    qkv_w, proj_w, expand_w, reduce_w = (w[...] for w in weights)
    center, scale, query, keys, values, prob, attended, center_two, scale_two, hidden = saved
    width, tokens = grad.shape
    head = width // heads
    two = 2 * head
    mask = pair_mask(width, head)
    grad_b = grad.astype(BF)
    grad_hidden = dot_tn(reduce_w, grad_b).astype(BF).astype(F32)
    grad_pre = (grad_hidden * slope).astype(BF)
    grad_two = dot(expand_w, grad_pre).astype(BF).astype(F32)
    grad_resid = grad + norm_back(grad_two, center_two, scale_two)
    grad_resid_b = grad_resid.astype(BF)
    grad_att = dot(proj_w, grad_resid_b)
    half = first_half((width, 128))
    tall_half = first_half((heads * 64, 128))
    grad_q, grad_k, grad_v = [], [], []
    grad_bias = jnp.zeros((heads * 64, 128), F32)
    for p in range(tokens // 128):
        lanes = slice(128 * p, 128 * p + 128)
        k = wide_of(keys[:, lanes], mask)
        v = wide_of(values[:, lanes], mask)
        p_f = prob[:, lanes]
        p_b = p_f.astype(BF)
        att = grad_att[:, lanes]
        att_b = att.astype(BF)
        zero = jnp.zeros_like(att)
        att_w = (jnp.where(half, att, zero).astype(BF), jnp.where(half, zero, att).astype(BF))
        query_f = query[:, lanes].astype(F32)
        query_w = (jnp.where(half, query_f, zero).astype(BF), jnp.where(half, zero, query_f).astype(BF))
        first, second = (by_pairs(dot_tn, one, att_b, heads, two, two) for one in v)
        grad_prob = jnp.where(tall_half, first, second)
        grad_prob = grad_prob.astype(BF).astype(F32)
        along = jnp.sum((p_f * grad_prob).reshape(heads, 64, 128), axis=1, keepdims=True)
        grad_score = p_f * (grad_prob.reshape(heads, 64, 128) - along).reshape(heads * 64, 128)
        grad_bias = grad_bias + grad_score
        score_b = grad_score.astype(BF)
        first, second = (by_pairs(dot, one, score_b, heads, two, 128) for one in k)
        grad_q.append(jnp.where(half, first, second))
        for store, lhs, rhs in ((grad_k, query_w, score_b), (grad_v, att_w, p_b)):
            both = []
            for w in range(2):
                folded = jnp.where(mask, by_pairs(dot_nt, lhs[w], rhs, heads, two, 128), 0.0)
                both.append(folded + pltpu.roll(folded, 64, 1))
            store.append(jnp.where(half, both[0], both[1]))
    grad_q = jnp.concatenate(grad_q, axis=1).astype(BF).astype(F32) * head ** (-0.5)
    grad_k = jnp.concatenate(grad_k, axis=1)
    grad_v = jnp.concatenate(grad_v, axis=1)
    grad_mixed = jnp.concatenate([grad_q, grad_k, grad_v], axis=0).astype(BF)
    grad_normed = dot(qkv_w, grad_mixed).astype(BF).astype(F32)
    grad_field = grad_resid + norm_back(grad_normed, center, scale)
    operands = (center.astype(BF), grad_mixed, attended, grad_resid_b, center_two.astype(BF), grad_pre, hidden, grad_b)
    return grad_field, operands, grad_bias


def pack_grads(operands, ahead, behind, buffer):
    normed, grad_mixed, attended, grad_resid, normed_two, grad_pre, hidden, grad = operands
    width = normed.shape[0]
    qkv = dot_nt(normed, grad_mixed)
    proj = dot_nt(attended, grad_resid)
    expand = dot_nt(normed_two, grad_pre)
    reduce = dot_nt(grad, hidden)
    inner = hidden.shape[0]
    at = 0

    def put(block):
        nonlocal at
        buffer[at : at + block.shape[0], :] = block.astype(BF)
        at += block.shape[0]

    full = 3 * width // 128
    for n in range(full):
        put(qkv[:, 128 * n : 128 * n + 128])
    put(jnp.concatenate([qkv[:, 128 * full :], proj[:, 128:]], axis=1))
    put(proj[:, :128])
    columns = inner // 128
    for n in range(columns // 2):
        put(expand[:, 128 * n : 128 * n + 128])
    half = buffer.shape[0] // 2
    if half > at:
        put(jnp.zeros((half - at, 128), F32))
    for n in range(columns // 2, columns):
        put(expand[:, 128 * n : 128 * n + 128])
    for n in range(columns):
        put(reduce[:, 128 * n : 128 * n + 128])
    heads = ahead.shape[0]
    put(jnp.concatenate([ahead, behind, jnp.zeros((16 - 2 * heads, 128), F32)], axis=0))
    if buffer.shape[0] > at:
        put(jnp.zeros((buffer.shape[0] - at, 128), F32))


class Taker:
    def __init__(self, buffer, factor):
        self.buffer, self.factor, self.at = buffer, factor, 0

    def __call__(self, rows):
        piece = self.buffer[self.at : self.at + rows, :]
        self.at += rows
        return piece.astype(F32) * self.factor


def unpack_first(buffer, qkv, proj, expand, sent, factor):
    take = Taker(buffer, factor)
    width = proj.shape[0]
    full = 3 * width // 128
    for n in range(full):
        qkv[:, 128 * n : 128 * n + 128] = take(width)
    shared = take(width)
    qkv[:, 128 * full :] = shared[:, :64]
    sent(0)
    proj[:, 128:] = shared[:, 64:]
    proj[:, :128] = take(width)
    sent(1)
    for n in range(expand.shape[1] // 128):
        expand[:, 128 * n : 128 * n + 128] = take(width)
    sent(2)


def unpack_second(buffer, expand, reduce, sent, table, block, factor):
    take = Taker(buffer, factor)
    width = reduce.shape[0]
    for which, one in enumerate((expand, reduce)):
        for n in range(one.shape[1] // 128):
            one[:, 128 * n : 128 * n + 128] = take(width)
        sent(which)
    vectors = buffer[take.at : take.at + 16, :]
    heads, _, entries = table.shape
    side = 2 * WIN - 1
    shape = (128, entries)
    rows, lanes = iota(shape, 0), iota(shape, 1)
    down, right = lanes // side - (WIN - 1), lanes % side - (WIN - 1)
    base = 8 * (down + 8) + right
    ahead = ((right >= 0) & (base == rows)).astype(F32).astype(BF)
    behind = ((right < 0) & (base + 8 == rows)).astype(F32).astype(BF)
    table[:, block, :] = (dot(vectors, ahead)[:heads] + dot(vectors, behind)[heads : 2 * heads]) * factor


def tokens_of(read):
    flat = [read(f, c).reshape(64, -1) for f in range(2) for c in range(2)]
    return jnp.concatenate(flat, axis=0).T


def tile_of(field, write):
    natural = field.T
    for f in range(2):
        for c in range(2):
            n = 64 * (2 * f + c)
            write(f, c, natural[n : n + 64].reshape(8, 8, -1))


def corners():
    return [(f, r, 16 * f + 4 * r) for f in range(2) for r in range(4)]


def plain_forward(x_far, cot_far, table_far, *refs):
    far, outs, (first, top, left, corner), (tight, *near), done = refs[:4], refs[4:8], refs[8:12], refs[12:21], refs[21]
    heads = table_far.shape[0]
    qkv_far, *rest = (there.at[0] for there in far)
    pairs = [(x_far, near[0]), (qkv_far, near[1]), *zip(rest, near[2:5], strict=True)]
    pairs[1:1] = [(table_far, near[7])]
    pairs.append((cot_far, near[5]))
    copies = [pltpu.make_async_copy(there, here, done.at[n]) for n, (there, here) in enumerate(pairs)]
    for copy in copies:
        copy.start()
    x_ref, table, qkv, proj, expand, reduce, cot = (
        Late(copy, here) for copy, (_, here) in zip(copies, pairs, strict=True)
    )
    whole = near[6]

    def write(f, c, piece):
        whole[f, :, 8 * c : 8 * c + 8, :] = piece

    bias = spread_bias(lambda: table[:, 0, :], table_far.shape[2], heads)
    field = tokens_of(lambda f, c: x_ref[f, :, 8 * c : 8 * c + 8, :].astype(F32))
    resid, hidden, _, _, _ = forward((qkv, proj, expand), field, bias, heads)
    tile_of(resid + dot(reduce[...], hidden), write)
    first[...] = whole[:, SHIFT:]
    top[0] = whole[:, :SHIFT].astype(BF)
    top[1] = cot[:, :SHIFT]
    for f, r, n in corners():
        tight[n : n + 4, :] = whole[f, r, :4, :]
        tight[32 + n : 36 + n, :] = cot[f, r, :8, :].astype(F32)[:4]
        tight[64 + n : 68 + n, :] = whole[f, 4 + r, :4, :]
        tight[96 + n : 100 + n, :] = cot[f, 4 + r, :8, :].astype(F32)[:4]
    corner[...] = tight[:64].astype(BF)
    left[...] = tight[64:].astype(BF)
    copies = [pltpu.make_async_copy(here, there, done.at[n]) for n, (here, there) in enumerate(zip((first, top, left, corner), outs, strict=True))]
    for copy in copies:
        copy.start()
    for copy in copies:
        copy.wait()


def keep_plain(n_row, n_col, x_ref, table, qkv, proj, expand, bias_out, slope_out, *outs):
    heads = table.shape[0]
    field = tokens_of(lambda f, c: x_ref[f, :, 8 * c : 8 * c + 8, :].astype(F32))
    _, _, pre, bell, saved = forward((qkv, proj, expand), field, spread_bias(lambda: table[:, 0, :], table.shape[2], heads), heads)
    slope_out[...] = slope_of(pre, bell)
    for ref, value in zip(outs, saved, strict=True):
        ref[...] = value
    last_row = lax.axis_index("row") == n_row - 1
    last_col = lax.axis_index("col") == n_col - 1
    bias_out[...] = spread_bias(lambda: table[:, 1, :], table.shape[2], heads) + shift_mask(bias_out.shape, last_row, last_col)


def shifted_block(
    first, cot, below, beside, across, bias, qkv, proj, expand, reduce,
    own, bottom, right, corner, keep, send, moved, turned, tight, buffer,
):
    heads = bias.shape[0] // 64
    moved[:, :4, :16, :] = first[...]
    moved[:, 4:, :16, :] = below[0].astype(F32)
    turned[:, :4, :16, :] = cot[:, 4:, :, :].astype(F32)
    turned[:, 4:, :16, :] = below[1].astype(F32)
    tight[:64] = across[...].astype(F32)
    tight[64:] = beside[...].astype(F32)
    for f, r, n in corners():
        moved[f, 4 + r, 16:20, :] = tight[n : n + 4, :]
        turned[f, 4 + r, 16:20, :] = tight[32 + n : 36 + n, :]
        moved[f, r, 16:20, :] = tight[64 + n : 68 + n, :]
        turned[f, r, 16:20, :] = tight[96 + n : 100 + n, :]
    field = tokens_of(lambda f, c: moved[f, :, 4 + 8 * c : 12 + 8 * c, :])
    cotangent = tokens_of(lambda f, c: turned[f, :, 4 + 8 * c : 12 + 8 * c, :])
    weights = (qkv, proj, expand, reduce)
    _, _, pre, bell, saved = forward(weights, field, bias[...], heads)
    grad_field, operands, grad_bias = backward(weights, saved, slope_of(pre, bell), cotangent, heads)

    def write(f, c, piece):
        moved[f, :, 4 + 8 * c : 12 + 8 * c, :] = piece

    tile_of(grad_field, write)
    own[...] = moved[:, :4, :16, :]
    bottom[...] = moved[:, 4:, :16, :].astype(BF)
    for f, r, n in corners():
        tight[n : n + 4, :] = moved[f, 4 + r, 16:20, :]
        tight[32 + n : 36 + n, :] = moved[f, r, 16:20, :]
    corner[...] = tight[:32].astype(BF)
    right[...] = tight[32:64].astype(BF)
    ahead, behind = fold_bias(grad_bias, heads)
    pack_grads(operands, ahead, behind, buffer)
    split_core(buffer, keep, send)


def split_core(buffer, keep, send):
    rows = keep.shape[0]
    core = lax.axis_index("row") % 2
    keep[...] = buffer[pl.ds(pl.multiple_of(core * rows, 16), rows), :]
    send[...] = buffer[pl.ds(pl.multiple_of((1 - core) * rows, 16), rows), :]


def plain_backward(own, above, beside, across, slope, *refs):
    saved, weights = refs[:10], refs[10:14]
    out, keep, send, middle, tight, buffer = refs[14:]
    heads = saved[5].shape[0] // 64
    middle[:, 4:] = own[...]
    middle[:, :4] = above[...].astype(F32)
    tight[:32] = across[...].astype(F32)
    tight[32:64] = beside[...].astype(F32)
    for f, r, n in corners():
        middle[f, r, :4, :] = tight[n : n + 4, :]
        middle[f, 4 + r, :4, :] = tight[32 + n : 36 + n, :]
    cotangent = tokens_of(lambda f, c: middle[f, :, 8 * c : 8 * c + 8, :])
    saved = tuple(ref[...] for ref in saved)
    grad_field, operands, grad_bias = backward(weights, saved, slope[...], cotangent, heads)

    def write(f, c, piece):
        out[f, :, 8 * c : 8 * c + 8, :] = piece

    tile_of(grad_field, write)
    ahead, behind = fold_bias(grad_bias, heads)
    pack_grads(operands, ahead, behind, buffer)
    split_core(buffer, keep, send)


def near_place():
    return lax.axis_index("row") // 2 * 2 + lax.axis_index("col") % 2


def cut(total, me, own, sends, partners, here=slice(None)):
    rows = total.shape[0] // (len(sends) + 1)
    own[here, :] = total[pl.ds(pl.multiple_of(me * rows, 16), rows), :]
    for d, send in zip(partners, sends, strict=True):
        send[here, :] = total[pl.ds(pl.multiple_of((me ^ d) * rows, 16), rows), :].astype(BF)


def add_core(keep, came, own, *rest):
    sends, total = rest[:-1], rest[-1]
    total[...] = keep[...].astype(F32) + came[...].astype(F32)
    cut(total, near_place(), own, sends, (1, 2, 3))


def sum_near(mine, one, two, three, out):
    out[...] = mine[...] + one[...].astype(F32) + two[...].astype(F32) + three[...].astype(F32)


def add_core_later(keep, came, other, *rest):
    add_core(keep, came, *rest)


def add_near(count, mine, one, two, three, other, own, *rest):
    sends, total = rest[: count - 1], rest[-1]
    rows = own.shape[0] // 2
    place = lax.axis_index("col") // 2
    partners = range(count - 1, 0, -1)
    sum_near(mine, one, two, three, total)
    cut(total, place, own, sends, partners, slice(0, rows))
    cut(other, place, own, sends, partners, slice(rows, 2 * rows))


def add_far(*refs):
    ins, out = refs[:-1], refs[-1]
    out[...] = (ins[0][...] + sum(one[...].astype(F32) for one in ins[1:])).astype(BF)


def join_far(*refs):
    ins, out = refs[:-1], refs[-1]
    rows, length = ins[0].shape[0] // 2, out.shape[0] // 2
    me = lax.axis_index("col") // 2
    for d, piece in enumerate(ins):
        for block in range(2):
            there = pl.multiple_of(block * length + (me ^ d) * rows, 16)
            out[pl.ds(there, rows), :] = piece[block * rows : block * rows + rows, :]


def finish(other, factor, *refs):
    ins, refs = refs[:4], refs[4 + 5 * other :]
    outs, buffer, done, (qkv, proj, expand, reduce, table) = refs[:5], refs[5], refs[6], refs[7:12]
    rows = ins[0].shape[0] // 2
    me = near_place()
    for block in range(2):
        for d, piece in enumerate(ins):
            there = pl.multiple_of((me ^ d) * rows, 16)
            buffer[block, pl.ds(there, rows), :] = piece[block * rows : block * rows + rows, :]
    half = (lax.axis_index("row") + other) % 2
    columns = expand.shape[2]
    copies = []

    def copy(here, there):
        copies.append(pltpu.make_async_copy(here, there, done.at[len(copies)]))
        copies[-1].start()

    @pl.when(half == 0)
    def _():
        copies.clear()
        for block in range(2):
            pairs = [
                (qkv.at[block], outs[0].at[block]),
                (proj.at[block], outs[1].at[block]),
                (expand.at[block], outs[2].at[block, :, pl.ds(0, columns)]),
            ]
            sent = lambda n, pairs=pairs: copy(*pairs[n])
            unpack_first(buffer.at[block], qkv.at[block], proj.at[block], expand.at[block], sent, factor)
        for one in copies:
            one.wait()

    @pl.when(half == 1)
    def _():
        copies.clear()
        for block in range(2):
            pairs = [
                (expand.at[block], outs[2].at[block, :, pl.ds(columns, columns)]),
                (reduce.at[block], outs[3].at[block]),
            ]
            sent = lambda n, pairs=pairs: copy(*pairs[n])
            unpack_second(buffer.at[block], expand.at[block], reduce.at[block], sent, table, block, factor)
        copy(table, outs[4])
        for one in copies:
            one.wait()


class Whole:
    def __init__(self, ref, block):
        self.ref, self.block = ref, block

    def __getitem__(self, index):
        return self.ref[self.block]


def call(kernel, outs, scratch, args, stacked=(), distant=(), micros=0.5, limit=LIMIT, far_outs=0, aliases=None):
    here, there = pl.BlockSpec(memory_space=pltpu.VMEM), pl.BlockSpec(memory_space=pltpu.HBM)
    count = len(args)

    def body(*refs):
        weights = [Whole(ref, block) for ref, (_, block) in zip(refs[count:], stacked)]
        kernel(*refs[:count], *weights, *refs[count + len(stacked) :])

    return pl.pallas_call(
        body,
        in_specs=[here] * (count + len(stacked)) + [there] * len(distant),
        out_specs=[there] * far_outs + [here] * (len(outs) - far_outs),
        out_shape=[jax.ShapeDtypeStruct(s, d) for s, d in outs],
        scratch_shapes=[pltpu.VMEM(*one) if isinstance(one, tuple) else one for one in scratch],
        input_output_aliases=aliases or {},
        compiler_params=pltpu.CompilerParams(vmem_limit_bytes=limit),
        cost_estimate=pl.CostEstimate(flops=int(micros * 1.1e9), bytes_accessed=0, transcendentals=0),
    )(*args, *(arg for arg, _ in stacked), *distant)


def local(block_input, cotangent, qkv_weight, proj_weight, expand_weight, reduce_weight, bias_table):
    frames, rows, cols, width = block_input.shape
    n_row, n_col = lax.axis_size("row"), lax.axis_size("col")
    inner = expand_weight.shape[2]
    heads = bias_table.shape[1]
    tokens = frames * rows * cols
    wide = jnp.swapaxes(reduce_weight, 1, 2)
    weights = (qkv_weight, proj_weight, expand_weight, wide)
    table = jnp.swapaxes(bias_table, 0, 1)
    axes = ("row", "col")

    def send(block, down, right):
        route = [
            (r * n_col + c, (r + down) % n_row * n_col + (c + right) % n_col)
            for r in range(n_row)
            for c in range(n_col)
        ]
        return lax.ppermute(block, axes, route)

    def swap(block, row_bits, col_bits):
        route = [
            (r * n_col + c, (r ^ row_bits) * n_col + (c ^ col_bits)) for r in range(n_row) for c in range(n_col)
        ]
        return lax.ppermute(block, axes, route)

    far = n_col // 2
    unit = 8 * far * 16
    used = (4 * width + 2 * inner) * width // 128 + 2 * 16
    size = -(-used // unit) * unit
    chunk = size // (8 * far)
    halves = [((size // 2, 128), BF)] * 2
    buffer = ((size, 128), BF)
    tile = (frames, rows, cols, width)
    strip = (frames, SHIFT, cols, width)
    patches = frames * SHIFT * SHIFT
    tight = ((4 * patches, width), F32)
    lines = ((heads * 64, 128), F32)
    sent = [(strip, F32), ((2, *strip), BF), ((2 * patches, width), BF), ((2 * patches, width), BF)]
    first, top, left, corner = call(
        plain_forward,
        sent,
        [*sent, tight, (tile, BF), *((w.shape[1:], BF) for w in weights), (tile, BF), (tile, F32), (table.shape, F32), pltpu.SemaphoreType.DMA((7,))],
        [],
        distant=(block_input, cotangent, table, *weights),
        micros=2.3,
        limit=FULL,
        far_outs=4,
    )
    halo = [send(top, -1, 0), send(left, 0, -1), send(corner, -1, -1)]
    bias, *kept = call(
        functools.partial(keep_plain, n_row, n_col),
        [
            lines,
            ((inner, tokens), F32),
            ((width, tokens), F32),
            ((1, tokens), F32),
            ((width, tokens), BF),
            ((width, tokens), BF),
            ((width, tokens), BF),
            ((heads * 64, tokens), F32),
            ((width, tokens), BF),
            ((width, tokens), F32),
            ((1, tokens), F32),
            ((inner, tokens), BF),
        ],
        [],
        [block_input, table],
        [(w, 0) for w in weights[:3]],
        micros=2.3,
    )
    own, bottom, right, corner, keep, away = call(
        shifted_block,
        [(strip, F32), (strip, BF), ((patches, width), BF), ((patches, width), BF), *halves],
        [((frames, rows, cols + 8, width), F32)] * 2 + [tight, buffer],
        [first, cotangent, *halo, bias],
        [(w, 1) for w in weights],
        micros=4.8,
    )
    back = [own, send(bottom, 1, 0), send(right, 0, 1), send(corner, 1, 1)]

    eighth, quarter, piece = (size // 8, 128), (size // 4, 128), (2 * chunk, 128)

    def near(own, *sends):
        came = [swap(one, d & 2, d & 1) for d, one in reversed(list(enumerate(sends, 1)))]
        return [own] + came[::-1]

    quarters = [(eighth, F32)] + [(eighth, BF)] * 3
    summed = [((size // 2, 128), F32)]
    shifted = call(add_core, quarters, summed, [keep, swap(away, 1, 0)])
    kept[0], *shifted = lax.optimization_barrier((kept[0], *shifted))
    (other,) = call(sum_near, [(eighth, F32)], [], near(*shifted), micros=4.0)
    input_grad, keep, away = call(
        plain_backward,
        [(tile, F32), *halves],
        [(tile, F32), tight, buffer],
        [*back, *kept],
        [(w, 0) for w in weights],
        micros=3.5,
    )
    plain = near(*call(add_core_later, quarters, summed, [keep, swap(away, 1, 0), other]))
    own, *sends = call(
        functools.partial(add_near, far),
        [(piece, F32)] + [(piece, BF)] * (far - 1),
        [(eighth, F32)],
        [*plain, other],
    )
    distant = [own] + [swap(one, 0, 2 * d) for d, one in zip(range(far - 1, 0, -1), sends, strict=True)]
    (done,) = call(add_far, [(piece, BF)], [], distant)
    distant = [done] + [swap(done, 0, 2 * d) for d in range(1, far)]
    (joined,) = call(join_far, [(quarter, BF)], [], distant)
    near = [joined] + [swap(joined, d & 2, d & 1) for d in range(1, 4)]
    factor = 1.0 / math.sqrt(frames * rows * n_row * cols * n_col)
    shapes = [(w.shape, F32) for w in (*weights, table)]
    stage = [((2, size // 2, 128), BF), pltpu.SemaphoreType.DMA((6,)), *shapes]
    stage[4] = ((2, width, inner // 2), F32)
    grads = call(functools.partial(finish, 0, factor), shapes, stage, near, far_outs=5, micros=1.2)
    qkv, proj, expand, reduce, table = call(
        functools.partial(finish, 1, factor),
        shapes,
        stage,
        [swap(one, 1, 0) for one in near],
        distant=grads,
        far_outs=5,
        aliases={4 + n: n for n in range(5)},
        micros=1.2,
    )
    return input_grad, qkv, proj, expand, jnp.swapaxes(reduce, 1, 2), jnp.swapaxes(table, 0, 1)


def solution(mesh):
    in_specs = (P(None, "row", "col", None), P(None, "row", "col", None), P(), P(), P(), P(), P())
    out_specs = (P(None, "row", "col", None), P(), P(), P(), P(), P())
    return jax.shard_map(local, mesh=mesh, in_specs=in_specs, out_specs=out_specs, check_vma=False)
```

```python
import functools
import math

import jax
import jax.numpy as jnp
from jax import lax
from jax.experimental import pallas as pl
from jax.experimental.pallas import tpu as pltpu
from jax.sharding import PartitionSpec as P

WIN = 8
SHIFT = 4
BF = jnp.bfloat16
F32 = jnp.float32
LIMIT = 48 * 1024 * 1024
FULL = 62 * 1024 * 1024
ROOT_HALF = 0.7071067811865476
DENSITY = 0.3989422804014327


def dot(a, b):
    return lax.dot_general(a, b, (((1,), (0,)), ((), ())), preferred_element_type=F32)


def dot_nt(a, b):
    return lax.dot_general(a, b, (((1,), (1,)), ((), ())), preferred_element_type=F32)


def dot_tn(a, b):
    return lax.dot_general(a, b, (((0,), (0,)), ((), ())), preferred_element_type=F32)


def iota(shape, axis):
    return lax.broadcasted_iota(jnp.int32, shape, axis)


def norm(field):
    center = field - jnp.mean(field, axis=0, keepdims=True)
    spread = jnp.mean(center * center, axis=0, keepdims=True)
    scale = lax.rsqrt(spread + 1e-05)
    return center * scale, scale


def norm_back(grad, normed, scale):
    along = jnp.mean(grad * normed, axis=0, keepdims=True)
    return scale * (grad - jnp.mean(grad, axis=0, keepdims=True) - normed * along)


class Late:
    def __init__(self, copy, here):
        self.copy, self.here = copy, here

    def ready(self):
        if self.copy is not None:
            self.copy.wait()
            self.copy = None

    def __getitem__(self, index):
        self.ready()
        return self.here[index]


def first_half(shape):
    return iota(shape, 1) < 64


def pair_mask(rows, head):
    return (iota((rows, 128), 0) // head) % 2 == iota((rows, 128), 1) // 64


def spread_bias(read, entries, heads):
    side = 2 * WIN - 1
    lanes = iota((entries, 256), 1)
    rows = iota((entries, 256), 0)
    place = lanes % 128
    down = place // 8 - 8
    right = place % 8 - jnp.where(lanes >= 128, 8, 0)
    wanted = (down + WIN - 1) * side + right + WIN - 1
    fits = (down >= 1 - WIN) & (right >= 1 - WIN)
    pick = (fits & (wanted == rows)).astype(F32)
    vectors = lax.dot_general(
        read(), pick, (((1,), (0,)), ((), ())), precision=lax.Precision.HIGHEST, preferred_element_type=F32
    )
    ahead = jnp.broadcast_to(vectors[:, None, :128], (heads, 8, 128)).reshape(heads * 8, 128)
    behind = jnp.broadcast_to(vectors[:, None, 128:], (heads, 8, 128)).reshape(heads * 8, 128)
    shape = (heads * 8, 128)
    col_j = iota(shape, 0) % 8
    col_i = iota(shape, 1) % 8
    built = jnp.zeros(shape, F32)
    for c in range(8):
        line = jnp.where(col_i >= c, pltpu.roll(ahead, 64 + c, 1), pltpu.roll(behind, 56 + c, 1))
        built = jnp.where(col_j == c, line, built)
    rolled = [built] + [pltpu.roll(built, 8 * r, 1) for r in range(1, 8)]
    rolled = [jnp.where(first_half(shape), one, pltpu.roll(one, 64, 1)) for one in rolled]
    parts = []
    for h in range(heads):
        for r in range(8):
            parts.append(rolled[r][8 * h : 8 * h + 8])
    return jnp.concatenate(parts, axis=0)


def fold_bias(grad, heads):
    folded = jnp.where(first_half(grad.shape), grad + pltpu.roll(grad, 64, 1), 0.0)
    split = folded.reshape(heads, 8, 8, 128)
    total = jnp.zeros((heads * 8, 128), F32)
    for r in range(8):
        piece = split[:, r].reshape(heads * 8, 128)
        total = total + pltpu.roll(piece, 64 - 8 * r, 1)
    shape = (heads * 8, 128)
    col_j = iota(shape, 0) % 8
    col_i = iota(shape, 1) % 8
    ahead = jnp.zeros(shape, F32)
    behind = jnp.zeros(shape, F32)
    for c in range(8):
        mine = jnp.where((col_j == c) & (col_i >= c), total, 0.0)
        ahead = ahead + (pltpu.roll(mine, 128 - c, 1) if c else mine)
        rest = jnp.where((col_j == c) & (col_i < c), total, 0.0)
        behind = behind + pltpu.roll(rest, 8 - c, 1)
    ahead = jnp.sum(ahead.reshape(heads, 8, 128), axis=1)
    behind = jnp.sum(behind.reshape(heads, 8, 128), axis=1)
    return ahead, behind


def shift_mask(shape, last_row, last_col):
    j = iota(shape, 0) % 64
    lane = iota(shape, 1)
    i = lane % 64
    low = (j // 8 >= SHIFT) != (i // 8 >= SHIFT)
    side = (j % 8 >= SHIFT) != (i % 8 >= SHIFT)
    differ = (low & last_row) | (side & (lane >= 64) & last_col)
    return jnp.where(differ, -10000.0, 0.0)


def wide_of(field, mask):
    field = field.astype(F32)
    half = first_half(field.shape)
    swapped = pltpu.roll(field, 64, 1)
    return [
        jnp.where(mask, one, 0.0).astype(BF) for one in (jnp.where(half, field, swapped), jnp.where(half, swapped, field))
    ]


def by_pairs(product, lhs, rhs, heads, left, right):
    return jnp.concatenate(
        [
            product(lhs[left * n : left * n + left], rhs[right * n : right * n + right])
            for n in range(heads // 2)
        ],
        axis=0,
    )


def forward(weights, field, bias, heads):
    width, tokens = field.shape
    head = width // heads
    two = 2 * head
    mask = pair_mask(width, head)
    center, scale = norm(field)
    normed = center.astype(BF)
    mixed = dot_tn(weights[0][...], normed)
    query = (mixed[:width] * head ** (-0.5)).astype(BF)
    keys = mixed[width : 2 * width].astype(BF)
    values = mixed[2 * width :].astype(BF)
    probs, attended = [], []
    half = first_half((width, 128))
    tall_half = first_half((heads * 64, 128))
    for p in range(tokens // 128):
        lanes = slice(128 * p, 128 * p + 128)
        k = wide_of(mixed[width : 2 * width, lanes], mask)
        v = wide_of(mixed[2 * width :, lanes], mask)
        q = query[:, lanes]
        first, second = (by_pairs(dot_tn, one, q, heads, two, two) for one in k)
        scores = jnp.where(tall_half, first, second) + bias
        scores = scores.reshape(heads, 64, 128)
        expos = jnp.exp(scores - jnp.max(scores, axis=1, keepdims=True))
        prob = (expos / jnp.sum(expos, axis=1, keepdims=True)).reshape(heads * 64, 128)
        prob_b = prob.astype(BF)
        first, second = (by_pairs(dot, one, prob_b, heads, two, 128) for one in v)
        attended.append(jnp.where(half, first, second))
        probs.append(prob)
    attended = jnp.concatenate(attended, axis=1).astype(BF)
    prob = jnp.concatenate(probs, axis=1)
    resid = field + dot_tn(weights[1][...], attended)
    center_two, scale_two = norm(resid)
    normed_two = center_two.astype(BF)
    pre = dot_tn(weights[2][...], normed_two)
    bell = 0.5 * (1.0 + lax.erf(pre * ROOT_HALF))
    hidden = (pre * bell).astype(BF)
    saved = (center, scale, query, keys, values, prob, attended, center_two, scale_two, hidden)
    return resid, hidden, pre, bell, saved


def slope_of(pre, bell):
    return bell + pre * (DENSITY * jnp.exp(-0.5 * pre * pre))


def backward(weights, saved, slope, grad, heads):
    proj_w, expand_w, reduce_w = (w[...] for w in weights[1:])
    center, scale, query, keys, values, prob, attended, center_two, scale_two, hidden = saved
    width, tokens = grad.shape
    head = width // heads
    two = 2 * head
    mask = pair_mask(width, head)
    grad_b = grad.astype(BF)
    grad_hidden = dot_tn(reduce_w, grad_b).astype(BF).astype(F32)
    grad_pre = (grad_hidden * slope).astype(BF)
    grad_two = dot(expand_w, grad_pre).astype(BF).astype(F32)
    grad_resid = grad + norm_back(grad_two, center_two, scale_two)
    grad_resid_b = grad_resid.astype(BF)
    grad_att = dot(proj_w, grad_resid_b)
    half = first_half((width, 128))
    tall_half = first_half((heads * 64, 128))
    grad_q, grad_k, grad_v = [], [], []
    grad_bias = jnp.zeros((heads * 64, 128), F32)
    for p in range(tokens // 128):
        lanes = slice(128 * p, 128 * p + 128)
        k = wide_of(keys[:, lanes], mask)
        v = wide_of(values[:, lanes], mask)
        p_f = prob[:, lanes]
        p_b = p_f.astype(BF)
        att = grad_att[:, lanes]
        att_b = att.astype(BF)
        zero = jnp.zeros_like(att)
        att_w = (jnp.where(half, att, zero).astype(BF), jnp.where(half, zero, att).astype(BF))
        query_f = query[:, lanes].astype(F32)
        query_w = (jnp.where(half, query_f, zero).astype(BF), jnp.where(half, zero, query_f).astype(BF))
        first, second = (by_pairs(dot_tn, one, att_b, heads, two, two) for one in v)
        grad_prob = jnp.where(tall_half, first, second)
        grad_prob = grad_prob.astype(BF).astype(F32)
        along = jnp.sum((p_f * grad_prob).reshape(heads, 64, 128), axis=1, keepdims=True)
        grad_score = p_f * (grad_prob.reshape(heads, 64, 128) - along).reshape(heads * 64, 128)
        grad_bias = grad_bias + grad_score
        score_b = grad_score.astype(BF)
        first, second = (by_pairs(dot, one, score_b, heads, two, 128) for one in k)
        grad_q.append(jnp.where(half, first, second))
        for store, lhs, rhs in ((grad_k, query_w, score_b), (grad_v, att_w, p_b)):
            both = []
            for w in range(2):
                folded = jnp.where(mask, by_pairs(dot_nt, lhs[w], rhs, heads, two, 128), 0.0)
                both.append(folded + pltpu.roll(folded, 64, 1))
            store.append(jnp.where(half, both[0], both[1]))
    grad_q = jnp.concatenate(grad_q, axis=1).astype(BF).astype(F32) * head ** (-0.5)
    grad_k = jnp.concatenate(grad_k, axis=1)
    grad_v = jnp.concatenate(grad_v, axis=1)
    grad_mixed = jnp.concatenate([grad_q, grad_k, grad_v], axis=0).astype(BF)
    operands = (center.astype(BF), grad_mixed, attended, grad_resid_b, center_two.astype(BF), grad_pre, hidden, grad_b)
    return grad_resid, operands, grad_bias


def field_grad(qkv_w, grad_mixed, grad_resid, center, scale):
    grad_normed = dot(qkv_w, grad_mixed).astype(BF).astype(F32)
    return grad_resid + norm_back(grad_normed, center, scale)


def pack_grads(operands, ahead, behind, buffer):
    normed, grad_mixed, attended, grad_resid, normed_two, grad_pre, hidden, grad = operands
    width = normed.shape[0]
    qkv = dot_nt(normed, grad_mixed)
    proj = dot_nt(attended, grad_resid)
    expand = dot_nt(normed_two, grad_pre)
    reduce = dot_nt(grad, hidden)
    inner = hidden.shape[0]
    at = 0

    def put(block):
        nonlocal at
        buffer[at : at + block.shape[0], :] = block.astype(BF)
        at += block.shape[0]

    full = 3 * width // 128
    for n in range(full):
        put(qkv[:, 128 * n : 128 * n + 128])
    put(jnp.concatenate([qkv[:, 128 * full :], proj[:, 128:]], axis=1))
    put(proj[:, :128])
    columns = inner // 128
    for n in range(columns // 2):
        put(expand[:, 128 * n : 128 * n + 128])
    half = buffer.shape[0] // 2
    if half > at:
        put(jnp.zeros((half - at, 128), F32))
    for n in range(columns // 2, columns):
        put(expand[:, 128 * n : 128 * n + 128])
    for n in range(columns):
        put(reduce[:, 128 * n : 128 * n + 128])
    heads = ahead.shape[0]
    put(jnp.concatenate([ahead, behind, jnp.zeros((16 - 2 * heads, 128), F32)], axis=0))
    if buffer.shape[0] > at:
        put(jnp.zeros((buffer.shape[0] - at, 128), F32))


class Taker:
    def __init__(self, buffer, factor):
        self.buffer, self.factor, self.at = buffer, factor, 0

    def __call__(self, rows):
        piece = self.buffer[self.at : self.at + rows, :]
        self.at += rows
        return piece.astype(F32) * self.factor


def unpack_first(buffer, qkv, proj, expand, sent, factor):
    take = Taker(buffer, factor)
    width = proj.shape[0]
    full = 3 * width // 128
    for n in range(full):
        qkv[:, 128 * n : 128 * n + 128] = take(width)
    shared = take(width)
    qkv[:, 128 * full :] = shared[:, :64]
    sent(0)
    proj[:, 128:] = shared[:, 64:]
    proj[:, :128] = take(width)
    sent(1)
    for n in range(expand.shape[1] // 128):
        expand[:, 128 * n : 128 * n + 128] = take(width)
    sent(2)


def unpack_second(buffer, expand, reduce, sent, table, block, factor):
    take = Taker(buffer, factor)
    width = reduce.shape[0]
    for which, one in enumerate((expand, reduce)):
        for n in range(one.shape[1] // 128):
            one[:, 128 * n : 128 * n + 128] = take(width)
        sent(which)
    vectors = buffer[take.at : take.at + 16, :]
    heads, _, entries = table.shape
    side = 2 * WIN - 1
    shape = (128, entries)
    rows, lanes = iota(shape, 0), iota(shape, 1)
    down, right = lanes // side - (WIN - 1), lanes % side - (WIN - 1)
    base = 8 * (down + 8) + right
    ahead = ((right >= 0) & (base == rows)).astype(F32).astype(BF)
    behind = ((right < 0) & (base + 8 == rows)).astype(F32).astype(BF)
    table[:, block, :] = (dot(vectors, ahead)[:heads] + dot(vectors, behind)[heads : 2 * heads]) * factor


def tokens_of(read):
    flat = [read(f, c).reshape(64, -1) for f in range(2) for c in range(2)]
    return jnp.concatenate(flat, axis=0).T


def tile_of(field, write):
    natural = field.T
    for f in range(2):
        for c in range(2):
            n = 64 * (2 * f + c)
            write(f, c, natural[n : n + 64].reshape(8, 8, -1))


def corners():
    return [(f, r, 16 * f + 4 * r) for f in range(2) for r in range(4)]


def plain_forward(x_far, cot_far, table_far, *refs):
    far, outs, (first, top, left, corner), (tight, *near), done = refs[:4], refs[4:8], refs[8:12], refs[12:21], refs[21]
    heads = table_far.shape[0]
    qkv_far, *rest = (there.at[0] for there in far)
    pairs = [(x_far, near[0]), (qkv_far, near[1]), *zip(rest, near[2:5], strict=True)]
    pairs[1:1] = [(table_far, near[7])]
    pairs.append((cot_far, near[5]))
    copies = [pltpu.make_async_copy(there, here, done.at[n]) for n, (there, here) in enumerate(pairs)]
    for copy in copies:
        copy.start()
    x_ref, table, qkv, proj, expand, reduce, cot = (
        Late(copy, here) for copy, (_, here) in zip(copies, pairs, strict=True)
    )
    whole = near[6]

    def write(f, c, piece):
        whole[f, :, 8 * c : 8 * c + 8, :] = piece

    def read():
        for one in (x_ref, qkv):
            one.ready()
        return table[:, 0, :]

    bias = spread_bias(read, table_far.shape[2], heads)
    field = tokens_of(lambda f, c: x_ref[f, :, 8 * c : 8 * c + 8, :].astype(F32))
    resid, hidden, _, _, _ = forward((qkv, proj, expand), field, bias, heads)
    tile_of(resid + dot(reduce[...], hidden), write)
    first[...] = whole[:, SHIFT:]
    top[0] = whole[:, :SHIFT].astype(BF)
    top[1] = cot[:, :SHIFT]
    for f, r, n in corners():
        tight[n : n + 4, :] = whole[f, r, :4, :]
        tight[32 + n : 36 + n, :] = cot[f, r, :8, :].astype(F32)[:4]
        tight[64 + n : 68 + n, :] = whole[f, 4 + r, :4, :]
        tight[96 + n : 100 + n, :] = cot[f, 4 + r, :8, :].astype(F32)[:4]
    corner[...] = tight[:64].astype(BF)
    left[...] = tight[64:].astype(BF)
    copies = [pltpu.make_async_copy(here, there, done.at[n]) for n, (here, there) in enumerate(zip((first, top, left, corner), outs, strict=True))]
    for copy in copies:
        copy.start()
    for copy in copies:
        copy.wait()


def keep_plain(n_row, n_col, x_ref, table, qkv, proj, expand, bias_out, slope_out, *outs):
    heads = table.shape[0]
    field = tokens_of(lambda f, c: x_ref[f, :, 8 * c : 8 * c + 8, :].astype(F32))
    _, _, pre, bell, saved = forward((qkv, proj, expand), field, spread_bias(lambda: table[:, 0, :], table.shape[2], heads), heads)
    slope_out[...] = slope_of(pre, bell)
    for ref, value in zip(outs, saved, strict=True):
        ref[...] = value
    last_row = lax.axis_index("row") == n_row - 1
    last_col = lax.axis_index("col") == n_col - 1
    bias_out[...] = spread_bias(lambda: table[:, 1, :], table.shape[2], heads) + shift_mask(bias_out.shape, last_row, last_col)


def shifted_block(
    first, cot, below, across, beside, bias, qkv, proj, expand, reduce,
    own, bottom, right, corner, keep, send, moved, turned, tight, buffer,
):
    heads = bias.shape[0] // 64
    moved[:, :4, :16, :] = first[...]
    moved[:, 4:, :16, :] = below[0].astype(F32)
    turned[:, :4, :16, :] = cot[:, 4:, :, :].astype(F32)
    turned[:, 4:, :16, :] = below[1].astype(F32)
    tight[:64] = across[...].astype(F32)
    tight[64:] = beside[...].astype(F32)
    for f, r, n in corners():
        moved[f, 4 + r, 16:20, :] = tight[n : n + 4, :]
        turned[f, 4 + r, 16:20, :] = tight[32 + n : 36 + n, :]
        moved[f, r, 16:20, :] = tight[64 + n : 68 + n, :]
        turned[f, r, 16:20, :] = tight[96 + n : 100 + n, :]
    field = tokens_of(lambda f, c: moved[f, :, 4 + 8 * c : 12 + 8 * c, :])
    cotangent = tokens_of(lambda f, c: turned[f, :, 4 + 8 * c : 12 + 8 * c, :])
    weights = (qkv, proj, expand, reduce)
    _, _, pre, bell, saved = forward(weights, field, bias[...], heads)
    grad_resid, operands, grad_bias = backward(weights, saved, slope_of(pre, bell), cotangent, heads)
    grad_field = field_grad(qkv[...], operands[1], grad_resid, *saved[:2])

    def write(f, c, piece):
        moved[f, :, 4 + 8 * c : 12 + 8 * c, :] = piece

    tile_of(grad_field, write)
    own[...] = moved[:, :4, :16, :]
    bottom[...] = moved[:, 4:, :16, :].astype(BF)
    for f, r, n in corners():
        tight[n : n + 4, :] = moved[f, 4 + r, 16:20, :]
        tight[32 + n : 36 + n, :] = moved[f, r, 16:20, :]
    corner[...] = tight[:32].astype(BF)
    right[...] = tight[32:64].astype(BF)
    ahead, behind = fold_bias(grad_bias, heads)
    pack_grads(operands, ahead, behind, buffer)
    split_core(buffer, keep, send)


def split_core(buffer, keep, send):
    rows = keep.shape[0]
    core = lax.axis_index("row") % 2
    keep[...] = buffer[pl.ds(pl.multiple_of(core * rows, 16), rows), :]
    send[...] = buffer[pl.ds(pl.multiple_of((1 - core) * rows, 16), rows), :]


def plain_backward(own, above, across, beside, slope, *refs):
    saved, weights = refs[:10], refs[10:14]
    keep, send, mixed_out, resid_out, middle, tight, buffer = refs[14:]
    heads = saved[5].shape[0] // 64
    middle[:, 4:] = own[...]
    middle[:, :4] = above[...].astype(F32)
    tight[:32] = across[...].astype(F32)
    tight[32:64] = beside[...].astype(F32)
    for f, r, n in corners():
        middle[f, r, :4, :] = tight[n : n + 4, :]
        middle[f, 4 + r, :4, :] = tight[32 + n : 36 + n, :]
    cotangent = tokens_of(lambda f, c: middle[f, :, 8 * c : 8 * c + 8, :])
    saved = tuple(ref[...] for ref in saved)
    grad_resid, operands, grad_bias = backward(weights, saved, slope[...], cotangent, heads)
    mixed_out[...] = operands[1]
    resid_out[...] = grad_resid
    ahead, behind = fold_bias(grad_bias, heads)
    pack_grads(operands, ahead, behind, buffer)
    split_core(buffer, keep, send)


def plain_field(mixed, resid, center, scale, qkv, out):
    grad_field = field_grad(qkv[...], mixed[...], resid[...], center[...], scale[...])

    def write(f, c, piece):
        out[f, :, 8 * c : 8 * c + 8, :] = piece

    tile_of(grad_field, write)


def near_place():
    return lax.axis_index("row") // 2 * 2 + lax.axis_index("col") % 2


def cut(total, me, own, sends, partners, here=slice(None)):
    rows = total.shape[0] // (len(sends) + 1)
    own[here, :] = total[pl.ds(pl.multiple_of(me * rows, 16), rows), :]
    for d, send in zip(partners, sends, strict=True):
        send[here, :] = total[pl.ds(pl.multiple_of((me ^ d) * rows, 16), rows), :].astype(BF)


def add_core(keep, came, own, *rest):
    sends, total = rest[:-1], rest[-1]
    total[...] = keep[...].astype(F32) + came[...].astype(F32)
    cut(total, near_place(), own, sends, (1, 2, 3))


def sum_near(mine, one, two, three, out):
    out[...] = mine[...] + one[...].astype(F32) + two[...].astype(F32) + three[...].astype(F32)


def add_core_later(keep, came, other, *rest):
    add_core(keep, came, *rest)


def add_near(count, mine, one, two, three, other, own, *rest):
    sends, total = rest[: count - 1], rest[-1]
    rows = own.shape[0] // 2
    place = lax.axis_index("col") // 2
    partners = range(count - 1, 0, -1)
    sum_near(mine, one, two, three, total)
    cut(total, place, own, sends, partners, slice(0, rows))
    cut(other, place, own, sends, partners, slice(rows, 2 * rows))


def add_far(*refs):
    ins, out = refs[:-1], refs[-1]
    out[...] = (ins[0][...] + sum(one[...].astype(F32) for one in ins[1:])).astype(BF)


def join_far(*refs):
    ins, out = refs[:-1], refs[-1]
    rows, length = ins[0].shape[0] // 2, out.shape[0] // 2
    me = lax.axis_index("col") // 2
    for d, piece in enumerate(ins):
        for block in range(2):
            there = pl.multiple_of(block * length + (me ^ d) * rows, 16)
            out[pl.ds(there, rows), :] = piece[block * rows : block * rows + rows, :]


def finish(other, factor, *refs):
    ins, refs = refs[:4], refs[4 + 5 * other :]
    outs, buffer, done, (qkv, proj, expand, reduce, table) = refs[:5], refs[5], refs[6], refs[7:12]
    rows = ins[0].shape[0] // 2
    me = near_place()
    for block in range(2):
        for d, piece in enumerate(ins):
            there = pl.multiple_of((me ^ d) * rows, 16)
            buffer[block, pl.ds(there, rows), :] = piece[block * rows : block * rows + rows, :]
    half = (lax.axis_index("row") + other) % 2
    columns = expand.shape[2]
    copies = []

    def copy(here, there):
        copies.append(pltpu.make_async_copy(here, there, done.at[len(copies)]))
        copies[-1].start()

    @pl.when(half == 0)
    def _():
        copies.clear()
        for block in range(2):
            pairs = [
                (qkv.at[block], outs[0].at[block]),
                (proj.at[block], outs[1].at[block]),
                (expand.at[block], outs[2].at[block, :, pl.ds(0, columns)]),
            ]
            sent = lambda n, pairs=pairs: copy(*pairs[n])
            unpack_first(buffer.at[block], qkv.at[block], proj.at[block], expand.at[block], sent, factor)
        for one in copies:
            one.wait()

    @pl.when(half == 1)
    def _():
        copies.clear()
        for block in range(2):
            pairs = [
                (expand.at[block], outs[2].at[block, :, pl.ds(columns, columns)]),
                (reduce.at[block], outs[3].at[block]),
            ]
            sent = lambda n, pairs=pairs: copy(*pairs[n])
            unpack_second(buffer.at[block], expand.at[block], reduce.at[block], sent, table, block, factor)
        copy(table, outs[4])
        for one in copies:
            one.wait()


class Whole:
    def __init__(self, ref, block):
        self.ref, self.block = ref, block

    def __getitem__(self, index):
        return self.ref[self.block]


def call(kernel, outs, scratch, args, stacked=(), distant=(), micros=0.5, limit=LIMIT, far_outs=0, aliases=None):
    here, there = pl.BlockSpec(memory_space=pltpu.VMEM), pl.BlockSpec(memory_space=pltpu.HBM)
    count = len(args)

    def body(*refs):
        weights = [Whole(ref, block) for ref, (_, block) in zip(refs[count:], stacked)]
        kernel(*refs[:count], *weights, *refs[count + len(stacked) :])

    return pl.pallas_call(
        body,
        in_specs=[here] * (count + len(stacked)) + [there] * len(distant),
        out_specs=[there] * far_outs + [here] * (len(outs) - far_outs),
        out_shape=[jax.ShapeDtypeStruct(s, d) for s, d in outs],
        scratch_shapes=[pltpu.VMEM(*one) if isinstance(one, tuple) else one for one in scratch],
        input_output_aliases=aliases or {},
        compiler_params=pltpu.CompilerParams(vmem_limit_bytes=limit),
        cost_estimate=pl.CostEstimate(flops=int(micros * 1.1e9), bytes_accessed=0, transcendentals=0),
    )(*args, *(arg for arg, _ in stacked), *distant)


def local(block_input, cotangent, qkv_weight, proj_weight, expand_weight, reduce_weight, bias_table):
    frames, rows, cols, width = block_input.shape
    n_row, n_col = lax.axis_size("row"), lax.axis_size("col")
    inner = expand_weight.shape[2]
    heads = bias_table.shape[1]
    tokens = frames * rows * cols
    wide = jnp.swapaxes(reduce_weight, 1, 2)
    weights = (qkv_weight, proj_weight, expand_weight, wide)
    table = jnp.swapaxes(bias_table, 0, 1)
    axes = ("row", "col")

    def send(block, down, right):
        route = [
            (r * n_col + c, (r + down) % n_row * n_col + (c + right) % n_col)
            for r in range(n_row)
            for c in range(n_col)
        ]
        return lax.ppermute(block, axes, route)

    def swap(block, row_bits, col_bits):
        route = [
            (r * n_col + c, (r ^ row_bits) * n_col + (c ^ col_bits)) for r in range(n_row) for c in range(n_col)
        ]
        return lax.ppermute(block, axes, route)

    far = n_col // 2
    unit = 8 * far * 16
    used = (4 * width + 2 * inner) * width // 128 + 2 * 16
    size = -(-used // unit) * unit
    chunk = size // (8 * far)
    halves = [((size // 2, 128), BF)] * 2
    buffer = ((size, 128), BF)
    tile = (frames, rows, cols, width)
    strip = (frames, SHIFT, cols, width)
    patches = frames * SHIFT * SHIFT
    tight = ((4 * patches, width), F32)
    lines = ((heads * 64, 128), F32)
    sent = [(strip, F32), ((2, *strip), BF), ((2 * patches, width), BF), ((2 * patches, width), BF)]
    first, top, left, corner = call(
        plain_forward,
        sent,
        [*sent, tight, (tile, BF), *((w.shape[1:], BF) for w in weights), (tile, BF), (tile, F32), (table.shape, F32), pltpu.SemaphoreType.DMA((7,))],
        [],
        distant=(block_input, cotangent, table, *weights),
        micros=2.3,
        limit=FULL,
        far_outs=4,
    )
    halo = [send(top, -1, 0), send(corner, -1, -1), send(left, 0, -1)]
    bias, *kept = call(
        functools.partial(keep_plain, n_row, n_col),
        [
            lines,
            ((inner, tokens), F32),
            ((width, tokens), F32),
            ((1, tokens), F32),
            ((width, tokens), BF),
            ((width, tokens), BF),
            ((width, tokens), BF),
            ((heads * 64, tokens), F32),
            ((width, tokens), BF),
            ((width, tokens), F32),
            ((1, tokens), F32),
            ((inner, tokens), BF),
        ],
        [],
        [block_input, table],
        [(w, 0) for w in weights[:3]],
        micros=2.3,
    )
    own, bottom, right, corner, keep, away = call(
        shifted_block,
        [(strip, F32), (strip, BF), ((patches, width), BF), ((patches, width), BF), *halves],
        [((frames, rows, cols + 8, width), F32)] * 2 + [tight, buffer],
        [first, cotangent, *halo, bias],
        [(w, 1) for w in weights],
        micros=4.8,
    )
    back = [own, send(bottom, 1, 0), send(corner, 1, 1), send(right, 0, 1)]

    eighth, quarter, piece = (size // 8, 128), (size // 4, 128), (2 * chunk, 128)

    def near(own, *sends):
        came = [swap(one, d & 2, d & 1) for d, one in reversed(list(enumerate(sends, 1)))]
        return [own] + came[::-1]

    quarters = [(eighth, F32)] + [(eighth, BF)] * 3
    summed = [((size // 2, 128), F32)]
    shifted = call(add_core, quarters, summed, [keep, swap(away, 1, 0)])
    kept[0], *shifted = lax.optimization_barrier((kept[0], *shifted))
    (other,) = call(sum_near, [(eighth, F32)], [], near(*shifted), micros=4.0)
    keep, away, mixed, resid = call(
        plain_backward,
        [*halves, ((3 * width, tokens), BF), ((width, tokens), F32)],
        [(tile, F32), tight, buffer],
        [*back, *kept],
        [(w, 0) for w in weights],
        micros=3.0,
    )
    (input_grad,) = call(
        plain_field, [(tile, F32)], [], [mixed, resid, kept[1], kept[2]], [(qkv_weight, 0)], micros=1.0
    )
    plain = near(*call(add_core_later, quarters, summed, [keep, swap(away, 1, 0), other]))
    own, *sends = call(
        functools.partial(add_near, far),
        [(piece, F32)] + [(piece, BF)] * (far - 1),
        [(eighth, F32)],
        [*plain, other],
    )
    distant = [own] + [swap(one, 0, 2 * d) for d, one in zip(range(far - 1, 0, -1), sends, strict=True)]
    distant[0], input_grad = lax.optimization_barrier((distant[0], input_grad))
    (done,) = call(add_far, [(piece, BF)], [], distant)
    distant = [done] + [swap(done, 0, 2 * d) for d in range(1, far)]
    (joined,) = call(join_far, [(quarter, BF)], [], distant)
    near = [joined] + [swap(joined, d & 2, d & 1) for d in range(1, 4)]
    factor = 1.0 / math.sqrt(frames * rows * n_row * cols * n_col)
    shapes = [(w.shape, F32) for w in (*weights, table)]
    stage = [((2, size // 2, 128), BF), pltpu.SemaphoreType.DMA((6,)), *shapes]
    stage[4] = ((2, width, inner // 2), F32)
    grads = call(functools.partial(finish, 0, factor), shapes, stage, near, far_outs=5, micros=1.2)
    qkv, proj, expand, reduce, table = call(
        functools.partial(finish, 1, factor),
        shapes,
        stage,
        [swap(one, 1, 0) for one in near],
        distant=grads,
        far_outs=5,
        aliases={4 + n: n for n in range(5)},
        micros=1.2,
    )
    return input_grad, qkv, proj, expand, jnp.swapaxes(reduce, 1, 2), jnp.swapaxes(table, 0, 1)


def solution(mesh):
    in_specs = (P(None, "row", "col", None), P(None, "row", "col", None), P(), P(), P(), P(), P())
    out_specs = (P(None, "row", "col", None), P(), P(), P(), P(), P())
    return jax.shard_map(local, mesh=mesh, in_specs=in_specs, out_specs=out_specs, check_vma=False)
```

```python
import functools
import math

import jax
import jax.numpy as jnp
from jax import lax
from jax.experimental import pallas as pl
from jax.experimental.pallas import tpu as pltpu
from jax.sharding import PartitionSpec as P

WIN = 8
SHIFT = 4
BF = jnp.bfloat16
F32 = jnp.float32
LIMIT = 48 * 1024 * 1024
FULL = 62 * 1024 * 1024
ROOT_HALF = 0.7071067811865476
DENSITY = 0.3989422804014327


def dot(a, b):
    return lax.dot_general(a, b, (((1,), (0,)), ((), ())), preferred_element_type=F32)


def dot_nt(a, b):
    return lax.dot_general(a, b, (((1,), (1,)), ((), ())), preferred_element_type=F32)


def dot_tn(a, b):
    return lax.dot_general(a, b, (((0,), (0,)), ((), ())), preferred_element_type=F32)


def iota(shape, axis):
    return lax.broadcasted_iota(jnp.int32, shape, axis)


def norm(field):
    center = field - jnp.mean(field, axis=0, keepdims=True)
    spread = jnp.mean(center * center, axis=0, keepdims=True)
    scale = lax.rsqrt(spread + 1e-05)
    return center * scale, scale


def norm_back(grad, normed, scale):
    along = jnp.mean(grad * normed, axis=0, keepdims=True)
    return scale * (grad - jnp.mean(grad, axis=0, keepdims=True) - normed * along)


class Late:
    def __init__(self, copy, here):
        self.copy, self.here = copy, here

    def ready(self):
        if self.copy is not None:
            self.copy.wait()
            self.copy = None

    def __getitem__(self, index):
        self.ready()
        return self.here[index]


def first_half(shape):
    return iota(shape, 1) < 64


def pair_mask(rows, head):
    return (iota((rows, 128), 0) // head) % 2 == iota((rows, 128), 1) // 64


def spread_bias(read, entries, heads):
    side = 2 * WIN - 1
    lanes = iota((entries, 256), 1)
    rows = iota((entries, 256), 0)
    place = lanes % 128
    down = place // 8 - 8
    right = place % 8 - jnp.where(lanes >= 128, 8, 0)
    wanted = (down + WIN - 1) * side + right + WIN - 1
    fits = (down >= 1 - WIN) & (right >= 1 - WIN)
    pick = (fits & (wanted == rows)).astype(F32)
    vectors = lax.dot_general(
        read(), pick, (((1,), (0,)), ((), ())), precision=lax.Precision.HIGHEST, preferred_element_type=F32
    )
    ahead = jnp.broadcast_to(vectors[:, None, :128], (heads, 8, 128)).reshape(heads * 8, 128)
    behind = jnp.broadcast_to(vectors[:, None, 128:], (heads, 8, 128)).reshape(heads * 8, 128)
    shape = (heads * 8, 128)
    col_j = iota(shape, 0) % 8
    col_i = iota(shape, 1) % 8
    built = jnp.zeros(shape, F32)
    for c in range(8):
        line = jnp.where(col_i >= c, pltpu.roll(ahead, 64 + c, 1), pltpu.roll(behind, 56 + c, 1))
        built = jnp.where(col_j == c, line, built)
    rolled = [built] + [pltpu.roll(built, 8 * r, 1) for r in range(1, 8)]
    rolled = [jnp.where(first_half(shape), one, pltpu.roll(one, 64, 1)) for one in rolled]
    parts = []
    for h in range(heads):
        for r in range(8):
            parts.append(rolled[r][8 * h : 8 * h + 8])
    return jnp.concatenate(parts, axis=0)


def fold_bias(grad, heads):
    folded = jnp.where(first_half(grad.shape), grad + pltpu.roll(grad, 64, 1), 0.0)
    split = folded.reshape(heads, 8, 8, 128)
    total = jnp.zeros((heads * 8, 128), F32)
    for r in range(8):
        piece = split[:, r].reshape(heads * 8, 128)
        total = total + pltpu.roll(piece, 64 - 8 * r, 1)
    shape = (heads * 8, 128)
    col_j = iota(shape, 0) % 8
    col_i = iota(shape, 1) % 8
    ahead = jnp.zeros(shape, F32)
    behind = jnp.zeros(shape, F32)
    for c in range(8):
        mine = jnp.where((col_j == c) & (col_i >= c), total, 0.0)
        ahead = ahead + (pltpu.roll(mine, 128 - c, 1) if c else mine)
        rest = jnp.where((col_j == c) & (col_i < c), total, 0.0)
        behind = behind + pltpu.roll(rest, 8 - c, 1)
    ahead = jnp.sum(ahead.reshape(heads, 8, 128), axis=1)
    behind = jnp.sum(behind.reshape(heads, 8, 128), axis=1)
    return ahead, behind


def shift_mask(shape, last_row, last_col):
    j = iota(shape, 0) % 64
    lane = iota(shape, 1)
    i = lane % 64
    low = (j // 8 >= SHIFT) != (i // 8 >= SHIFT)
    side = (j % 8 >= SHIFT) != (i % 8 >= SHIFT)
    differ = (low & last_row) | (side & (lane >= 64) & last_col)
    return jnp.where(differ, -10000.0, 0.0)


def wide_of(field, mask):
    field = field.astype(F32)
    half = first_half(field.shape)
    swapped = pltpu.roll(field, 64, 1)
    return [
        jnp.where(mask, one, 0.0).astype(BF) for one in (jnp.where(half, field, swapped), jnp.where(half, swapped, field))
    ]


def by_pairs(product, lhs, rhs, heads, left, right):
    return jnp.concatenate(
        [
            product(lhs[left * n : left * n + left], rhs[right * n : right * n + right])
            for n in range(heads // 2)
        ],
        axis=0,
    )


def forward(weights, field, bias, heads):
    width, tokens = field.shape
    head = width // heads
    two = 2 * head
    mask = pair_mask(width, head)
    center, scale = norm(field)
    normed = center.astype(BF)
    mixed = dot_tn(weights[0][...], normed)
    query = (mixed[:width] * head ** (-0.5)).astype(BF)
    keys = mixed[width : 2 * width].astype(BF)
    values = mixed[2 * width :].astype(BF)
    probs, attended = [], []
    half = first_half((width, 128))
    tall_half = first_half((heads * 64, 128))
    for p in range(tokens // 128):
        lanes = slice(128 * p, 128 * p + 128)
        k = wide_of(mixed[width : 2 * width, lanes], mask)
        v = wide_of(mixed[2 * width :, lanes], mask)
        q = query[:, lanes]
        first, second = (by_pairs(dot_tn, one, q, heads, two, two) for one in k)
        scores = jnp.where(tall_half, first, second) + bias
        scores = scores.reshape(heads, 64, 128)
        expos = jnp.exp(scores - jnp.max(scores, axis=1, keepdims=True))
        prob = (expos / jnp.sum(expos, axis=1, keepdims=True)).reshape(heads * 64, 128)
        prob_b = prob.astype(BF)
        first, second = (by_pairs(dot, one, prob_b, heads, two, 128) for one in v)
        attended.append(jnp.where(half, first, second))
        probs.append(prob)
    attended = jnp.concatenate(attended, axis=1).astype(BF)
    prob = jnp.concatenate(probs, axis=1)
    resid = field + dot_tn(weights[1][...], attended)
    center_two, scale_two = norm(resid)
    normed_two = center_two.astype(BF)
    pre = dot_tn(weights[2][...], normed_two)
    bell = 0.5 * (1.0 + lax.erf(pre * ROOT_HALF))
    hidden = (pre * bell).astype(BF)
    saved = (center, scale, query, keys, values, prob, attended, center_two, scale_two, hidden)
    return resid, hidden, pre, bell, saved


def slope_of(pre, bell):
    return bell + pre * (DENSITY * jnp.exp(-0.5 * pre * pre))


def backward(weights, saved, slope, grad, heads):
    proj_w, expand_w, reduce_w = (w[...] for w in weights[1:])
    center, scale, query, keys, values, prob, attended, center_two, scale_two, hidden = saved
    width, tokens = grad.shape
    head = width // heads
    two = 2 * head
    mask = pair_mask(width, head)
    grad_b = grad.astype(BF)
    grad_hidden = dot_tn(reduce_w, grad_b).astype(BF).astype(F32)
    grad_pre = (grad_hidden * slope).astype(BF)
    grad_two = dot(expand_w, grad_pre).astype(BF).astype(F32)
    grad_resid = grad + norm_back(grad_two, center_two, scale_two)
    grad_resid_b = grad_resid.astype(BF)
    grad_att = dot(proj_w, grad_resid_b)
    half = first_half((width, 128))
    tall_half = first_half((heads * 64, 128))
    grad_q, grad_k, grad_v = [], [], []
    grad_bias = jnp.zeros((heads * 64, 128), F32)
    for p in range(tokens // 128):
        lanes = slice(128 * p, 128 * p + 128)
        k = wide_of(keys[:, lanes], mask)
        v = wide_of(values[:, lanes], mask)
        p_f = prob[:, lanes]
        p_b = p_f.astype(BF)
        att = grad_att[:, lanes]
        att_b = att.astype(BF)
        zero = jnp.zeros_like(att)
        att_w = (jnp.where(half, att, zero).astype(BF), jnp.where(half, zero, att).astype(BF))
        query_f = query[:, lanes].astype(F32)
        query_w = (jnp.where(half, query_f, zero).astype(BF), jnp.where(half, zero, query_f).astype(BF))
        first, second = (by_pairs(dot_tn, one, att_b, heads, two, two) for one in v)
        grad_prob = jnp.where(tall_half, first, second)
        grad_prob = grad_prob.astype(BF).astype(F32)
        along = jnp.sum((p_f * grad_prob).reshape(heads, 64, 128), axis=1, keepdims=True)
        grad_score = p_f * (grad_prob.reshape(heads, 64, 128) - along).reshape(heads * 64, 128)
        grad_bias = grad_bias + grad_score
        score_b = grad_score.astype(BF)
        first, second = (by_pairs(dot, one, score_b, heads, two, 128) for one in k)
        grad_q.append(jnp.where(half, first, second))
        for store, lhs, rhs in ((grad_k, query_w, score_b), (grad_v, att_w, p_b)):
            both = []
            for w in range(2):
                folded = jnp.where(mask, by_pairs(dot_nt, lhs[w], rhs, heads, two, 128), 0.0)
                both.append(folded + pltpu.roll(folded, 64, 1))
            store.append(jnp.where(half, both[0], both[1]))
    grad_q = jnp.concatenate(grad_q, axis=1).astype(BF).astype(F32) * head ** (-0.5)
    grad_k = jnp.concatenate(grad_k, axis=1)
    grad_v = jnp.concatenate(grad_v, axis=1)
    grad_mixed = jnp.concatenate([grad_q, grad_k, grad_v], axis=0).astype(BF)
    operands = (center.astype(BF), grad_mixed, attended, grad_resid_b, center_two.astype(BF), grad_pre, hidden, grad_b)
    return grad_resid, operands, grad_bias


def field_grad(qkv_w, grad_mixed, grad_resid, center, scale):
    grad_normed = dot(qkv_w, grad_mixed).astype(BF).astype(F32)
    return grad_resid + norm_back(grad_normed, center, scale)


def pack_grads(operands, ahead, behind, buffer):
    normed, grad_mixed, attended, grad_resid, normed_two, grad_pre, hidden, grad = operands
    width = normed.shape[0]
    qkv = dot_nt(normed, grad_mixed)
    proj = dot_nt(attended, grad_resid)
    expand = dot_nt(normed_two, grad_pre)
    reduce = dot_nt(grad, hidden)
    inner = hidden.shape[0]
    at = 0

    def put(block):
        nonlocal at
        buffer[at : at + block.shape[0], :] = block.astype(BF)
        at += block.shape[0]

    full = 3 * width // 128
    for n in range(full):
        put(qkv[:, 128 * n : 128 * n + 128])
    put(jnp.concatenate([qkv[:, 128 * full :], proj[:, 128:]], axis=1))
    put(proj[:, :128])
    columns = inner // 128
    for n in range(columns // 2):
        put(expand[:, 128 * n : 128 * n + 128])
    half = buffer.shape[0] // 2
    if half > at:
        put(jnp.zeros((half - at, 128), F32))
    for n in range(columns // 2, columns):
        put(expand[:, 128 * n : 128 * n + 128])
    for n in range(columns):
        put(reduce[:, 128 * n : 128 * n + 128])
    heads = ahead.shape[0]
    put(jnp.concatenate([ahead, behind, jnp.zeros((16 - 2 * heads, 128), F32)], axis=0))
    if buffer.shape[0] > at:
        put(jnp.zeros((buffer.shape[0] - at, 128), F32))


class Taker:
    def __init__(self, buffer, factor):
        self.buffer, self.factor, self.at = buffer, factor, 0

    def __call__(self, rows):
        piece = self.buffer[self.at : self.at + rows, :]
        self.at += rows
        return piece.astype(F32) * self.factor


def unpack_first(buffer, qkv, proj, expand, sent, factor):
    take = Taker(buffer, factor)
    width = proj.shape[0]
    full = 3 * width // 128
    for n in range(full):
        qkv[:, 128 * n : 128 * n + 128] = take(width)
    shared = take(width)
    qkv[:, 128 * full :] = shared[:, :64]
    sent(0)
    proj[:, 128:] = shared[:, 64:]
    proj[:, :128] = take(width)
    sent(1)
    for n in range(expand.shape[1] // 128):
        expand[:, 128 * n : 128 * n + 128] = take(width)
    sent(2)


def unpack_second(buffer, expand, reduce, sent, table, block, factor):
    take = Taker(buffer, factor)
    width = reduce.shape[0]
    for which, one in enumerate((expand, reduce)):
        for n in range(one.shape[1] // 128):
            one[:, 128 * n : 128 * n + 128] = take(width)
        sent(which)
    vectors = buffer[take.at : take.at + 16, :]
    heads, _, entries = table.shape
    side = 2 * WIN - 1
    shape = (128, entries)
    rows, lanes = iota(shape, 0), iota(shape, 1)
    down, right = lanes // side - (WIN - 1), lanes % side - (WIN - 1)
    base = 8 * (down + 8) + right
    ahead = ((right >= 0) & (base == rows)).astype(F32).astype(BF)
    behind = ((right < 0) & (base + 8 == rows)).astype(F32).astype(BF)
    table[:, block, :] = (dot(vectors, ahead)[:heads] + dot(vectors, behind)[heads : 2 * heads]) * factor


def tokens_of(read):
    flat = [read(f, c).reshape(64, -1) for f in range(2) for c in range(2)]
    return jnp.concatenate(flat, axis=0).T


def tile_of(field, write):
    natural = field.T
    for f in range(2):
        for c in range(2):
            n = 64 * (2 * f + c)
            write(f, c, natural[n : n + 64].reshape(8, 8, -1))


def corners():
    return [(f, r, 16 * f + 4 * r) for f in range(2) for r in range(4)]


def plain_forward(x_far, cot_far, table_far, *refs):
    far, outs, (first, top, left, corner), (tight, *near), done = refs[:4], refs[4:8], refs[8:12], refs[12:21], refs[21]
    heads = table_far.shape[0]
    qkv_far, *rest = (there.at[0] for there in far)
    pairs = [(x_far, near[0]), (qkv_far, near[1]), *zip(rest, near[2:5], strict=True)]
    pairs[1:1] = [(table_far, near[7])]
    pairs.append((cot_far, near[5]))
    copies = [pltpu.make_async_copy(there, here, done.at[n]) for n, (there, here) in enumerate(pairs)]
    for copy in copies:
        copy.start()
    x_ref, table, qkv, proj, expand, reduce, cot = (
        Late(copy, here) for copy, (_, here) in zip(copies, pairs, strict=True)
    )
    whole = near[6]

    def write(f, c, piece):
        whole[f, :, 8 * c : 8 * c + 8, :] = piece

    def read():
        for one in (x_ref, qkv):
            one.ready()
        return table[:, 0, :]

    bias = spread_bias(read, table_far.shape[2], heads)
    field = tokens_of(lambda f, c: x_ref[f, :, 8 * c : 8 * c + 8, :].astype(F32))
    resid, hidden, _, _, _ = forward((qkv, proj, expand), field, bias, heads)
    tile_of(resid + dot(reduce[...], hidden), write)
    first[...] = whole[:, SHIFT:]
    top[0] = whole[:, :SHIFT].astype(BF)
    top[1] = cot[:, :SHIFT]
    for f, r, n in corners():
        tight[n : n + 4, :] = whole[f, r, :4, :]
        tight[32 + n : 36 + n, :] = cot[f, r, :8, :].astype(F32)[:4]
        tight[64 + n : 68 + n, :] = whole[f, 4 + r, :4, :]
        tight[96 + n : 100 + n, :] = cot[f, 4 + r, :8, :].astype(F32)[:4]
    corner[...] = tight[:64].astype(BF)
    left[...] = tight[64:].astype(BF)
    copies = [pltpu.make_async_copy(here, there, done.at[n]) for n, (here, there) in enumerate(zip((first, top, left, corner), outs, strict=True))]
    for copy in copies:
        copy.start()
    for copy in copies:
        copy.wait()


def keep_plain(n_row, n_col, x_ref, table, qkv, proj, expand, bias_out, slope_out, *outs):
    heads = table.shape[0]
    field = tokens_of(lambda f, c: x_ref[f, :, 8 * c : 8 * c + 8, :].astype(F32))
    _, _, pre, bell, saved = forward((qkv, proj, expand), field, spread_bias(lambda: table[:, 0, :], table.shape[2], heads), heads)
    slope_out[...] = slope_of(pre, bell)
    for ref, value in zip(outs, saved, strict=True):
        ref[...] = value
    last_row = lax.axis_index("row") == n_row - 1
    last_col = lax.axis_index("col") == n_col - 1
    bias_out[...] = spread_bias(lambda: table[:, 1, :], table.shape[2], heads) + shift_mask(bias_out.shape, last_row, last_col)


def shifted_block(
    first, cot, below, across, beside, bias, qkv, proj, expand, reduce,
    own, bottom, right, corner, keep, send, moved, turned, tight, buffer,
):
    heads = bias.shape[0] // 64
    moved[:, :4, :16, :] = first[...]
    moved[:, 4:, :16, :] = below[0].astype(F32)
    turned[:, :4, :16, :] = cot[:, 4:, :, :].astype(F32)
    turned[:, 4:, :16, :] = below[1].astype(F32)
    tight[:64] = across[...].astype(F32)
    tight[64:] = beside[...].astype(F32)
    for f, r, n in corners():
        moved[f, 4 + r, 16:20, :] = tight[n : n + 4, :]
        turned[f, 4 + r, 16:20, :] = tight[32 + n : 36 + n, :]
        moved[f, r, 16:20, :] = tight[64 + n : 68 + n, :]
        turned[f, r, 16:20, :] = tight[96 + n : 100 + n, :]
    field = tokens_of(lambda f, c: moved[f, :, 4 + 8 * c : 12 + 8 * c, :])
    cotangent = tokens_of(lambda f, c: turned[f, :, 4 + 8 * c : 12 + 8 * c, :])
    weights = (qkv, proj, expand, reduce)
    _, _, pre, bell, saved = forward(weights, field, bias[...], heads)
    grad_resid, operands, grad_bias = backward(weights, saved, slope_of(pre, bell), cotangent, heads)
    grad_field = field_grad(qkv[...], operands[1], grad_resid, *saved[:2])

    def write(f, c, piece):
        moved[f, :, 4 + 8 * c : 12 + 8 * c, :] = piece

    tile_of(grad_field, write)
    own[...] = moved[:, :4, :16, :]
    bottom[...] = moved[:, 4:, :16, :].astype(BF)
    for f, r, n in corners():
        tight[n : n + 4, :] = moved[f, 4 + r, 16:20, :]
        tight[32 + n : 36 + n, :] = moved[f, r, 16:20, :]
    corner[...] = tight[:32].astype(BF)
    right[...] = tight[32:64].astype(BF)
    ahead, behind = fold_bias(grad_bias, heads)
    pack_grads(operands, ahead, behind, buffer)
    split_core(buffer, keep, send)


def split_core(buffer, keep, send):
    rows = keep.shape[0]
    core = lax.axis_index("row") % 2
    keep[...] = buffer[pl.ds(pl.multiple_of(core * rows, 16), rows), :]
    send[...] = buffer[pl.ds(pl.multiple_of((1 - core) * rows, 16), rows), :]


def plain_backward(own, above, across, beside, slope, *refs):
    saved, weights = refs[:10], refs[10:14]
    keep, send, mixed_out, resid_out, middle, tight, buffer = refs[14:]
    heads = saved[5].shape[0] // 64
    middle[:, 4:] = own[...]
    middle[:, :4] = above[...].astype(F32)
    tight[:32] = across[...].astype(F32)
    tight[32:64] = beside[...].astype(F32)
    for f, r, n in corners():
        middle[f, r, :4, :] = tight[n : n + 4, :]
        middle[f, 4 + r, :4, :] = tight[32 + n : 36 + n, :]
    cotangent = tokens_of(lambda f, c: middle[f, :, 8 * c : 8 * c + 8, :])
    saved = tuple(ref[...] for ref in saved)
    grad_resid, operands, grad_bias = backward(weights, saved, slope[...], cotangent, heads)
    mixed_out[...] = operands[1]
    resid_out[...] = grad_resid
    ahead, behind = fold_bias(grad_bias, heads)
    pack_grads(operands, ahead, behind, buffer)
    split_core(buffer, keep, send)


def plain_field(mixed, resid, center, scale, qkv, out):
    grad_field = field_grad(qkv[...], mixed[...], resid[...], center[...], scale[...])

    def write(f, c, piece):
        out[f, :, 8 * c : 8 * c + 8, :] = piece

    tile_of(grad_field, write)


def near_place():
    return lax.axis_index("row") // 2 * 2 + lax.axis_index("col") % 2


def cut(total, me, own, sends, partners, here=slice(None)):
    rows = total.shape[0] // (len(sends) + 1)
    own[here, :] = total[pl.ds(pl.multiple_of(me * rows, 16), rows), :]
    for d, send in zip(partners, sends, strict=True):
        send[here, :] = total[pl.ds(pl.multiple_of((me ^ d) * rows, 16), rows), :].astype(BF)


def add_core(keep, came, own, *rest):
    sends, total = rest[:-1], rest[-1]
    total[...] = keep[...].astype(F32) + came[...].astype(F32)
    cut(total, near_place(), own, sends, (1, 2, 3))


def sum_near(mine, one, two, three, out):
    out[...] = mine[...] + one[...].astype(F32) + two[...].astype(F32) + three[...].astype(F32)


def add_core_later(keep, came, other, *rest):
    add_core(keep, came, *rest)


def add_near(count, mine, one, two, three, other, own, *rest):
    sends, total = rest[: count - 1], rest[-1]
    rows = own.shape[0] // 2
    place = lax.axis_index("col") // 2
    partners = range(count - 1, 0, -1)
    sum_near(mine, one, two, three, total)
    cut(total, place, own, sends, partners, slice(0, rows))
    cut(other, place, own, sends, partners, slice(rows, 2 * rows))


def add_far(*refs):
    ins, out = refs[:-1], refs[-1]
    out[...] = (ins[0][...] + sum(one[...].astype(F32) for one in ins[1:])).astype(BF)


def join_far(*refs):
    ins, out = refs[:-1], refs[-1]
    rows, length = ins[0].shape[0] // 2, out.shape[0] // 2
    me = lax.axis_index("col") // 2
    for d, piece in enumerate(ins):
        for block in range(2):
            there = pl.multiple_of(block * length + (me ^ d) * rows, 16)
            out[pl.ds(there, rows), :] = piece[block * rows : block * rows + rows, :]


def finish(other, factor, *refs):
    ins, refs = refs[:4], refs[4 + 5 * other :]
    outs, buffer, done, (qkv, proj, expand, reduce, table) = refs[:5], refs[5], refs[6], refs[7:12]
    rows = ins[0].shape[0] // 2
    me = near_place()
    for block in range(2):
        for d, piece in enumerate(ins):
            there = pl.multiple_of((me ^ d) * rows, 16)
            buffer[block, pl.ds(there, rows), :] = piece[block * rows : block * rows + rows, :]
    half = (lax.axis_index("row") + other) % 2
    columns = expand.shape[2]
    copies = []

    def copy(here, there):
        copies.append(pltpu.make_async_copy(here, there, done.at[len(copies)]))
        copies[-1].start()

    @pl.when(half == 0)
    def _():
        copies.clear()
        for block in range(2):
            pairs = [
                (qkv.at[block], outs[0].at[block]),
                (proj.at[block], outs[1].at[block]),
                (expand.at[block], outs[2].at[block, :, pl.ds(0, columns)]),
            ]
            sent = lambda n, pairs=pairs: copy(*pairs[n])
            unpack_first(buffer.at[block], qkv.at[block], proj.at[block], expand.at[block], sent, factor)
        for one in copies:
            one.wait()

    @pl.when(half == 1)
    def _():
        copies.clear()
        for block in range(2):
            pairs = [
                (expand.at[block], outs[2].at[block, :, pl.ds(columns, columns)]),
                (reduce.at[block], outs[3].at[block]),
            ]
            sent = lambda n, pairs=pairs: copy(*pairs[n])
            unpack_second(buffer.at[block], expand.at[block], reduce.at[block], sent, table, block, factor)
        copy(table, outs[4])
        for one in copies:
            one.wait()


class Whole:
    def __init__(self, ref, block):
        self.ref, self.block = ref, block

    def __getitem__(self, index):
        return self.ref[self.block]


def call(kernel, outs, scratch, args, stacked=(), distant=(), micros=0.5, limit=LIMIT, far_outs=0, aliases=None):
    here, there = pl.BlockSpec(memory_space=pltpu.VMEM), pl.BlockSpec(memory_space=pltpu.HBM)
    count = len(args)

    def body(*refs):
        weights = [Whole(ref, block) for ref, (_, block) in zip(refs[count:], stacked)]
        kernel(*refs[:count], *weights, *refs[count + len(stacked) :])

    return pl.pallas_call(
        body,
        in_specs=[here] * (count + len(stacked)) + [there] * len(distant),
        out_specs=[there] * far_outs + [here] * (len(outs) - far_outs),
        out_shape=[jax.ShapeDtypeStruct(s, d) for s, d in outs],
        scratch_shapes=[pltpu.VMEM(*one) if isinstance(one, tuple) else one for one in scratch],
        input_output_aliases=aliases or {},
        compiler_params=pltpu.CompilerParams(vmem_limit_bytes=limit),
        cost_estimate=pl.CostEstimate(flops=int(micros * 1.1e9), bytes_accessed=0, transcendentals=0),
    )(*args, *(arg for arg, _ in stacked), *distant)


def local(block_input, cotangent, qkv_weight, proj_weight, expand_weight, reduce_weight, bias_table):
    frames, rows, cols, width = block_input.shape
    n_row, n_col = lax.axis_size("row"), lax.axis_size("col")
    inner = expand_weight.shape[2]
    heads = bias_table.shape[1]
    tokens = frames * rows * cols
    wide = jnp.swapaxes(reduce_weight, 1, 2)
    weights = (qkv_weight, proj_weight, expand_weight, wide)
    table = jnp.swapaxes(bias_table, 0, 1)
    axes = ("row", "col")

    def send(block, down, right):
        route = [
            (r * n_col + c, (r + down) % n_row * n_col + (c + right) % n_col)
            for r in range(n_row)
            for c in range(n_col)
        ]
        return lax.ppermute(block, axes, route)

    def swap(block, row_bits, col_bits):
        route = [
            (r * n_col + c, (r ^ row_bits) * n_col + (c ^ col_bits)) for r in range(n_row) for c in range(n_col)
        ]
        return lax.ppermute(block, axes, route)

    far = n_col // 2
    unit = 8 * far * 16
    used = (4 * width + 2 * inner) * width // 128 + 2 * 16
    size = -(-used // unit) * unit
    chunk = size // (8 * far)
    halves = [((size // 2, 128), BF)] * 2
    buffer = ((size, 128), BF)
    tile = (frames, rows, cols, width)
    strip = (frames, SHIFT, cols, width)
    patches = frames * SHIFT * SHIFT
    tight = ((4 * patches, width), F32)
    lines = ((heads * 64, 128), F32)
    sent = [(strip, F32), ((2, *strip), BF), ((2 * patches, width), BF), ((2 * patches, width), BF)]
    first, top, left, corner = call(
        plain_forward,
        sent,
        [*sent, tight, (tile, BF), *((w.shape[1:], BF) for w in weights), (tile, BF), (tile, F32), (table.shape, F32), pltpu.SemaphoreType.DMA((7,))],
        [],
        distant=(block_input, cotangent, table, *weights),
        micros=2.3,
        limit=FULL,
        far_outs=4,
    )
    halo = [send(top, -1, 0), send(corner, -1, -1), send(left, 0, -1)]
    bias, *kept = call(
        functools.partial(keep_plain, n_row, n_col),
        [
            lines,
            ((inner, tokens), F32),
            ((width, tokens), F32),
            ((1, tokens), F32),
            ((width, tokens), BF),
            ((width, tokens), BF),
            ((width, tokens), BF),
            ((heads * 64, tokens), F32),
            ((width, tokens), BF),
            ((width, tokens), F32),
            ((1, tokens), F32),
            ((inner, tokens), BF),
        ],
        [],
        [block_input, table],
        [(w, 0) for w in weights[:3]],
        micros=2.3,
    )
    own, bottom, right, corner, keep, away = call(
        shifted_block,
        [(strip, F32), (strip, BF), ((patches, width), BF), ((patches, width), BF), *halves],
        [((frames, rows, cols + 8, width), F32)] * 2 + [tight, buffer],
        [first, cotangent, *halo, bias],
        [(w, 1) for w in weights],
        micros=4.8,
    )
    back = [own, send(bottom, 1, 0), send(corner, 1, 1), send(right, 0, 1)]

    eighth, quarter, piece = (size // 8, 128), (size // 4, 128), (2 * chunk, 128)

    def near(own, *sends):
        came = [swap(one, d & 2, d & 1) for d, one in reversed(list(enumerate(sends, 1)))]
        return [own] + came[::-1]

    quarters = [(eighth, F32)] + [(eighth, BF)] * 3
    summed = [((size // 2, 128), F32)]
    shifted = call(add_core, quarters, summed, [keep, swap(away, 1, 0)])
    kept[0], *shifted = lax.optimization_barrier((kept[0], *shifted))
    (other,) = call(sum_near, [(eighth, F32)], [], near(*shifted), micros=4.0)
    keep, away, mixed, resid = call(
        plain_backward,
        [*halves, ((3 * width, tokens), BF), ((width, tokens), F32)],
        [(tile, F32), tight, buffer],
        [*back, *kept],
        [(w, 0) for w in weights],
        micros=3.0,
    )
    (input_grad,) = call(
        plain_field, [(tile, F32)], [], [mixed, resid, kept[1], kept[2]], [(qkv_weight, 0)], micros=1.0
    )
    plain = near(*call(add_core_later, quarters, summed, [keep, swap(away, 1, 0), other]))
    plain[0], input_grad = lax.optimization_barrier((plain[0], input_grad))
    own, *sends = call(
        functools.partial(add_near, far),
        [(piece, F32)] + [(piece, BF)] * (far - 1),
        [(eighth, F32)],
        [*plain, other],
    )
    distant = [own] + [swap(one, 0, 2 * d) for d, one in zip(range(far - 1, 0, -1), sends, strict=True)]
    (done,) = call(add_far, [(piece, BF)], [], distant)
    distant = [done] + [swap(done, 0, 2 * d) for d in range(1, far)]
    (joined,) = call(join_far, [(quarter, BF)], [], distant)
    near = [joined] + [swap(joined, d & 2, d & 1) for d in range(1, 4)]
    factor = 1.0 / math.sqrt(frames * rows * n_row * cols * n_col)
    shapes = [(w.shape, F32) for w in (*weights, table)]
    stage = [((2, size // 2, 128), BF), pltpu.SemaphoreType.DMA((6,)), *shapes]
    stage[4] = ((2, width, inner // 2), F32)
    grads = call(functools.partial(finish, 0, factor), shapes, stage, near, far_outs=5, micros=1.2)
    qkv, proj, expand, reduce, table = call(
        functools.partial(finish, 1, factor),
        shapes,
        stage,
        [swap(one, 1, 0) for one in near],
        distant=grads,
        far_outs=5,
        aliases={4 + n: n for n in range(5)},
        micros=1.2,
    )
    return input_grad, qkv, proj, expand, jnp.swapaxes(reduce, 1, 2), jnp.swapaxes(table, 0, 1)


def solution(mesh):
    in_specs = (P(None, "row", "col", None), P(None, "row", "col", None), P(), P(), P(), P(), P())
    out_specs = (P(None, "row", "col", None), P(), P(), P(), P(), P())
    return jax.shard_map(local, mesh=mesh, in_specs=in_specs, out_specs=out_specs, check_vma=False)
```

```python
import functools
import math

import jax
import jax.numpy as jnp
from jax import lax
from jax.experimental import pallas as pl
from jax.experimental.pallas import tpu as pltpu
from jax.sharding import PartitionSpec as P

WIN = 8
SHIFT = 4
BF = jnp.bfloat16
F32 = jnp.float32
LIMIT = 48 * 1024 * 1024
FULL = 62 * 1024 * 1024
ROOT_HALF = 0.7071067811865476
DENSITY = 0.3989422804014327


def dot(a, b):
    return lax.dot_general(a, b, (((1,), (0,)), ((), ())), preferred_element_type=F32)


def dot_nt(a, b):
    return lax.dot_general(a, b, (((1,), (1,)), ((), ())), preferred_element_type=F32)


def dot_tn(a, b):
    return lax.dot_general(a, b, (((0,), (0,)), ((), ())), preferred_element_type=F32)


def iota(shape, axis):
    return lax.broadcasted_iota(jnp.int32, shape, axis)


def norm(field):
    center = field - jnp.mean(field, axis=0, keepdims=True)
    spread = jnp.mean(center * center, axis=0, keepdims=True)
    scale = lax.rsqrt(spread + 1e-05)
    return center * scale, scale


def norm_back(grad, normed, scale):
    along = jnp.mean(grad * normed, axis=0, keepdims=True)
    return scale * (grad - jnp.mean(grad, axis=0, keepdims=True) - normed * along)


class Late:
    def __init__(self, copy, here):
        self.copy, self.here = copy, here

    def ready(self):
        if self.copy is not None:
            self.copy.wait()
            self.copy = None

    def __getitem__(self, index):
        self.ready()
        return self.here[index]


def first_half(shape):
    return iota(shape, 1) < 64


def pair_mask(rows, head):
    return (iota((rows, 128), 0) // head) % 2 == iota((rows, 128), 1) // 64


def spread_bias(read, entries, heads):
    side = 2 * WIN - 1
    lanes = iota((entries, 256), 1)
    rows = iota((entries, 256), 0)
    place = lanes % 128
    down = place // 8 - 8
    right = place % 8 - jnp.where(lanes >= 128, 8, 0)
    wanted = (down + WIN - 1) * side + right + WIN - 1
    fits = (down >= 1 - WIN) & (right >= 1 - WIN)
    pick = (fits & (wanted == rows)).astype(F32)
    vectors = lax.dot_general(
        read(), pick, (((1,), (0,)), ((), ())), precision=lax.Precision.HIGHEST, preferred_element_type=F32
    )
    ahead = jnp.broadcast_to(vectors[:, None, :128], (heads, 8, 128)).reshape(heads * 8, 128)
    behind = jnp.broadcast_to(vectors[:, None, 128:], (heads, 8, 128)).reshape(heads * 8, 128)
    shape = (heads * 8, 128)
    col_j = iota(shape, 0) % 8
    col_i = iota(shape, 1) % 8
    built = jnp.zeros(shape, F32)
    for c in range(8):
        line = jnp.where(col_i >= c, pltpu.roll(ahead, 64 + c, 1), pltpu.roll(behind, 56 + c, 1))
        built = jnp.where(col_j == c, line, built)
    rolled = [built] + [pltpu.roll(built, 8 * r, 1) for r in range(1, 8)]
    rolled = [jnp.where(first_half(shape), one, pltpu.roll(one, 64, 1)) for one in rolled]
    parts = []
    for h in range(heads):
        for r in range(8):
            parts.append(rolled[r][8 * h : 8 * h + 8])
    return jnp.concatenate(parts, axis=0)


def fold_bias(grad, heads):
    folded = jnp.where(first_half(grad.shape), grad + pltpu.roll(grad, 64, 1), 0.0)
    split = folded.reshape(heads, 8, 8, 128)
    total = jnp.zeros((heads * 8, 128), F32)
    for r in range(8):
        piece = split[:, r].reshape(heads * 8, 128)
        total = total + pltpu.roll(piece, 64 - 8 * r, 1)
    shape = (heads * 8, 128)
    col_j = iota(shape, 0) % 8
    col_i = iota(shape, 1) % 8
    ahead = jnp.zeros(shape, F32)
    behind = jnp.zeros(shape, F32)
    for c in range(8):
        mine = jnp.where((col_j == c) & (col_i >= c), total, 0.0)
        ahead = ahead + (pltpu.roll(mine, 128 - c, 1) if c else mine)
        rest = jnp.where((col_j == c) & (col_i < c), total, 0.0)
        behind = behind + pltpu.roll(rest, 8 - c, 1)
    ahead = jnp.sum(ahead.reshape(heads, 8, 128), axis=1)
    behind = jnp.sum(behind.reshape(heads, 8, 128), axis=1)
    return ahead, behind


def shift_mask(shape, last_row, last_col):
    j = iota(shape, 0) % 64
    lane = iota(shape, 1)
    i = lane % 64
    low = (j // 8 >= SHIFT) != (i // 8 >= SHIFT)
    side = (j % 8 >= SHIFT) != (i % 8 >= SHIFT)
    differ = (low & last_row) | (side & (lane >= 64) & last_col)
    return jnp.where(differ, -10000.0, 0.0)


def wide_of(field, mask):
    field = field.astype(F32)
    half = first_half(field.shape)
    swapped = pltpu.roll(field, 64, 1)
    return [
        jnp.where(mask, one, 0.0).astype(BF) for one in (jnp.where(half, field, swapped), jnp.where(half, swapped, field))
    ]


def by_pairs(product, lhs, rhs, heads, left, right):
    return jnp.concatenate(
        [
            product(lhs[left * n : left * n + left], rhs[right * n : right * n + right])
            for n in range(heads // 2)
        ],
        axis=0,
    )


def forward(weights, field, bias, heads):
    width, tokens = field.shape
    head = width // heads
    two = 2 * head
    mask = pair_mask(width, head)
    center, scale = norm(field)
    normed = center.astype(BF)
    mixed = dot_tn(weights[0][...], normed)
    query = (mixed[:width] * head ** (-0.5)).astype(BF)
    keys = mixed[width : 2 * width].astype(BF)
    values = mixed[2 * width :].astype(BF)
    probs, attended = [], []
    half = first_half((width, 128))
    tall_half = first_half((heads * 64, 128))
    for p in range(tokens // 128):
        lanes = slice(128 * p, 128 * p + 128)
        k = wide_of(mixed[width : 2 * width, lanes], mask)
        v = wide_of(mixed[2 * width :, lanes], mask)
        q = query[:, lanes]
        first, second = (by_pairs(dot_tn, one, q, heads, two, two) for one in k)
        scores = jnp.where(tall_half, first, second) + bias
        scores = scores.reshape(heads, 64, 128)
        expos = jnp.exp(scores - jnp.max(scores, axis=1, keepdims=True))
        prob = (expos / jnp.sum(expos, axis=1, keepdims=True)).reshape(heads * 64, 128)
        prob_b = prob.astype(BF)
        first, second = (by_pairs(dot, one, prob_b, heads, two, 128) for one in v)
        attended.append(jnp.where(half, first, second))
        probs.append(prob)
    attended = jnp.concatenate(attended, axis=1).astype(BF)
    prob = jnp.concatenate(probs, axis=1)
    resid = field + dot_tn(weights[1][...], attended)
    center_two, scale_two = norm(resid)
    normed_two = center_two.astype(BF)
    pre = dot_tn(weights[2][...], normed_two)
    bell = 0.5 * (1.0 + lax.erf(pre * ROOT_HALF))
    hidden = (pre * bell).astype(BF)
    saved = (center, scale, query, keys, values, prob, attended, center_two, scale_two, hidden)
    return resid, hidden, pre, bell, saved


def slope_of(pre, bell):
    return bell + pre * (DENSITY * jnp.exp(-0.5 * pre * pre))


def backward(weights, saved, slope, grad, heads):
    proj_w, expand_w, reduce_w = (w[...] for w in weights[1:])
    center, scale, query, keys, values, prob, attended, center_two, scale_two, hidden = saved
    width, tokens = grad.shape
    head = width // heads
    two = 2 * head
    mask = pair_mask(width, head)
    grad_b = grad.astype(BF)
    grad_hidden = dot_tn(reduce_w, grad_b).astype(BF).astype(F32)
    grad_pre = (grad_hidden * slope).astype(BF)
    grad_two = dot(expand_w, grad_pre).astype(BF).astype(F32)
    grad_resid = grad + norm_back(grad_two, center_two, scale_two)
    grad_resid_b = grad_resid.astype(BF)
    grad_att = dot(proj_w, grad_resid_b)
    half = first_half((width, 128))
    tall_half = first_half((heads * 64, 128))
    grad_q, grad_k, grad_v = [], [], []
    grad_bias = jnp.zeros((heads * 64, 128), F32)
    for p in range(tokens // 128):
        lanes = slice(128 * p, 128 * p + 128)
        k = wide_of(keys[:, lanes], mask)
        v = wide_of(values[:, lanes], mask)
        p_f = prob[:, lanes]
        p_b = p_f.astype(BF)
        att = grad_att[:, lanes]
        att_b = att.astype(BF)
        zero = jnp.zeros_like(att)
        att_w = (jnp.where(half, att, zero).astype(BF), jnp.where(half, zero, att).astype(BF))
        query_f = query[:, lanes].astype(F32)
        query_w = (jnp.where(half, query_f, zero).astype(BF), jnp.where(half, zero, query_f).astype(BF))
        first, second = (by_pairs(dot_tn, one, att_b, heads, two, two) for one in v)
        grad_prob = jnp.where(tall_half, first, second)
        grad_prob = grad_prob.astype(BF).astype(F32)
        along = jnp.sum((p_f * grad_prob).reshape(heads, 64, 128), axis=1, keepdims=True)
        grad_score = p_f * (grad_prob.reshape(heads, 64, 128) - along).reshape(heads * 64, 128)
        grad_bias = grad_bias + grad_score
        score_b = grad_score.astype(BF)
        first, second = (by_pairs(dot, one, score_b, heads, two, 128) for one in k)
        grad_q.append(jnp.where(half, first, second))
        for store, lhs, rhs in ((grad_k, query_w, score_b), (grad_v, att_w, p_b)):
            both = []
            for w in range(2):
                folded = jnp.where(mask, by_pairs(dot_nt, lhs[w], rhs, heads, two, 128), 0.0)
                both.append(folded + pltpu.roll(folded, 64, 1))
            store.append(jnp.where(half, both[0], both[1]))
    grad_q = jnp.concatenate(grad_q, axis=1).astype(BF).astype(F32) * head ** (-0.5)
    grad_k = jnp.concatenate(grad_k, axis=1)
    grad_v = jnp.concatenate(grad_v, axis=1)
    grad_mixed = jnp.concatenate([grad_q, grad_k, grad_v], axis=0).astype(BF)
    operands = (center.astype(BF), grad_mixed, attended, grad_resid_b, center_two.astype(BF), grad_pre, hidden, grad_b)
    return grad_resid, operands, grad_bias


def field_grad(qkv_w, grad_mixed, grad_resid, center, scale):
    grad_normed = dot(qkv_w, grad_mixed).astype(BF).astype(F32)
    return grad_resid + norm_back(grad_normed, center, scale)


def pack_grads(operands, ahead, behind, buffer):
    normed, grad_mixed, attended, grad_resid, normed_two, grad_pre, hidden, grad = operands
    width = normed.shape[0]
    qkv = dot_nt(normed, grad_mixed)
    proj = dot_nt(attended, grad_resid)
    expand = dot_nt(normed_two, grad_pre)
    reduce = dot_nt(grad, hidden)
    inner = hidden.shape[0]
    at = 0

    def put(block):
        nonlocal at
        buffer[at : at + block.shape[0], :] = block.astype(BF)
        at += block.shape[0]

    full = 3 * width // 128
    for n in range(full):
        put(qkv[:, 128 * n : 128 * n + 128])
    put(jnp.concatenate([qkv[:, 128 * full :], proj[:, 128:]], axis=1))
    put(proj[:, :128])
    columns = inner // 128
    for n in range(columns // 2):
        put(expand[:, 128 * n : 128 * n + 128])
    half = buffer.shape[0] // 2
    if half > at:
        put(jnp.zeros((half - at, 128), F32))
    for n in range(columns // 2, columns):
        put(expand[:, 128 * n : 128 * n + 128])
    for n in range(columns):
        put(reduce[:, 128 * n : 128 * n + 128])
    heads = ahead.shape[0]
    put(jnp.concatenate([ahead, behind, jnp.zeros((16 - 2 * heads, 128), F32)], axis=0))
    if buffer.shape[0] > at:
        put(jnp.zeros((buffer.shape[0] - at, 128), F32))


class Taker:
    def __init__(self, buffer, factor):
        self.buffer, self.factor, self.at = buffer, factor, 0

    def __call__(self, rows):
        piece = self.buffer[self.at : self.at + rows, :]
        self.at += rows
        return piece.astype(F32) * self.factor


def unpack_first(buffer, qkv, proj, expand, sent, factor):
    take = Taker(buffer, factor)
    width = proj.shape[0]
    full = 3 * width // 128
    for n in range(full):
        qkv[:, 128 * n : 128 * n + 128] = take(width)
    shared = take(width)
    qkv[:, 128 * full :] = shared[:, :64]
    sent(0)
    proj[:, 128:] = shared[:, 64:]
    proj[:, :128] = take(width)
    sent(1)
    for n in range(expand.shape[1] // 128):
        expand[:, 128 * n : 128 * n + 128] = take(width)
    sent(2)


def unpack_second(buffer, expand, reduce, sent, table, block, factor):
    take = Taker(buffer, factor)
    width = reduce.shape[0]
    for which, one in ((1, reduce), (0, expand)):
        take.at = which * expand.shape[1] // 128 * width
        for n in range(one.shape[1] // 128):
            one[:, 128 * n : 128 * n + 128] = take(width)
        sent(which)
    at = (expand.shape[1] + reduce.shape[1]) // 128 * width
    vectors = buffer[at : at + 16, :]
    heads, _, entries = table.shape
    side = 2 * WIN - 1
    shape = (128, entries)
    rows, lanes = iota(shape, 0), iota(shape, 1)
    down, right = lanes // side - (WIN - 1), lanes % side - (WIN - 1)
    base = 8 * (down + 8) + right
    ahead = ((right >= 0) & (base == rows)).astype(F32).astype(BF)
    behind = ((right < 0) & (base + 8 == rows)).astype(F32).astype(BF)
    table[:, block, :] = (dot(vectors, ahead)[:heads] + dot(vectors, behind)[heads : 2 * heads]) * factor


def tokens_of(read):
    flat = [read(f, c).reshape(64, -1) for f in range(2) for c in range(2)]
    return jnp.concatenate(flat, axis=0).T


def tile_of(field, write):
    natural = field.T
    for f in range(2):
        for c in range(2):
            n = 64 * (2 * f + c)
            write(f, c, natural[n : n + 64].reshape(8, 8, -1))


def corners():
    return [(f, r, 16 * f + 4 * r) for f in range(2) for r in range(4)]


def plain_forward(x_far, cot_far, table_far, *refs):
    far, outs, (first, top, left, corner), (tight, *near), done = refs[:4], refs[4:8], refs[8:12], refs[12:21], refs[21]
    heads = table_far.shape[0]
    qkv_far, *rest = (there.at[0] for there in far)
    pairs = [(x_far, near[0]), (qkv_far, near[1]), *zip(rest, near[2:5], strict=True)]
    pairs[1:1] = [(table_far, near[7])]
    pairs.append((cot_far, near[5]))
    copies = [pltpu.make_async_copy(there, here, done.at[n]) for n, (there, here) in enumerate(pairs)]
    for copy in copies:
        copy.start()
    x_ref, table, qkv, proj, expand, reduce, cot = (
        Late(copy, here) for copy, (_, here) in zip(copies, pairs, strict=True)
    )
    whole = near[6]

    def write(f, c, piece):
        whole[f, :, 8 * c : 8 * c + 8, :] = piece

    def read():
        for one in (x_ref, qkv):
            one.ready()
        return table[:, 0, :]

    bias = spread_bias(read, table_far.shape[2], heads)
    field = tokens_of(lambda f, c: x_ref[f, :, 8 * c : 8 * c + 8, :].astype(F32))
    resid, hidden, _, _, _ = forward((qkv, proj, expand), field, bias, heads)
    tile_of(resid + dot(reduce[...], hidden), write)
    first[...] = whole[:, SHIFT:]
    top[0] = whole[:, :SHIFT].astype(BF)
    top[1] = cot[:, :SHIFT]
    for f, r, n in corners():
        tight[n : n + 4, :] = whole[f, r, :4, :]
        tight[32 + n : 36 + n, :] = cot[f, r, :8, :].astype(F32)[:4]
        tight[64 + n : 68 + n, :] = whole[f, 4 + r, :4, :]
        tight[96 + n : 100 + n, :] = cot[f, 4 + r, :8, :].astype(F32)[:4]
    corner[...] = tight[:64].astype(BF)
    left[...] = tight[64:].astype(BF)
    copies = [pltpu.make_async_copy(here, there, done.at[n]) for n, (here, there) in enumerate(zip((first, top, left, corner), outs, strict=True))]
    for copy in copies:
        copy.start()
    for copy in copies:
        copy.wait()


def keep_plain(n_row, n_col, x_ref, table, qkv, proj, expand, bias_out, slope_out, *outs):
    heads = table.shape[0]
    field = tokens_of(lambda f, c: x_ref[f, :, 8 * c : 8 * c + 8, :].astype(F32))
    _, _, pre, bell, saved = forward((qkv, proj, expand), field, spread_bias(lambda: table[:, 0, :], table.shape[2], heads), heads)
    slope_out[...] = slope_of(pre, bell)
    for ref, value in zip(outs, saved, strict=True):
        ref[...] = value
    last_row = lax.axis_index("row") == n_row - 1
    last_col = lax.axis_index("col") == n_col - 1
    bias_out[...] = spread_bias(lambda: table[:, 1, :], table.shape[2], heads) + shift_mask(bias_out.shape, last_row, last_col)


def shifted_block(
    first, cot, below, across, beside, bias, qkv, proj, expand, reduce,
    own, bottom, right, corner, keep, send, moved, turned, tight, buffer,
):
    heads = bias.shape[0] // 64
    moved[:, :4, :16, :] = first[...]
    moved[:, 4:, :16, :] = below[0].astype(F32)
    turned[:, :4, :16, :] = cot[:, 4:, :, :].astype(F32)
    turned[:, 4:, :16, :] = below[1].astype(F32)
    tight[:64] = across[...].astype(F32)
    tight[64:] = beside[...].astype(F32)
    for f, r, n in corners():
        moved[f, 4 + r, 16:20, :] = tight[n : n + 4, :]
        turned[f, 4 + r, 16:20, :] = tight[32 + n : 36 + n, :]
        moved[f, r, 16:20, :] = tight[64 + n : 68 + n, :]
        turned[f, r, 16:20, :] = tight[96 + n : 100 + n, :]
    field = tokens_of(lambda f, c: moved[f, :, 4 + 8 * c : 12 + 8 * c, :])
    cotangent = tokens_of(lambda f, c: turned[f, :, 4 + 8 * c : 12 + 8 * c, :])
    weights = (qkv, proj, expand, reduce)
    _, _, pre, bell, saved = forward(weights, field, bias[...], heads)
    grad_resid, operands, grad_bias = backward(weights, saved, slope_of(pre, bell), cotangent, heads)
    grad_field = field_grad(qkv[...], operands[1], grad_resid, *saved[:2])

    def write(f, c, piece):
        moved[f, :, 4 + 8 * c : 12 + 8 * c, :] = piece

    tile_of(grad_field, write)
    own[...] = moved[:, :4, :16, :]
    bottom[...] = moved[:, 4:, :16, :].astype(BF)
    for f, r, n in corners():
        tight[n : n + 4, :] = moved[f, 4 + r, 16:20, :]
        tight[32 + n : 36 + n, :] = moved[f, r, 16:20, :]
    corner[...] = tight[:32].astype(BF)
    right[...] = tight[32:64].astype(BF)
    ahead, behind = fold_bias(grad_bias, heads)
    pack_grads(operands, ahead, behind, buffer)
    split_core(buffer, keep, send)


def split_core(buffer, keep, send):
    rows = keep.shape[0]
    core = lax.axis_index("row") % 2
    keep[...] = buffer[pl.ds(pl.multiple_of(core * rows, 16), rows), :]
    send[...] = buffer[pl.ds(pl.multiple_of((1 - core) * rows, 16), rows), :]


def plain_backward(own, above, across, beside, slope, *refs):
    saved, weights = refs[:10], refs[10:14]
    keep, send, mixed_out, resid_out, middle, tight, buffer = refs[14:]
    heads = saved[5].shape[0] // 64
    middle[:, 4:] = own[...]
    middle[:, :4] = above[...].astype(F32)
    tight[:32] = across[...].astype(F32)
    tight[32:64] = beside[...].astype(F32)
    for f, r, n in corners():
        middle[f, r, :4, :] = tight[n : n + 4, :]
        middle[f, 4 + r, :4, :] = tight[32 + n : 36 + n, :]
    cotangent = tokens_of(lambda f, c: middle[f, :, 8 * c : 8 * c + 8, :])
    saved = tuple(ref[...] for ref in saved)
    grad_resid, operands, grad_bias = backward(weights, saved, slope[...], cotangent, heads)
    mixed_out[...] = operands[1]
    resid_out[...] = grad_resid
    ahead, behind = fold_bias(grad_bias, heads)
    pack_grads(operands, ahead, behind, buffer)
    split_core(buffer, keep, send)


def plain_field(mixed, resid, center, scale, qkv, out):
    grad_field = field_grad(qkv[...], mixed[...], resid[...], center[...], scale[...])

    def write(f, c, piece):
        out[f, :, 8 * c : 8 * c + 8, :] = piece

    tile_of(grad_field, write)


def near_place():
    return lax.axis_index("row") // 2 * 2 + lax.axis_index("col") % 2


def cut(total, me, own, sends, partners, here=slice(None)):
    rows = total.shape[0] // (len(sends) + 1)
    own[here, :] = total[pl.ds(pl.multiple_of(me * rows, 16), rows), :]
    for d, send in zip(partners, sends, strict=True):
        send[here, :] = total[pl.ds(pl.multiple_of((me ^ d) * rows, 16), rows), :].astype(BF)


def add_core(keep, came, own, *rest):
    sends, total = rest[:-1], rest[-1]
    total[...] = keep[...].astype(F32) + came[...].astype(F32)
    cut(total, near_place(), own, sends, (1, 2, 3))


def sum_near(mine, one, two, three, out):
    out[...] = mine[...] + one[...].astype(F32) + two[...].astype(F32) + three[...].astype(F32)


def add_core_later(keep, came, other, *rest):
    add_core(keep, came, *rest)


def add_near(count, mine, one, two, three, other, own, *rest):
    sends, total = rest[: count - 1], rest[-1]
    rows = own.shape[0] // 2
    place = lax.axis_index("col") // 2
    partners = range(count - 1, 0, -1)
    sum_near(mine, one, two, three, total)
    cut(total, place, own, sends, partners, slice(0, rows))
    cut(other, place, own, sends, partners, slice(rows, 2 * rows))


def add_far(*refs):
    ins, out = refs[:-1], refs[-1]
    out[...] = (ins[0][...] + sum(one[...].astype(F32) for one in ins[1:])).astype(BF)


def join_far(*refs):
    ins, out = refs[:-1], refs[-1]
    rows, length = ins[0].shape[0] // 2, out.shape[0] // 2
    me = lax.axis_index("col") // 2
    for d, piece in enumerate(ins):
        for block in range(2):
            there = pl.multiple_of(block * length + (me ^ d) * rows, 16)
            out[pl.ds(there, rows), :] = piece[block * rows : block * rows + rows, :]


def finish(other, factor, *refs):
    ins, refs = refs[:4], refs[4 + 5 * other :]
    outs, buffer, done, (qkv, proj, expand, reduce, table) = refs[:5], refs[5], refs[6], refs[7:12]
    rows = ins[0].shape[0] // 2
    me = near_place()
    for block in range(2):
        for d, piece in enumerate(ins):
            there = pl.multiple_of((me ^ d) * rows, 16)
            buffer[block, pl.ds(there, rows), :] = piece[block * rows : block * rows + rows, :]
    half = (lax.axis_index("row") + other) % 2
    columns = expand.shape[2]
    copies = []

    def copy(here, there):
        copies.append(pltpu.make_async_copy(here, there, done.at[len(copies)]))
        copies[-1].start()

    @pl.when(half == 0)
    def _():
        copies.clear()
        for block in range(2):
            pairs = [
                (qkv.at[block], outs[0].at[block]),
                (proj.at[block], outs[1].at[block]),
                (expand.at[block], outs[2].at[block, :, pl.ds(0, columns)]),
            ]
            sent = lambda n, pairs=pairs: copy(*pairs[n])
            unpack_first(buffer.at[block], qkv.at[block], proj.at[block], expand.at[block], sent, factor)
        for one in copies:
            one.wait()

    @pl.when(half == 1)
    def _():
        copies.clear()
        for block in range(2):
            pairs = [
                (expand.at[block], outs[2].at[block, :, pl.ds(columns, columns)]),
                (reduce.at[block], outs[3].at[block]),
            ]
            sent = lambda n, pairs=pairs: copy(*pairs[n])
            unpack_second(buffer.at[block], expand.at[block], reduce.at[block], sent, table, block, factor)
        copy(table, outs[4])
        for one in copies:
            one.wait()


class Whole:
    def __init__(self, ref, block):
        self.ref, self.block = ref, block

    def __getitem__(self, index):
        return self.ref[self.block]


def call(kernel, outs, scratch, args, stacked=(), distant=(), micros=0.5, limit=LIMIT, far_outs=0, aliases=None):
    here, there = pl.BlockSpec(memory_space=pltpu.VMEM), pl.BlockSpec(memory_space=pltpu.HBM)
    count = len(args)

    def body(*refs):
        weights = [Whole(ref, block) for ref, (_, block) in zip(refs[count:], stacked)]
        kernel(*refs[:count], *weights, *refs[count + len(stacked) :])

    return pl.pallas_call(
        body,
        in_specs=[here] * (count + len(stacked)) + [there] * len(distant),
        out_specs=[there] * far_outs + [here] * (len(outs) - far_outs),
        out_shape=[jax.ShapeDtypeStruct(s, d) for s, d in outs],
        scratch_shapes=[pltpu.VMEM(*one) if isinstance(one, tuple) else one for one in scratch],
        input_output_aliases=aliases or {},
        compiler_params=pltpu.CompilerParams(vmem_limit_bytes=limit),
        cost_estimate=pl.CostEstimate(flops=int(micros * 1.1e9), bytes_accessed=0, transcendentals=0),
    )(*args, *(arg for arg, _ in stacked), *distant)


def local(block_input, cotangent, qkv_weight, proj_weight, expand_weight, reduce_weight, bias_table):
    frames, rows, cols, width = block_input.shape
    n_row, n_col = lax.axis_size("row"), lax.axis_size("col")
    inner = expand_weight.shape[2]
    heads = bias_table.shape[1]
    tokens = frames * rows * cols
    wide = jnp.swapaxes(reduce_weight, 1, 2)
    weights = (qkv_weight, proj_weight, expand_weight, wide)
    table = jnp.swapaxes(bias_table, 0, 1)
    axes = ("row", "col")

    def send(block, down, right):
        route = [
            (r * n_col + c, (r + down) % n_row * n_col + (c + right) % n_col)
            for r in range(n_row)
            for c in range(n_col)
        ]
        return lax.ppermute(block, axes, route)

    def swap(block, row_bits, col_bits):
        route = [
            (r * n_col + c, (r ^ row_bits) * n_col + (c ^ col_bits)) for r in range(n_row) for c in range(n_col)
        ]
        return lax.ppermute(block, axes, route)

    far = n_col // 2
    unit = 8 * far * 16
    used = (4 * width + 2 * inner) * width // 128 + 2 * 16
    size = -(-used // unit) * unit
    chunk = size // (8 * far)
    halves = [((size // 2, 128), BF)] * 2
    buffer = ((size, 128), BF)
    tile = (frames, rows, cols, width)
    strip = (frames, SHIFT, cols, width)
    patches = frames * SHIFT * SHIFT
    tight = ((4 * patches, width), F32)
    lines = ((heads * 64, 128), F32)
    sent = [(strip, F32), ((2, *strip), BF), ((2 * patches, width), BF), ((2 * patches, width), BF)]
    first, top, left, corner = call(
        plain_forward,
        sent,
        [*sent, tight, (tile, BF), *((w.shape[1:], BF) for w in weights), (tile, BF), (tile, F32), (table.shape, F32), pltpu.SemaphoreType.DMA((7,))],
        [],
        distant=(block_input, cotangent, table, *weights),
        micros=2.3,
        limit=FULL,
        far_outs=4,
    )
    halo = [send(top, -1, 0), send(corner, -1, -1), send(left, 0, -1)]
    bias, *kept = call(
        functools.partial(keep_plain, n_row, n_col),
        [
            lines,
            ((inner, tokens), F32),
            ((width, tokens), F32),
            ((1, tokens), F32),
            ((width, tokens), BF),
            ((width, tokens), BF),
            ((width, tokens), BF),
            ((heads * 64, tokens), F32),
            ((width, tokens), BF),
            ((width, tokens), F32),
            ((1, tokens), F32),
            ((inner, tokens), BF),
        ],
        [],
        [block_input, table],
        [(w, 0) for w in weights[:3]],
        micros=2.3,
    )
    own, bottom, right, corner, keep, away = call(
        shifted_block,
        [(strip, F32), (strip, BF), ((patches, width), BF), ((patches, width), BF), *halves],
        [((frames, rows, cols + 8, width), F32)] * 2 + [tight, buffer],
        [first, cotangent, *halo, bias],
        [(w, 1) for w in weights],
        micros=4.8,
    )
    back = [own, send(bottom, 1, 0), send(corner, 1, 1), send(right, 0, 1)]

    eighth, quarter, piece = (size // 8, 128), (size // 4, 128), (2 * chunk, 128)

    def near(own, *sends):
        came = [swap(one, d & 2, d & 1) for d, one in reversed(list(enumerate(sends, 1)))]
        return [own] + came[::-1]

    quarters = [(eighth, F32)] + [(eighth, BF)] * 3
    summed = [((size // 2, 128), F32)]
    shifted = call(add_core, quarters, summed, [keep, swap(away, 1, 0)])
    kept[0], *shifted = lax.optimization_barrier((kept[0], *shifted))
    (other,) = call(sum_near, [(eighth, F32)], [], near(*shifted), micros=4.0)
    keep, away, mixed, resid = call(
        plain_backward,
        [*halves, ((3 * width, tokens), BF), ((width, tokens), F32)],
        [(tile, F32), tight, buffer],
        [*back, *kept],
        [(w, 0) for w in weights],
        micros=3.0,
    )
    (input_grad,) = call(
        plain_field, [(tile, F32)], [], [mixed, resid, kept[1], kept[2]], [(qkv_weight, 0)], micros=1.0
    )
    plain = near(*call(add_core_later, quarters, summed, [keep, swap(away, 1, 0), other]))
    plain[0], input_grad = lax.optimization_barrier((plain[0], input_grad))
    own, *sends = call(
        functools.partial(add_near, far),
        [(piece, F32)] + [(piece, BF)] * (far - 1),
        [(eighth, F32)],
        [*plain, other],
    )
    distant = [own] + [swap(one, 0, 2 * d) for d, one in zip(range(far - 1, 0, -1), sends, strict=True)]
    (done,) = call(add_far, [(piece, BF)], [], distant)
    distant = [done] + [swap(done, 0, 2 * d) for d in range(1, far)]
    (joined,) = call(join_far, [(quarter, BF)], [], distant)
    near = [joined] + [swap(joined, d & 2, d & 1) for d in range(1, 4)]
    factor = 1.0 / math.sqrt(frames * rows * n_row * cols * n_col)
    shapes = [(w.shape, F32) for w in (*weights, table)]
    stage = [((2, size // 2, 128), BF), pltpu.SemaphoreType.DMA((6,)), *shapes]
    stage[4] = ((2, width, inner // 2), F32)
    grads = call(functools.partial(finish, 0, factor), shapes, stage, near, far_outs=5, micros=1.2)
    qkv, proj, expand, reduce, table = call(
        functools.partial(finish, 1, factor),
        shapes,
        stage,
        [swap(one, 1, 0) for one in near],
        distant=grads,
        far_outs=5,
        aliases={4 + n: n for n in range(5)},
        micros=1.2,
    )
    return input_grad, qkv, proj, expand, jnp.swapaxes(reduce, 1, 2), jnp.swapaxes(table, 0, 1)


def solution(mesh):
    in_specs = (P(None, "row", "col", None), P(None, "row", "col", None), P(), P(), P(), P(), P())
    out_specs = (P(None, "row", "col", None), P(), P(), P(), P(), P())
    return jax.shard_map(local, mesh=mesh, in_specs=in_specs, out_specs=out_specs, check_vma=False)
```
